32 devices in a mesh: lat: 8 (over y, x, core), chan: 4 (over z).
Axes of the slice: x: 2, y: 2, z: 4, core: 2. Of those that a mesh axis runs over, the one named last changes fastest.
Arguments:
- grid_field: float32 [16, 1440, 256], P('lat', 'chan'), may hold values from -6 to 6
- filters: float32 [16, 4, 3, 5], P('lat'), may hold values from -1.5 to 1.5
- disco_weight: float32 [4, 256], replicated, may hold values from -3 to 3
- band_start: int32 [16], P('lat'), may hold values from -2 to 0
- band_reach: int32 [16], P('lat'), may hold values from 1 to 3
- spec_weight: float32 [256, 256], replicated, may hold values from -0.375 to 0.375
- degree_gain: float32 [360, 256], replicated, may hold values from 0.5 to 2
- cotangent: float32 [16, 1440, 256], P('lat', 'chan'), may hold values from -6 to 6
Outputs:
- output: float32 [16, 1440, 256], P('lat', 'chan')
- grad_input: float32 [16, 1440, 256], P('lat', 'chan')
- grad_weight: float32 [256, 256], replicated
The draws below stay inside these ranges and needn't reach their ends.
Inputs may be any that keep to these rules, and one draw needn't show every extreme that they name: The block of latitude i covers rows i + band_start[i] to i + band_start[i] + 2. Rows of a block at or past band_reach[i] are padding.
All inputs are finite; a program needn't handle non-finite values.
Results may differ from the reference program's by a relative error of at most 0.0003.
Values sent between devices are 32-bit elements; how exact they have to be, the bound alone decides.
No kernel may reach another device: no remote copies, remote signals or barrier semaphores. Data moves between devices by JAX's collectives and lax.ppermute only.
A program may use at most 64 MiB of HBM per device.

```python
import math
import jax
import jax.numpy as jnp
from jax import lax

NLON = 1440
C = 256
L = 360
M = 256
K = 4
WIN = 3
HMAX = 2
KLON = 5
POLAR = 720
NLAT = 16


def with_ends(array, stream_key, least, high):
    shape = array.shape
    place = [jax.random.randint(jax.random.fold_in(stream_key, axis), (), 0, shape[axis]) for axis in range(len(shape))]
    array = array.at[tuple(place)].set(least)
    longest = shape.index(max(shape))
    place[longest] = (place[longest] + 1) % shape[longest]
    return array.at[tuple(place)].set(high)


def steps_of(stream_key, shape, shards, smallest, top_value):
    gain, own = 1.0, jax.random.fold_in(stream_key, 6)
    for dim, shards_of in shards:
        draws = jnp.exp(jax.random.uniform(jax.random.fold_in(own, dim), (shards_of,), jnp.float32, smallest / len(shards), top_value / len(shards)))
        gain = gain * jnp.repeat(draws, shape[dim] // shards_of).reshape([-1 if axis == dim else 1 for axis in range(len(shape))])
    return gain


def normal_values(rng, dims, width, bound, shards=(), held_as=jnp.bfloat16):
    loudness = steps_of(rng, dims, shards, -0.22, 0.18) if shards else 1.0
    drawn = jax.random.normal(rng, dims, jnp.float32) * width * loudness
    return jnp.minimum(jnp.maximum(drawn, -bound), bound).astype(held_as)


def setup_inputs(seed: int = 0) -> dict:
    splits = jax.random.split(jax.random.key(seed), 9)
    return {
        "grid_field": normal_values(splits[0], (NLAT, NLON, C), 1.0, 6.0, ((0, 8), (1, 4)), jnp.float32),
        "filters": normal_values(splits[1], (NLAT, K, WIN, KLON), (WIN * KLON) ** -0.5, 1.5, ((0, 8),), jnp.float32),
        "disco_weight": normal_values(splits[2], (K, C), K ** -0.5, 3.0, (), jnp.float32),
        "band_start": with_ends(jax.random.randint(splits[3], (NLAT,), 0 - HMAX, HMAX - WIN + 2), jax.random.fold_in(splits[3], 1), 0 - HMAX, (HMAX - WIN + 2) - 1).astype(jnp.int32),
        "band_reach": with_ends(jax.random.randint(splits[4], (NLAT,), 1, WIN + 1), jax.random.fold_in(splits[4], 1), 1, WIN).astype(jnp.int32),
        "spec_weight": normal_values(splits[5], (C, C), C ** -0.5, 0.375, (), jnp.float32),
        "degree_gain": jnp.clip(jnp.exp(jax.random.uniform(splits[6], (L, C), jnp.float32, math.log(0.5), math.log(2.0))), 0.5, 2.0),
        "cotangent": normal_values(splits[7], (NLAT, NLON, C), 1.0, 6.0, ((0, 8), (1, 4)), jnp.float32),
    }


highest = lax.Precision.HIGHEST
upper_bound = 2.0 ** 32
lower_factor = 2.0 ** (-32)
log_step = 32.0 * math.log(2.0)

def grid_tables(lat_total):
    first_row = (POLAR - lat_total) // 2
    colatitude = math.pi * (jnp.arange(lat_total, dtype=jnp.float32) + float(first_row)) / POLAR
    quad_weight = 2.0 * math.pi * math.pi / POLAR * jnp.sin(colatitude)
    return (colatitude, quad_weight)

def log_norms(order_count):
    order_index = jnp.arange(order_count, dtype=jnp.float32)
    log_terms = jnp.where(order_index > 0.0, jnp.log((2.0 * order_index + 1.0) / jnp.maximum(2.0 * order_index, 1.0)), 0.0)
    return -0.5 * math.log(4.0 * math.pi) + 0.5 * jnp.cumsum(log_terms)

def legendre(colatitude, orders, log_norm, degree_count):
    cosine = jnp.cos(colatitude)[:, None]
    log_sine = jnp.log(jnp.sin(colatitude))[:, None]
    order_f = orders.astype(jnp.float32)[None, :]
    norm_start = jnp.exp(log_norm)[None, :] + jnp.zeros_like(cosine)
    zeros_state = jnp.zeros((colatitude.shape[0], orders.shape[0]), jnp.float32)

    def advance(carry, degree):
        previous, second, log_scale = carry
        degree_f = degree.astype(jnp.float32)
        step_factor = jnp.where(degree > orders[None, :], jnp.sqrt(jnp.maximum(4.0 * degree_f * degree_f - 1.0, 0.0) / jnp.maximum(degree_f * degree_f - order_f * order_f, 1.0)), 0.0)
        lower_degree = degree_f - 1.0
        back_factor = jnp.sqrt(jnp.maximum(lower_degree * lower_degree - order_f * order_f, 0.0) / (4.0 * lower_degree * lower_degree - 1.0))
        current = jnp.where(degree == orders[None, :], norm_start, step_factor * (cosine * previous - back_factor * second))
        too_large = jnp.abs(current) > upper_bound
        current = jnp.where(too_large, current * lower_factor, current)
        previous = jnp.where(too_large, previous * lower_factor, previous)
        log_scale = jnp.where(too_large, log_scale + log_step, log_scale)
        return ((current, previous, log_scale), current * jnp.exp(log_scale))
    start_state = (zeros_state, zeros_state, order_f * log_sine)
    _, tables = lax.scan(advance, start_state, jnp.arange(degree_count, dtype=jnp.int32), unroll=8)
    return tables

def filter_coeff(filters, disco_weight, band_reach):
    summed = jnp.einsum('ikrt,kc->irtc', filters, disco_weight, precision=highest)
    live_rows = jnp.arange(filters.shape[2], dtype=jnp.int32)[None, :] < band_reach[:, None]
    return jnp.where(live_rows[:, :, None, None], summed, 0.0)

def disco_apply(grid_field, coefficient, band_start):
    lat_total = grid_field.shape[0]
    padded = jnp.pad(grid_field, ((HMAX, HMAX), (0, 0), (0, 0)))
    row_index = jnp.arange(lat_total, dtype=jnp.int32)[:, None] + HMAX + band_start[:, None] + jnp.arange(WIN, dtype=jnp.int32)[None, :]
    summed = jnp.zeros_like(grid_field)
    for offset in range(WIN):
        window = jnp.take(padded, row_index[:, offset], axis=0)
        for tap_index in range(KLON):
            summed = summed + coefficient[:, offset, tap_index][:, None, :] * jnp.roll(window, -(tap_index - KLON // 2), axis=1)
    return summed

def spectral_path(grid_field, weight, degree_gain, legendre_rows, quad_weight):
    transform = jnp.fft.rfft(grid_field, axis=1)[:, :M, :] / NLON
    spectrum = jnp.stack([jnp.real(transform), jnp.imag(transform)], axis=2)
    degree = jnp.einsum('ljm,jmpc->lmpc', legendre_rows, spectrum * quad_weight[:, None, None, None], precision=highest)
    mixed_modes = jnp.einsum('lmpc,cd->lmpd', degree, weight, precision=highest) * degree_gain[:, None, None, :]
    synthesis = jnp.einsum('ljm,lmpd->jmpd', legendre_rows, mixed_modes, precision=highest)
    complex_field = lax.complex(synthesis[:, :, 0, :], synthesis[:, :, 1, :])
    padded = jnp.zeros((grid_field.shape[0], NLON // 2 + 1, grid_field.shape[2]), complex_field.dtype).at[:, :M, :].set(complex_field)
    return jnp.fft.irfft(padded, n=NLON, axis=1) * NLON

def reference(grid_field, filters, disco_weight, band_start, band_reach, spec_weight, degree_gain, cotangent):
    colatitude, quad_weight = grid_tables(grid_field.shape[0])
    legendre_rows = legendre(colatitude, jnp.arange(M, dtype=jnp.int32), log_norms(M), L)
    coefficient = filter_coeff(filters, disco_weight, band_reach)

    def apply_layer(field_value, weight):
        local_out = disco_apply(field_value, coefficient, band_start)
        spectral = spectral_path(field_value, weight, degree_gain, legendre_rows, quad_weight)
        return field_value + jax.nn.silu(local_out + spectral)
    output, pullback = jax.vjp(apply_layer, grid_field, spec_weight)
    grad_input, grad_weight = pullback(cotangent)
    return (output, grad_input, grad_weight)
```

```python
import functools
import math

import jax
import jax.numpy as jnp
import ml_dtypes
import numpy as np
from jax import lax
from jax.experimental import pallas as pl
from jax.experimental.pallas import tpu as pltpu
from jax.sharding import PartitionSpec as P

L = 360
M = 256
WIN = 3
HMAX = 2
KLON = 5
POLAR = 720
SPAN = 2 * HMAX + 1
LANES = 128
HALF = 64
MIB = 2**20


highest = lax.Precision.HIGHEST
upper_bound = 2.0**32
lower_factor = 2.0 ** (-32)
log_step = 32.0 * math.log(2.0)

f32 = jnp.float32
bf16 = jnp.bfloat16
VMEM = pltpu.VMEM


@functools.lru_cache(maxsize=None)
def wave_tables(lon_total, own_count):
    orders = np.arange(M).reshape(-1, own_count)
    angle = (orders[:, :, None] * np.arange(lon_total)) % lon_total * (2.0 * np.pi / lon_total)
    table = np.stack([np.cos(angle), -np.sin(angle)], axis=1).reshape(2 * M, lon_total)
    high = table.astype(ml_dtypes.bfloat16)
    low = (table - high.astype(np.float64)).astype(ml_dtypes.bfloat16)
    return high, low


def grid_tables(lat_total):
    first_row = (POLAR - lat_total) // 2
    colatitude = math.pi * (jnp.arange(lat_total, dtype=f32) + float(first_row)) / POLAR
    quad_weight = 2.0 * math.pi * math.pi / POLAR * jnp.sin(colatitude)
    return (colatitude, quad_weight)


def log_norms(order_count):
    order_index = jnp.arange(order_count, dtype=f32)
    log_terms = jnp.where(
        order_index > 0.0,
        jnp.log((2.0 * order_index + 1.0) / jnp.maximum(2.0 * order_index, 1.0)),
        0.0,
    )
    return -0.5 * math.log(4.0 * math.pi) + 0.5 * jnp.cumsum(log_terms)


def split(x):
    high = x.astype(bf16)
    return high, (x - high.astype(f32)).astype(bf16)


def dot_split(a, b, dims):
    (ah, al), (bh, bl) = split(a), split(b)
    dot = lambda u, v: lax.dot_general(u, v, (dims, ((), ())), preferred_element_type=f32)
    return dot(ah, bh) + (dot(ah, bl) + dot(al, bh))


def lower_lanes(shape):
    return lax.broadcasted_iota(jnp.int32, shape, len(shape) - 1) < HALF


def swap(x):
    return pltpu.roll(x, HALF, x.ndim - 1)


def pair(first, second, odd):
    low = lower_lanes(first.shape)
    return jnp.where(low, swap(first), second) if odd else jnp.where(low, first, swap(second))


def call(kernel, out_shape, in_specs, scratch=(), flops=0, limit=48):
    return pl.pallas_call(
        kernel,
        out_shape=out_shape,
        in_specs=in_specs,
        out_specs=jax.tree.map(lambda _: pl.BlockSpec(memory_space=VMEM), out_shape),
        scratch_shapes=list(scratch),
        compiler_params=pltpu.CompilerParams(vmem_limit_bytes=limit * MIB),
    )


def vmem(count):
    return [pl.BlockSpec(memory_space=VMEM)] * count


smem = pl.BlockSpec(memory_space=pltpu.SMEM)


def struct(*shape, dtype=f32):
    return jax.ShapeDtypeStruct(shape, dtype)


def pack_kernel(x_ref, o_ref):
    for part in range(o_ref.shape[0]):
        lanes = pl.ds(part // 2 * LANES, LANES)
        o_ref[part] = pair(x_ref[0, :, lanes], x_ref[1, :, lanes], part % 2)


def unpack_kernel(p_ref, o_ref):
    for group in range(p_ref.shape[0] // 2):
        lanes = pl.ds(group * LANES, LANES)
        first, second = p_ref[2 * group], p_ref[2 * group + 1]
        for row in range(2):
            o_ref[row, :, lanes] = pair(first, second, row)


def pack(x, parts):
    return call(pack_kernel, struct(parts, x.shape[1], LANES), vmem(1))(x)


def unpack(p):
    return call(unpack_kernel, struct(2, p.shape[1], p.shape[0] * HALF), vmem(1))(p)


def wide(x):
    high, low = split(x)
    return jnp.concatenate([high, low], axis=1)


def three(table_high, table_low, both):
    y = jnp.dot(table_high, both, preferred_element_type=f32)
    return y[:, :LANES] + (
        y[:, LANES:] + jnp.dot(table_low, both[:, :LANES], preferred_element_type=f32)
    )


def analyze_kernel(scale, x_ref, high_ref, low_ref, o_ref):
    both = wide(x_ref[...])
    tile = 256
    for part in range(high_ref.shape[0] // tile):
        rows = pl.ds(part * tile, tile)
        o_ref[rows, :] = three(high_ref[rows, :], low_ref[rows, :], both) * scale


def grid_kernel(s_ref, x_ref, local_ref, cot_ref, high_ref, low_ref, thigh_ref, tlow_ref,
                out_ref, err_ref, mode_ref, both_ref):
    modes = wide(s_ref[...])
    lons = x_ref.shape[0]
    tile = lons // 5
    for part in range(5):
        rows = pl.ds(part * tile, tile)
        hidden = local_ref[rows, :] + three(thigh_ref[rows, :], tlow_ref[rows, :], modes)
        gate = 1.0 / (1.0 + jnp.exp(-hidden))
        out_ref[rows, :] = x_ref[rows, :] + hidden * gate
        error = cot_ref[rows, :] * (gate * (1.0 + hidden * (1.0 - gate)))
        err_ref[rows, :] = error
        both_ref[rows, :] = wide(error)
    both = both_ref[...]
    tile = 256
    for part in range(high_ref.shape[0] // tile):
        rows = pl.ds(part * tile, tile)
        mode_ref[rows, :] = three(high_ref[rows, :], low_ref[rows, :], both)


def final_kernel(scale, s_ref, base_ref, thigh_ref, tlow_ref, o_ref):
    modes = wide(s_ref[...])
    tile = base_ref.shape[0] // 5
    for part in range(5):
        rows = pl.ds(part * tile, tile)
        o_ref[rows, :] = base_ref[rows, :] + scale * three(
            thigh_ref[rows, :], tlow_ref[rows, :], modes
        )


def filter_kernel(add, prev_ref, own_ref, next_ref, coef_ref, *refs):
    base_ref = refs[0] if add else None
    o_ref, sums_ref = refs[-2], refs[-1]
    lons = own_ref.shape[0]
    tile = lons // 18
    low = lower_lanes((tile, LANES))

    @pl.loop(0, 18)
    def _(part):
        rows = pl.ds(pl.multiple_of(part * tile, 8), tile)
        prev, own, after = prev_ref[rows, :], own_ref[rows, :], next_ref[rows, :]
        swapped = swap(own)
        sources = (
            prev,
            jnp.where(low, swap(prev), swapped),
            own,
            jnp.where(low, swapped, swap(after)),
            after,
        )
        out_rows = pl.ds(pl.multiple_of(part * tile + 8, 8), tile)
        for tap in range(KLON):
            total = sources[0] * coef_ref[pl.ds(tap, 1), :]
            for offset in range(1, SPAN):
                total = total + sources[offset] * coef_ref[pl.ds(offset * KLON + tap, 1), :]
            sums_ref[tap, out_rows, :] = total

    for tap in range(KLON):
        sums_ref[tap, pl.ds(0, 8), :] = sums_ref[tap, pl.ds(lons, 8), :]
        sums_ref[tap, pl.ds(lons + 8, 8), :] = sums_ref[tap, pl.ds(8, 8), :]
    for part in range(18):
        rows = pl.ds(part * tile, tile)
        total = base_ref[rows, :] if add else None
        for tap in range(KLON):
            value = sums_ref[tap, pl.ds(part * tile + 8 + tap - KLON // 2, tile), :]
            total = value if total is None else total + value
        o_ref[rows, :] = total


def local_filter(prev, own, after, coef, base=None):
    lons = own.shape[0]
    args = (prev, own, after, coef) + (() if base is None else (base,))
    return call(
        functools.partial(filter_kernel, base is not None),
        struct(lons, LANES),
        vmem(len(args)),
        [VMEM((KLON, lons + 16, LANES), f32)],
    )(*args)


def coupling_kernel(lat_total, first_ref, gain_ref, o_ref, step_ref, back_ref, leg_ref, scale_ref,
                    padded_ref, column_ref):
    degree_count, chans = gain_ref.shape
    depth = padded_ref.shape[0]
    own = LANES // lat_total
    first_row = float((POLAR - lat_total) // 2)
    lane = lax.broadcasted_iota(jnp.int32, (1, LANES), 1)
    order = lane % own + first_ref[0]
    colatitude = math.pi * ((lane // own).astype(f32) + first_row) / POLAR
    cosine, log_sine = jnp.cos(colatitude), jnp.log(jnp.sin(colatitude))
    k = lax.broadcasted_iota(jnp.int32, (M, LANES), 0)
    k_f = k.astype(f32)
    log_terms = jnp.log((2.0 * k_f + 1.0) / jnp.maximum(2.0 * k_f, 1.0))
    log_norm = -0.5 * math.log(4.0 * math.pi) + 0.5 * jnp.sum(
        jnp.where((k > 0) & (k <= order), log_terms, 0.0), axis=0, keepdims=True
    )
    norm_start = jnp.exp(log_norm)
    degree = lax.broadcasted_iota(jnp.int32, (degree_count, LANES), 0)
    degree_f, order_f = degree.astype(f32), order.astype(f32)
    step_ref[...] = jnp.where(
        degree > order,
        jnp.sqrt(
            jnp.maximum(4.0 * degree_f * degree_f - 1.0, 0.0)
            / jnp.maximum(degree_f * degree_f - order_f * order_f, 1.0)
        ),
        0.0,
    )
    lower = degree_f - 1.0
    back_ref[...] = jnp.sqrt(
        jnp.maximum(lower * lower - order_f * order_f, 0.0) / (4.0 * lower * lower - 1.0)
    )
    zeros = jnp.zeros((1, LANES), f32)

    def block(index, carry):
        previous, second, log_scale = carry
        first = pl.multiple_of(index * 8, 8)
        rows = pl.ds(first, 8)
        steps, backs = step_ref[rows, :], back_ref[rows, :]
        produced, scales = [], []
        for offset in range(8):
            current = jnp.where(
                first + offset == order,
                norm_start,
                steps[offset : offset + 1] * (cosine * previous - backs[offset : offset + 1] * second),
            )
            too_large = jnp.abs(current) > upper_bound
            current = jnp.where(too_large, current * lower_factor, current)
            previous = jnp.where(too_large, previous * lower_factor, previous)
            log_scale = jnp.where(too_large, log_scale + log_step, log_scale)
            produced.append(current)
            scales.append(log_scale)
            second, previous = previous, current
        leg_ref[rows, :] = jnp.concatenate(produced, axis=0)
        scale_ref[rows, :] = jnp.concatenate(scales, axis=0)
        return previous, second, log_scale

    lax.fori_loop(0, degree_count // 8, block, (zeros, zeros, order_f * log_sine))
    leg_ref[pl.ds(0, degree_count), :] = leg_ref[pl.ds(0, degree_count), :] * jnp.exp(scale_ref[...])
    rest = depth - degree_count
    leg_ref[pl.ds(degree_count, rest), :] = jnp.zeros((rest, LANES), f32)
    padded_ref[pl.ds(0, degree_count), :] = gain_ref[...]
    padded_ref[pl.ds(degree_count, rest), :] = jnp.zeros((rest, chans), f32)
    column_ref[...] = leg_ref[...].T

    high, low = split(padded_ref[...])
    row = lax.broadcasted_iota(jnp.int32, (LANES, LANES), 0)
    quad = 2.0 * math.pi * math.pi / POLAR * jnp.sin(
        math.pi * ((row // own).astype(f32) + first_row) / POLAR
    )
    weight = quad * jnp.where(row % own + first_ref[0] == 0, 1.0, 2.0)
    weight = jnp.concatenate([weight] * (chans // LANES), axis=1)

    @pl.loop(0, lat_total)
    def _(j):
        mine = column_ref[pl.ds(pl.multiple_of(j * own, own), own), :]
        both = column_ref[...] * jnp.concatenate([mine] * lat_total, axis=0)
        both_high, both_low = split(both)
        total = jnp.dot(both_high, high, preferred_element_type=f32) + (
            jnp.dot(both_high, low, preferred_element_type=f32)
            + jnp.dot(both_low, high, preferred_element_type=f32)
        )
        o_ref[j] = (total * weight).reshape(lat_total, own, chans)


def coupling(first_order, degree_gain, lat_total):
    degrees, chans = degree_gain.shape
    own = LANES // lat_total
    depth = (degrees + LANES - 1) // LANES * LANES
    return call(
        functools.partial(coupling_kernel, lat_total),
        struct(lat_total, lat_total, own, chans),
        [smem] + vmem(1),
        [
            VMEM((degrees, LANES), f32),
            VMEM((degrees, LANES), f32),
            VMEM((depth, LANES), f32),
            VMEM((degrees, LANES), f32),
            VMEM((depth, chans), f32),
            VMEM((LANES, depth), f32),
        ],
    )(first_order, degree_gain)


def gather_modes(r_ref, write, parts):
    for band in range(r_ref.shape[0] // parts):
        for group in range(parts // 2):
            lanes = pl.ds(group * LANES, LANES)
            first, second = r_ref[band * parts + 2 * group], r_ref[band * parts + 2 * group + 1]
            for row in range(2):
                write(2 * band + row, lanes, pair(first, second, row))


def scatter_modes(read, s_ref, parts):
    for band in range(s_ref.shape[0] // parts):
        for part in range(parts):
            lanes = pl.ds(part // 2 * LANES, LANES)
            s_ref[band * parts + part] = pair(
                read(2 * band, lanes), read(2 * band + 1, lanes), part % 2
            )


def forward_modes_kernel(parts, r_ref, coupling_ref, w_ref, x_ref, s_ref, y_ref, z_ref):
    def write(j, lanes, value):
        x_ref[j, :, lanes] = value

    gather_modes(r_ref, write, parts)
    lats, rows, chans = x_ref.shape
    own = rows // 2
    y_ref[...] = dot_split(
        x_ref[...].reshape(lats * rows, chans), w_ref[...], ((1,), (0,))
    ).reshape(lats, rows, chans)

    @pl.loop(0, lats)
    def _(j):
        totals = [jnp.zeros((own, chans), f32)] * 2
        for other in range(lats):
            factor = coupling_ref[j, other]
            for p in range(2):
                totals[p] = totals[p] + factor * y_ref[other, pl.ds(p * own, own), :]
        for p in range(2):
            z_ref[j, pl.ds(p * own, own), :] = totals[p]

    scatter_modes(lambda j, lanes: z_ref[j, :, lanes], s_ref, parts)


def backward_modes_kernel(parts, r_ref, coupling_ref, w_ref, x_ref, s_ref, gw_ref, e_ref, v_ref):
    def write(j, lanes, value):
        e_ref[j, :, lanes] = value

    gather_modes(r_ref, write, parts)
    lats, rows, chans = x_ref.shape
    own = rows // 2

    @pl.loop(0, lats)
    def _(j):
        totals = [jnp.zeros((own, chans), f32)] * 2
        for other in range(lats):
            factor = coupling_ref[other, j]
            for p in range(2):
                totals[p] = totals[p] + factor * e_ref[other, pl.ds(p * own, own), :]
        for p in range(2):
            v_ref[j, pl.ds(p * own, own), :] = totals[p]

    v = v_ref[...].reshape(lats * rows, chans)
    e_ref[...] = dot_split(v, w_ref[...], ((1,), (1,))).reshape(lats, rows, chans)
    scatter_modes(lambda j, lanes: e_ref[j, :, lanes], s_ref, parts)
    gw_ref[...] = dot_split(x_ref[...].reshape(lats * rows, chans), v, ((0,), (0,)))


def legendre_orders(colatitude, orders, log_norm, degree_count):
    cosine = jnp.cos(colatitude)[None, :]
    log_sine = jnp.log(jnp.sin(colatitude))[None, :]
    order_f = orders.astype(f32)[:, None]
    norm_start = jnp.exp(log_norm)[:, None] + jnp.zeros_like(cosine)
    zeros_state = jnp.zeros((orders.shape[0], colatitude.shape[0]), f32)

    def advance(carry, degree):
        previous, second, log_scale = carry
        degree_f = degree.astype(f32)
        step_factor = jnp.where(
            degree > orders[:, None],
            jnp.sqrt(
                jnp.maximum(4.0 * degree_f * degree_f - 1.0, 0.0)
                / jnp.maximum(degree_f * degree_f - order_f * order_f, 1.0)
            ),
            0.0,
        )
        lower_degree = degree_f - 1.0
        back_factor = jnp.sqrt(
            jnp.maximum(lower_degree * lower_degree - order_f * order_f, 0.0)
            / (4.0 * lower_degree * lower_degree - 1.0)
        )
        current = jnp.where(
            degree == orders[:, None],
            norm_start,
            step_factor * (cosine * previous - back_factor * second),
        )
        too_large = jnp.abs(current) > upper_bound
        current = jnp.where(too_large, current * lower_factor, current)
        previous = jnp.where(too_large, previous * lower_factor, previous)
        log_scale = jnp.where(too_large, log_scale + log_step, log_scale)
        return ((current, previous, log_scale), current * jnp.exp(log_scale))

    start_state = (zeros_state, zeros_state, order_f * log_sine)
    _, tables = lax.scan(advance, start_state, jnp.arange(degree_count, dtype=jnp.int32), unroll=8)
    return tables


def plain_gather(received, parts, own):
    bands = received.shape[0] // parts
    blocks = received.reshape(bands, parts, 2, own, 2, HALF)
    return blocks.transpose(0, 4, 2, 3, 1, 5).reshape(2 * bands, 2, own, parts * HALF)


def plain_scatter(modes, parts):
    lats, _, own, chans = modes.shape
    blocks = modes.reshape(lats // 2, 2, 2, own, parts, HALF)
    return blocks.transpose(0, 4, 2, 3, 1, 5).reshape(lats // 2 * parts, 2 * own, LANES)


def mode_stages(first_order, own, lat_total, parts, degree_gain, spec_weight):
    if own % 8 == 0 and own * lat_total == LANES:
        factors = coupling(first_order[None], degree_gain, lat_total)
        chans = spec_weight.shape[0]
        shape = (lat_total, 2 * own, chans)

        def forward(received):
            return call(
                functools.partial(forward_modes_kernel, parts),
                (struct(*shape), struct(*received.shape)),
                vmem(3),
                [VMEM(shape, f32), VMEM(shape, f32)],
            )(received, factors, spec_weight)

        def backward(received, spectrum):
            return call(
                functools.partial(backward_modes_kernel, parts),
                (struct(*received.shape), struct(chans, chans)),
                vmem(4),
                [VMEM(shape, f32), VMEM(shape, f32)],
            )(received, factors, spec_weight, spectrum)

        return forward, backward

    colatitude, quad_weight = grid_tables(lat_total)
    orders = first_order + jnp.arange(own, dtype=jnp.int32)
    log_norm = lax.dynamic_slice_in_dim(log_norms(M), first_order, own)
    legendre = legendre_orders(colatitude, orders, log_norm, degree_gain.shape[0])
    order_weight = jnp.where(orders == 0, 1.0, 2.0).astype(f32)[None, None, :, None]
    quad_column = quad_weight[:, None, None, None]
    dot = functools.partial(jnp.einsum, precision=highest)

    def forward(received):
        spectrum = plain_gather(received, parts, own)
        mixed = dot("jpmc,cd->jpmd", spectrum, spec_weight) * quad_column
        degree = dot("lmj,jpmd->lpmd", legendre, mixed) * degree_gain[:, None, None, :]
        synthesis = dot("lmj,lpmd->jpmd", legendre, degree) * order_weight
        return spectrum, plain_scatter(synthesis, parts)

    def backward(received, spectrum):
        error = plain_gather(received, parts, own) * order_weight
        gained = dot("lmj,jpmd->lpmd", legendre, error) * degree_gain[:, None, None, :]
        back = dot("lmj,lpmd->jpmd", legendre, gained) * quad_column
        sent = plain_scatter(dot("jpmd,cd->jpmc", back, spec_weight), parts)
        return sent, dot("jpmc,jpmd->cd", spectrum, back)

    return forward, backward


def swap_parts(x, axis):
    return lax.all_to_all(x, axis, split_axis=0, concat_axis=0, tiled=True)


def body(
    grid_field, filters, disco_weight, band_start, band_reach, spec_weight, degree_gain, cotangent
):
    band_rows, lon_local, chans = grid_field.shape
    bands, parts = lax.axis_size("lat"), lax.axis_size("chan")
    devices = bands * parts
    lat_total, lon_total = band_rows * bands, lon_local * parts
    own = M // devices
    assert band_rows == HMAX and chans == parts * HALF
    band, part = lax.axis_index("lat"), lax.axis_index("chan")
    both_axes = ("lat", "chan")
    high, low = wave_tables(lon_total, own)
    high_t, low_t = (jnp.asarray(np.ascontiguousarray(t.T)) for t in (high, low))
    high, low = jnp.asarray(high), jnp.asarray(low)
    up = [(i, i + 1) for i in range(bands - 1)]
    down = [(i + 1, i) for i in range(bands - 1)]

    def spread_lons(x):
        return swap_parts(pack(x, parts), "chan").reshape(lon_total, LANES)

    def return_lons(x):
        return unpack(swap_parts(x.reshape(parts, lon_local, LANES), "chan"))

    def exchange(modes):
        return swap_parts(modes.reshape(devices, 2 * own, LANES), both_axes)

    field = spread_lons(grid_field)
    cot = spread_lons(cotangent)

    mine = lax.dynamic_slice_in_dim(disco_weight, part * HALF, HALF, axis=1)
    coefficient = jnp.einsum("ikrt,kc->irtc", filters, mine, precision=highest)
    window = jnp.arange(WIN, dtype=jnp.int32)
    coefficient = jnp.where(
        (window[None, :] < band_reach[:, None])[:, :, None, None], coefficient, 0.0
    )
    offset = jnp.arange(-HMAX, HMAX + 1, dtype=jnp.int32)
    lands = offset[None, :, None] == band_start[:, None, None] + window[None, None, :]
    by_offset = jnp.sum(
        jnp.where(lands[:, :, :, None, None], coefficient[:, None], 0.0), axis=2
    )
    before = lax.ppermute(by_offset, "lat", up)
    after = lax.ppermute(by_offset, "lat", down)
    rows = jnp.concatenate([before, by_offset, after], axis=0)
    coef = by_offset.transpose(1, 2, 0, 3).reshape(SPAN * KLON, LANES)
    adjoint = jnp.stack(
        [
            jnp.stack([rows[HMAX + i + u, HMAX - u, ::-1] for i in range(band_rows)], axis=1)
            for u in range(-HMAX, HMAX + 1)
        ]
    ).reshape(SPAN * KLON, LANES)

    forward, backward = mode_stages(
        (band * parts + part) * own, own, lat_total, parts, degree_gain, spec_weight
    )

    modes = call(
        functools.partial(analyze_kernel, 1.0 / lon_total), struct(2 * M, LANES), vmem(3)
    )(field, high, low)
    spectrum, synthesis = forward(exchange(modes))
    local = local_filter(
        lax.ppermute(field, "lat", up), field, lax.ppermute(field, "lat", down), coef
    )
    output, error, error_modes = call(
        grid_kernel,
        (struct(lon_total, LANES), struct(lon_total, LANES), struct(2 * M, LANES)),
        vmem(8),
        [VMEM((lon_total, 2 * LANES), bf16)],
    )(exchange(synthesis).reshape(2 * M, LANES), field, local, cot, high, low, high_t, low_t)
    sent, weight_part = backward(exchange(error_modes), spectrum)
    base = local_filter(
        lax.ppermute(error, "lat", up), error, lax.ppermute(error, "lat", down), adjoint, cot
    )
    gradient = call(
        functools.partial(final_kernel, 1.0 / lon_total), struct(lon_total, LANES), vmem(4)
    )(exchange(sent).reshape(2 * M, LANES), base, high_t, low_t)
    grad_input = return_lons(gradient)
    output = return_lons(output)
    shares = swap_parts(weight_part.reshape(devices, chans // devices, chans), both_axes)
    share = jnp.sum(shares, axis=0)
    grad_weight = swap_parts(
        jnp.broadcast_to(share[None], shares.shape), both_axes
    ).reshape(chans, chans)
    return (output, grad_input, grad_weight)


def solution(mesh):
    in_specs = (
        P("lat", "chan", None),
        P("lat", None, None, None),
        P(),
        P("lat"),
        P("lat"),
        P(),
        P(),
        P("lat", "chan", None),
    )
    out_specs = (P("lat", "chan", None), P("lat", "chan", None), P())
    return jax.shard_map(body, mesh=mesh, in_specs=in_specs, out_specs=out_specs, check_vma=False)
```

```python
import functools
import math

import jax
import jax.numpy as jnp
import ml_dtypes
import numpy as np
from jax import lax
from jax.experimental import pallas as pl
from jax.experimental.pallas import tpu as pltpu
from jax.sharding import PartitionSpec as P

L = 360
M = 256
WIN = 3
HMAX = 2
KLON = 5
POLAR = 720
SPAN = 2 * HMAX + 1
TAPS = 32
EDGES = 16
LANES = 128
MIB = 2**20


highest = lax.Precision.HIGHEST
upper_bound = 2.0**32
lower_factor = 2.0 ** (-32)
log_step = 32.0 * math.log(2.0)

f32 = jnp.float32
bf16 = jnp.bfloat16
VMEM = pltpu.VMEM


@functools.lru_cache(maxsize=None)
def wave_tables(lon_total, own_count):
    orders = np.concatenate([np.arange(0, M, 2), np.arange(1, M, 2)]).reshape(-1, own_count)
    lons = np.arange(lon_total // 2)
    angle = (orders[:, :, None] * lons) % lon_total * (2.0 * np.pi / lon_total)
    table = np.stack([np.cos(angle), -np.sin(angle)], axis=1).reshape(2 * M, lon_total // 2)
    high = table.astype(ml_dtypes.bfloat16)
    low = (table - high.astype(np.float64)).astype(ml_dtypes.bfloat16)
    return high, low


def owned_orders(owner, devices):
    half = devices // 2
    return owner % half * (2 * (M // devices)) + owner // half


def grid_tables(lat_total):
    first_row = (POLAR - lat_total) // 2
    colatitude = math.pi * (jnp.arange(lat_total, dtype=f32) + float(first_row)) / POLAR
    quad_weight = 2.0 * math.pi * math.pi / POLAR * jnp.sin(colatitude)
    return (colatitude, quad_weight)


def log_norms(order_count):
    order_index = jnp.arange(order_count, dtype=f32)
    log_terms = jnp.where(
        order_index > 0.0,
        jnp.log((2.0 * order_index + 1.0) / jnp.maximum(2.0 * order_index, 1.0)),
        0.0,
    )
    return -0.5 * math.log(4.0 * math.pi) + 0.5 * jnp.cumsum(log_terms)


def split(x):
    high = x.astype(bf16)
    return high, (x - high.astype(f32)).astype(bf16)


def dot_split(a, b, dims):
    (ah, al), (bh, bl) = split(a), split(b)
    dot = lambda u, v: lax.dot_general(u, v, (dims, ((), ())), preferred_element_type=f32)
    return dot(ah, bh) + (dot(ah, bl) + dot(al, bh))


def cost(us):
    return pl.CostEstimate(flops=int(us * 1e9), bytes_accessed=int(us * 3e6), transcendentals=0)


def call(kernel, out_shape, in_specs, scratch=(), us=1.0, limit=16, out_spaces=None):
    run = pl.pallas_call(
        kernel,
        out_shape=out_shape,
        in_specs=[pl.BlockSpec(memory_space=space) for space, _ in in_specs],
        out_specs=jax.tree.map(
            lambda space: pl.BlockSpec(memory_space=space),
            out_spaces or jax.tree.map(lambda _: VMEM, out_shape),
        ),
        scratch_shapes=list(scratch),
        compiler_params=pltpu.CompilerParams(vmem_limit_bytes=limit * MIB),
        cost_estimate=cost(us),
    )
    keeps = [keep for _, keep in in_specs]
    return lambda *args: run(
        *[held(x) if keep else x for x, keep in zip(args, keeps, strict=True)]
    )


def held(x):
    return pltpu.with_memory_space_constraint(x, pltpu.HBM)


def vmem(count):
    return [(VMEM, False)] * count


def loaded(count):
    return [(VMEM, True)] * count


def hbm(count):
    return [(pltpu.HBM, True)] * count


smem = (pltpu.SMEM, False)


def struct(*shape, dtype=f32):
    return jax.ShapeDtypeStruct(shape, dtype)


def kept(*shape, dtype=f32):
    return pltpu.HBM(shape, dtype)


def own_half(part):
    return part % 2


def lane_half(x_ref, half):
    return x_ref.at[:, :, pl.ds(pl.multiple_of(half * LANES, LANES), LANES)]


def lon_half(x_ref, half):
    width = x_ref.shape[1] // 2
    return x_ref.at[:, pl.ds(pl.multiple_of(half * width, 8), width), :]


def pair_copies(half, own_hbm, other_hbms, target, sems):
    copies = [pltpu.make_async_copy(lane_half(own_hbm, half), lon_half(target, half), sems.at[0])]
    there = lon_half(target, 1 - half)
    for row, other_hbm in enumerate(other_hbms):
        copies.append(
            pltpu.make_async_copy(other_hbm, there.at[pl.ds(row, 1)], sems.at[1 + row])
        )
    for copy in copies:
        copy.start()
    return copies


def join_kernel(part_ref, own_ref, *refs):
    o_ref = refs[-1]
    half = own_half(part_ref[0])
    mine, theirs = (
        pl.ds(pl.multiple_of(place * LANES, LANES), LANES) for place in (half, 1 - half)
    )
    o_ref[:, :, mine] = own_ref[...]
    for row, other_ref in enumerate(refs[:-1]):
        o_ref[pl.ds(row, other_ref.shape[0]), :, theirs] = other_ref[...]


def join(part, own, *others):
    rows, lons, _ = own.shape
    return call(
        join_kernel, kept(rows, lons, 2 * LANES), [smem] + vmem(1 + len(others))
    )(part, own, *others)


def side_by_side(x):
    return jnp.concatenate([x[0], x[1]], axis=1)


def three(table_high, table_low, high, low):
    dot = lambda u, v: jnp.dot(u, v, preferred_element_type=f32)
    return dot(table_high, high) + (dot(table_high, low) + dot(table_low, high))


def fetches(sources, targets, sems, pieces):
    copies = []
    for index, (source, target) in enumerate(zip(sources, targets, strict=True)):
        tile = source.shape[0] // pieces
        copies.append(
            [
                pltpu.make_async_copy(
                    source.at[pl.ds(piece * tile, tile)],
                    target.at[pl.ds(piece * tile, tile)],
                    sems.at[index, piece],
                )
                for piece in range(pieces)
            ]
        )
    for piece in range(pieces):
        for group in copies:
            group[piece].start()
    return lambda index, piece: copies[index][piece].wait()


def analyze_rows(x, sign, high_ref, low_ref, wait, store):
    high, low = split(x)
    tile = high_ref.shape[0] // 2
    for parity in range(2):
        rows = pl.ds(parity * tile, tile)
        wait(0, parity)
        wait(1, parity)
        value = three(high_ref[rows, :], low_ref[rows, :], high, low)
        store(rows, value * sign if parity else value)


def compose_rows(modes, sign, thigh_ref, tlow_ref, wait, store):
    count = modes.shape[0] // 2
    high, low = split(jnp.concatenate([modes[:count], modes[count:] * sign], axis=0))
    tile = thigh_ref.shape[0] // 3
    for piece in range(3):
        rows = pl.ds(piece * tile, tile)
        wait(0, piece)
        wait(1, piece)
        store(rows, three(thigh_ref[rows, :], tlow_ref[rows, :], high, low))


def turn_sign(part):
    return (1 - 2 * (part // 2)).astype(f32)


def analyze_kernel(scale, part_ref, own_hbm, other_ref, high_hbm, low_hbm, o_ref, field_hbm,
                   x_ref, high_ref, low_ref, pair_sem, sems, out_sem):
    part = part_ref[0]
    half = own_half(part)
    mine = pltpu.make_async_copy(lane_half(own_hbm, half), lon_half(x_ref, half), pair_sem)
    mine.start()
    wait = fetches((high_hbm, low_hbm), (high_ref, low_ref), sems, 2)
    lon_half(x_ref, 1 - half)[...] = other_ref[...]
    mine.wait()
    out = pltpu.make_async_copy(x_ref, field_hbm, out_sem)
    out.start()

    def store(rows, value):
        o_ref[rows, :] = value * scale

    analyze_rows(side_by_side(x_ref[...]), turn_sign(part), high_ref, low_ref, wait, store)
    out.wait()


def analyze(part, lon_total, own, other, high, low):
    rows, lons, _ = own.shape
    field = (rows, 2 * lons, LANES)
    return call(
        functools.partial(analyze_kernel, 1.0 / lon_total),
        (struct(2 * M, rows * LANES), kept(*field)),
        [smem] + hbm(1) + vmem(1) + hbm(2),
        [VMEM(field, f32), VMEM(high.shape, bf16), VMEM(high.shape, bf16)]
        + [pltpu.SemaphoreType.DMA, pltpu.SemaphoreType.DMA((2, 2)), pltpu.SemaphoreType.DMA],
        us=3.0,
        out_spaces=(VMEM, pltpu.HBM),
    )(part, own, other, high, low)


def grid_kernel(part_ref, s_ref, field_hbm, local_hbm, cot_hbm, first_hbm, second_hbm,
                high_hbm, low_hbm, thigh_hbm, tlow_hbm,
                mode_ref, own_hbm, send_first_hbm, send_second_hbm, err_hbm,
                x_ref, local_ref, cot_ref, spec_ref, out_ref, err_ref,
                high_ref, low_ref, thigh_ref, tlow_ref,
                back_sems, sems, cot_sems, other_sems, out_sems):
    part = part_ref[0]
    half, sign = own_half(part), turn_sign(part)
    wait_back = fetches((thigh_hbm, tlow_hbm), (thigh_ref, tlow_ref), back_sems, 3)
    others = [
        pltpu.make_async_copy(source, target, other_sems.at[index])
        for index, (source, target) in enumerate(((local_hbm, local_ref), (field_hbm, x_ref)))
    ]
    for copy in others:
        copy.start()
    others += pair_copies(half, cot_hbm, (first_hbm, second_hbm), cot_ref, cot_sems)
    wait = fetches((high_hbm, low_hbm), (high_ref, low_ref), sems, 2)

    def store_spec(rows, value):
        spec_ref[rows, :] = value

    modes = s_ref[...].reshape(thigh_ref.shape[1], s_ref.shape[2])
    compose_rows(modes, sign, thigh_ref, tlow_ref, wait_back, store_spec)
    for copy in others:
        copy.wait()
    tile = x_ref.shape[1] // 6
    for row in range(x_ref.shape[0]):
        for piece in range(6):
            lons = pl.ds(piece * tile, tile)
            hidden = local_ref[row, lons, :] + spec_ref[lons, pl.ds(row * LANES, LANES)]
            gate = 1.0 / (1.0 + jnp.exp(-hidden))
            out_ref[row, lons, :] = x_ref[row, lons, :] + hidden * gate
            err_ref[row, lons, :] = cot_ref[row, lons, :] * (gate * (1.0 + hidden * (1.0 - gate)))
    there = lon_half(out_ref, 1 - half)
    outs = [
        pltpu.make_async_copy(source, target, out_sems.at[index])
        for index, (source, target) in enumerate(
            (
                (err_ref, err_hbm),
                (lon_half(out_ref, half), own_hbm),
                (there.at[pl.ds(0, 1)], send_first_hbm),
                (there.at[pl.ds(1, 1)], send_second_hbm),
            )
        )
    ]
    for copy in outs:
        copy.start()

    def store(rows, value):
        mode_ref[rows, :] = value

    analyze_rows(side_by_side(err_ref[...]), sign, high_ref, low_ref, wait, store)
    for copy in outs:
        copy.wait()


def grid_stage(part, synthesis, field, local, cotangent, others, tables):
    rows, lons, _ = field.shape
    block = (rows, lons // 2, LANES)
    grid = VMEM(field.shape, f32)
    return call(
        grid_kernel,
        (
            struct(2 * M, rows * LANES),
            kept(*block),
            kept(1, *block[1:]),
            kept(1, *block[1:]),
            kept(*field.shape),
        ),
        [smem] + vmem(1) + hbm(9),
        [grid, grid, grid, VMEM((lons, rows * LANES), f32), grid, grid]
        + [VMEM(table.shape, bf16) for table in tables]
        + [pltpu.SemaphoreType.DMA((2, 3)), pltpu.SemaphoreType.DMA((2, 2))]
        + [pltpu.SemaphoreType.DMA((count,)) for count in (3, 2, 4)],
        us=4.0,
        limit=32,
        out_spaces=(VMEM,) + (pltpu.HBM,) * 4,
    )(part, synthesis, field, local, cotangent, *others, *tables)


def final_kernel(scale, rows_own, part_ref, s_ref, base_hbm, thigh_hbm, tlow_hbm,
                 send_ref, own_ref, share_ref, base_ref, thigh_ref, tlow_ref, sems, base_sem):
    part = part_ref[0]
    half = own_half(part)
    wait = fetches((thigh_hbm, tlow_hbm), (thigh_ref, tlow_ref), sems, 3)
    base_copy = pltpu.make_async_copy(base_hbm, base_ref, base_sem)
    base_copy.start()
    if rows_own < s_ref.shape[1]:
        share = jnp.sum(s_ref[:, pl.ds(rows_own, share_ref.shape[1]), :], axis=0)
        share_ref[...] = jnp.broadcast_to(share[None], share_ref.shape)
    modes = s_ref[:, pl.ds(0, rows_own), :].reshape(thigh_ref.shape[1], s_ref.shape[2])
    base_copy.wait()

    def store(lons, value):
        for row in range(base_ref.shape[0]):
            lanes = slice(row * LANES, (row + 1) * LANES)
            base_ref[row, lons, :] = base_ref[row, lons, :] + scale * value[:, lanes]

    compose_rows(modes, turn_sign(part), thigh_ref, tlow_ref, wait, store)
    own_ref[...] = lon_half(base_ref, half)[...]
    send_ref[...] = lon_half(base_ref, 1 - half)[...]


def final_stage(part, lon_total, rows_own, modes, base, high_t, low_t):
    rows, lons, _ = base.shape
    block = (rows, lons // 2, LANES)
    return call(
        functools.partial(final_kernel, 1.0 / lon_total, rows_own),
        (
            struct(*block),
            kept(*block),
            struct(modes.shape[0], max(modes.shape[1] - rows_own, 8), modes.shape[2]),
        ),
        [smem] + vmem(1) + hbm(3),
        [VMEM(base.shape, f32), VMEM(high_t.shape, bf16), VMEM(high_t.shape, bf16)]
        + [pltpu.SemaphoreType.DMA((2, 3)), pltpu.SemaphoreType.DMA],
        us=3.0,
    )(part, modes, base, high_t, low_t)


def filter_sums(prev_ref, own_ref, next_ref, edge_refs, coef_ref, finish, sums_ref):
    lons = own_ref.shape[1]
    tile = lons // 18
    sources = [(x_ref, row) for x_ref in (prev_ref, own_ref, next_ref) for row in range(2)]
    for row in range(2):
        def add(values, rows, row=row):
            for tap in range(KLON):
                total = values[0] * coef_ref[row, pl.ds(tap, 1), :]
                for offset in range(1, SPAN):
                    total = total + values[offset] * coef_ref[row, pl.ds(offset * KLON + tap, 1), :]
                sums_ref[tap, rows, :] = total

        near = sources[row : row + SPAN]
        edges = [(edge_ref, k) for edge_ref in edge_refs for k in range(2)][row : row + SPAN]
        add([edge_ref[k, pl.ds(8, 8), :] for edge_ref, k in edges], pl.ds(0, 8))
        add([edge_ref[k, pl.ds(0, 8), :] for edge_ref, k in edges], pl.ds(lons + 8, 8))

        @pl.loop(0, 18)
        def _(piece, near=near, add=add):
            start = pl.multiple_of(piece * tile, 8)
            values = [x_ref[k, pl.ds(start, tile), :] for x_ref, k in near]
            add(values, pl.ds(pl.multiple_of(start + 8, 8), tile))

        for piece in range(18):
            total = None
            for tap in range(KLON):
                value = sums_ref[tap, pl.ds(piece * tile + 8 + tap - KLON // 2, tile), :]
                total = value if total is None else total + value
            finish(row, pl.ds(piece * tile, tile), total)


def filter_kernel(prev_ref, own_ref, next_ref, lower_ref, middle_ref, upper_ref, o_ref, adjoint_ref,
                  sums_ref):
    def finish(row, lons, value):
        o_ref[row, lons, :] = value

    taps = pl.ds(EDGES, TAPS)
    coef_refs = [ref.at[:, taps] for ref in (lower_ref, middle_ref, upper_ref)]
    filter_sums(
        prev_ref, own_ref, next_ref, (lower_ref, middle_ref, upper_ref), coef_refs[1], finish, sums_ref
    )
    adjoint_ref[...] = jnp.zeros_like(adjoint_ref)
    sources = [(c_ref, row) for c_ref in coef_refs for row in range(2)]
    for row in range(2):
        for offset in range(SPAN):
            c_ref, k = sources[row + offset]
            for tap in range(KLON):
                mirrored = (SPAN - 1 - offset) * KLON + KLON - 1 - tap
                adjoint_ref[row, pl.ds(offset * KLON + tap, 1), :] = c_ref[k, pl.ds(mirrored, 1), :]


def adjoint_kernel(part_ref, prev_ref, own_ref, next_ref, lower_ref, middle_ref, upper_ref, coef_ref,
                   cot_hbm, first_hbm, second_hbm,
                   o_ref, sums_ref, cot_ref, cot_sems):
    copies = pair_copies(
        own_half(part_ref[0]), cot_hbm, (first_hbm, second_hbm), cot_ref, cot_sems
    )
    for copy in copies:
        copy.wait()

    def finish(row, lons, value):
        o_ref[row, lons, :] = cot_ref[row, lons, :] + value

    filter_sums(prev_ref, own_ref, next_ref, (lower_ref, middle_ref, upper_ref), coef_ref, finish, sums_ref)


def local_filter(prev, own, behind, *edges):
    return call(
        filter_kernel,
        (kept(*own.shape), kept(own.shape[0], TAPS, LANES)),
        loaded(3) + vmem(3),
        [VMEM((KLON, own.shape[1] + 16, LANES), f32)],
        us=4.0,
    )(prev, own, behind, *edges)


def adjoint_filter(part, prev, own, behind, lower, middle, upper, coef, cotangent, others):
    return call(
        adjoint_kernel,
        kept(*own.shape),
        [smem] + loaded(3) + vmem(4) + hbm(3),
        [VMEM((KLON, own.shape[1] + 16, LANES), f32), VMEM(own.shape, f32)]
        + [pltpu.SemaphoreType.DMA((3,))],
        us=4.0,
    )(part, prev, own, behind, lower, middle, upper, coef, cotangent, *others)


def coupling_kernel(lat_total, first_ref, gain_ref, o_hbm, step_ref, back_ref, start_ref, leg_ref,
                    scale_ref, padded_ref, column_ref, o_ref, out_sems):
    degree_count, chans = gain_ref.shape
    depth = padded_ref.shape[0]
    own = LANES // lat_total
    first_row = float((POLAR - lat_total) // 2)
    lane = lax.broadcasted_iota(jnp.int32, (1, LANES), 1)
    order = 2 * (lane % own) + first_ref[0]
    colatitude = math.pi * ((lane // own).astype(f32) + first_row) / POLAR
    cosine, log_sine = jnp.cos(colatitude), jnp.log(jnp.sin(colatitude))
    k = lax.broadcasted_iota(jnp.int32, (M, LANES), 0)
    k_f = k.astype(f32)
    log_terms = jnp.log((2.0 * k_f + 1.0) / jnp.maximum(2.0 * k_f, 1.0))
    log_norm = -0.5 * math.log(4.0 * math.pi) + 0.5 * jnp.sum(
        jnp.where((k > 0) & (k <= order), log_terms, 0.0), axis=0, keepdims=True
    )
    norm_start = jnp.exp(log_norm)
    degree = lax.broadcasted_iota(jnp.int32, (degree_count, LANES), 0)
    degree_f, order_f = degree.astype(f32), order.astype(f32)
    step = jnp.where(
        degree > order,
        jnp.sqrt(
            jnp.maximum(4.0 * degree_f * degree_f - 1.0, 0.0)
            / jnp.maximum(degree_f * degree_f - order_f * order_f, 1.0)
        ),
        0.0,
    )
    lower = degree_f - 1.0
    back = jnp.sqrt(
        jnp.maximum(lower * lower - order_f * order_f, 0.0) / (4.0 * lower * lower - 1.0)
    )
    step_ref[...] = step * cosine
    back_ref[...] = step * back
    start_ref[...] = jnp.where(degree == order, norm_start, 0.0)
    zeros = jnp.zeros((1, LANES), f32)

    def block(index, carry):
        previous, second, log_scale = carry
        first = pl.multiple_of(index * 8, 8)
        scale_ref[pl.ds(first, 8), :] = jnp.broadcast_to(log_scale, (8, LANES))
        for offset in range(8):
            row = pl.ds(first + offset, 1)
            rest = start_ref[row, :] - back_ref[row, :] * second
            current = step_ref[row, :] * previous + rest
            leg_ref[row, :] = current
            second, previous = previous, current
        too_large = jnp.abs(previous) > upper_bound
        second = jnp.where(too_large, second * lower_factor, second)
        previous = jnp.where(too_large, previous * lower_factor, previous)
        return previous, second, jnp.where(too_large, log_scale + log_step, log_scale)

    lax.fori_loop(0, degree_count // 8, block, (zeros, zeros, order_f * log_sine))
    leg_ref[pl.ds(0, degree_count), :] = leg_ref[pl.ds(0, degree_count), :] * jnp.exp(scale_ref[...])
    rest = depth - degree_count
    leg_ref[pl.ds(degree_count, rest), :] = jnp.zeros((rest, LANES), f32)
    padded_ref[pl.ds(0, degree_count), :] = gain_ref[...]
    padded_ref[pl.ds(degree_count, rest), :] = jnp.zeros((rest, chans), f32)
    column_ref[...] = leg_ref[...].T

    high, low = split(padded_ref[...])
    row = lax.broadcasted_iota(jnp.int32, (LANES, LANES), 0)
    quad = 2.0 * math.pi * math.pi / POLAR * jnp.sin(
        math.pi * ((row // own).astype(f32) + first_row) / POLAR
    )
    weight = quad * jnp.where(row % own + first_ref[0] == 0, 1.0, 2.0)
    weight = jnp.concatenate([weight] * (chans // LANES), axis=1)
    group = lat_total // out_sems.shape[0]
    copies = []
    for piece in range(out_sems.shape[0]):
        both = jnp.concatenate(
            [
                column_ref[...]
                * jnp.concatenate([column_ref[pl.ds(j * own, own), :]] * lat_total, axis=0)
                for j in range(piece * group, (piece + 1) * group)
            ],
            axis=0,
        )
        total = three(*split(both), high, low)
        for j in range(group):
            o_ref[piece * group + j] = (total[j * LANES : (j + 1) * LANES] * weight).reshape(
                lat_total, own, chans
            )
        block_of = pl.ds(piece * group, group)
        copies.append(
            pltpu.make_async_copy(o_ref.at[block_of], o_hbm.at[block_of], out_sems.at[piece])
        )
        copies[-1].start()
    for copy in copies:
        copy.wait()


def coupling(first_order, degree_gain, lat_total):
    degrees, chans = degree_gain.shape
    own = LANES // lat_total
    depth = (degrees + LANES - 1) // LANES * LANES
    table = (lat_total, lat_total, own, chans)
    rows = VMEM((degrees, LANES), f32)
    return call(
        functools.partial(coupling_kernel, lat_total),
        kept(*table),
        [smem] + loaded(1),
        [rows, rows, rows, VMEM((depth, LANES), f32), rows]
        + [VMEM((depth, chans), f32), VMEM((LANES, depth), f32), VMEM(table, f32)]
        + [pltpu.SemaphoreType.DMA((4,))],
        us=6.0,
        out_spaces=pltpu.HBM,
    )(first_order, degree_gain)


def gather_modes(r_ref, write, parts):
    for band in range(r_ref.shape[0] // parts):
        for half in range(2):
            both = r_ref[band * parts + half]
            for other in range(half + 2, parts, 2):
                both = both + r_ref[band * parts + other]
            for row in range(2):
                lanes = slice(row * LANES, (row + 1) * LANES)
                write(2 * band + row, pl.ds(half * LANES, LANES), both[:, lanes])


def scatter_modes(read, s_ref, parts, rows):
    for band in range(s_ref.shape[0] // parts):
        for part in range(parts):
            for row in range(2):
                lanes = pl.ds(row * LANES, LANES)
                value = read(2 * band + row, pl.ds(part % 2 * LANES, LANES))
                s_ref[band * parts + part, pl.ds(0, rows), lanes] = value


def forward_modes_kernel(parts, r_ref, coupling_hbm, w_hbm, x_ref, s_ref, y_ref, z_ref,
                         coupling_ref, w_ref, sems):
    wait_w = fetches((w_hbm,), (w_ref,), sems.at[pl.ds(0, 1)], 2)
    wait = fetches((coupling_hbm,), (coupling_ref,), sems.at[pl.ds(1, 1)], 8)

    def write(j, lanes, value):
        x_ref[j, :, lanes] = value

    gather_modes(r_ref, write, parts)
    lats, rows, chans = x_ref.shape
    own = rows // 2
    for piece in range(2):
        wait_w(0, piece)
    y_ref[...] = dot_split(
        x_ref[...].reshape(lats * rows, chans), w_ref[...], ((1,), (0,))
    ).reshape(lats, rows, chans)
    for piece in range(8):
        wait(0, piece)

        @pl.loop(piece * (lats // 8), (piece + 1) * (lats // 8))
        def _(j):
            totals = [jnp.zeros((own, chans), f32)] * 2
            for other in range(lats):
                factor = coupling_ref[j, other]
                for p in range(2):
                    totals[p] = totals[p] + factor * y_ref[other, pl.ds(p * own, own), :]
            for p in range(2):
                z_ref[j, pl.ds(p * own, own), :] = totals[p]

    scatter_modes(lambda j, lanes: z_ref[j, :, lanes], s_ref, parts, rows)


def backward_modes_kernel(parts, r_ref, coupling_hbm, w_hbm, x_hbm, s_ref, e_ref, v_ref,
                          coupling_ref, w_ref, x_ref, sems):
    wait = fetches((coupling_hbm,), (coupling_ref,), sems.at[pl.ds(0, 1)], 8)
    wait_rest = fetches((w_hbm, x_hbm), (w_ref, x_ref), sems.at[pl.ds(1, 2)], 2)

    def write(j, lanes, value):
        e_ref[j, :, lanes] = value

    gather_modes(r_ref, write, parts)
    lats, rows, chans = x_ref.shape
    own = rows // 2
    for piece in range(8):
        wait(0, piece)

    @pl.loop(0, lats)
    def _(j):
        totals = [jnp.zeros((own, chans), f32)] * 2
        for other in range(lats):
            factor = coupling_ref[other, j]
            for p in range(2):
                totals[p] = totals[p] + factor * e_ref[other, pl.ds(p * own, own), :]
        for p in range(2):
            v_ref[j, pl.ds(p * own, own), :] = totals[p]

    for piece in range(2):
        for index in range(2):
            wait_rest(index, piece)
    v = v_ref[...].reshape(lats * rows, chans)
    e_ref[...] = dot_split(v, w_ref[...], ((1,), (1,))).reshape(lats, rows, chans)
    scatter_modes(lambda j, lanes: e_ref[j, :, lanes], s_ref, parts, rows)
    weight_part = dot_split(x_ref[...].reshape(lats * rows, chans), v, ((0,), (0,)))
    share = chans // s_ref.shape[0]
    s_ref[:, pl.ds(rows, share), :] = weight_part.reshape(s_ref.shape[0], share, chans)


def legendre_orders(colatitude, orders, log_norm, degree_count):
    cosine = jnp.cos(colatitude)[None, :]
    log_sine = jnp.log(jnp.sin(colatitude))[None, :]
    order_f = orders.astype(f32)[:, None]
    norm_start = jnp.exp(log_norm)[:, None] + jnp.zeros_like(cosine)
    zeros_state = jnp.zeros((orders.shape[0], colatitude.shape[0]), f32)

    def advance(carry, degree):
        previous, second, log_scale = carry
        degree_f = degree.astype(f32)
        step_factor = jnp.where(
            degree > orders[:, None],
            jnp.sqrt(
                jnp.maximum(4.0 * degree_f * degree_f - 1.0, 0.0)
                / jnp.maximum(degree_f * degree_f - order_f * order_f, 1.0)
            ),
            0.0,
        )
        lower_degree = degree_f - 1.0
        back_factor = jnp.sqrt(
            jnp.maximum(lower_degree * lower_degree - order_f * order_f, 0.0)
            / (4.0 * lower_degree * lower_degree - 1.0)
        )
        current = jnp.where(
            degree == orders[:, None],
            norm_start,
            step_factor * (cosine * previous - back_factor * second),
        )
        too_large = jnp.abs(current) > upper_bound
        current = jnp.where(too_large, current * lower_factor, current)
        previous = jnp.where(too_large, previous * lower_factor, previous)
        log_scale = jnp.where(too_large, log_scale + log_step, log_scale)
        return ((current, previous, log_scale), current * jnp.exp(log_scale))

    start_state = (zeros_state, zeros_state, order_f * log_sine)
    _, tables = lax.scan(advance, start_state, jnp.arange(degree_count, dtype=jnp.int32), unroll=8)
    return tables


def plain_gather(received, parts, own):
    bands = received.shape[0] // parts
    blocks = received.reshape(bands, parts // 2, 2, 2, own, 2, LANES).sum(axis=1)
    return blocks.transpose(0, 4, 2, 3, 1, 5).reshape(2 * bands, 2, own, 2 * LANES)


def plain_scatter(modes, parts):
    lats, _, own, _ = modes.shape
    bands = lats // 2
    blocks = modes.reshape(bands, 2, 2, own, 2, LANES).transpose(0, 4, 2, 3, 1, 5)
    blocks = jnp.broadcast_to(blocks[:, None], (bands, parts // 2) + blocks.shape[1:])
    return blocks.reshape(bands * parts, 2 * own, 2 * LANES)


def mode_factors(first_order, own, lat_total, degree_gain):
    if own % 8 == 0 and own * lat_total == LANES and degree_gain.shape[0] % 8 == 0:
        return coupling(first_order[None], degree_gain, lat_total)
    orders = first_order + 2 * jnp.arange(own, dtype=jnp.int32)
    log_norm = jnp.take(log_norms(M), orders)
    return legendre_orders(grid_tables(lat_total)[0], orders, log_norm, degree_gain.shape[0])


def mode_stages(first_order, own, parts, factors, degree_gain, spec_weight):
    if factors.ndim == 4:
        chans = spec_weight.shape[0]
        shape = (factors.shape[0], 2 * own, chans)

        def forward(received):
            return call(
                functools.partial(forward_modes_kernel, parts),
                (kept(*shape), struct(*received.shape)),
                vmem(1) + hbm(2),
                [VMEM(shape, f32), VMEM(shape, f32), VMEM(factors.shape, f32)]
                + [VMEM(spec_weight.shape, f32), pltpu.SemaphoreType.DMA((2, 8))],
                us=2.0,
            )(received, factors, spec_weight)

        def backward(received, spectrum):
            return call(
                functools.partial(backward_modes_kernel, parts),
                struct(received.shape[0], 2 * own + chans // received.shape[0], chans),
                vmem(1) + hbm(3),
                [VMEM(shape, f32), VMEM(shape, f32), VMEM(factors.shape, f32)]
                + [VMEM(spec_weight.shape, f32), VMEM(shape, f32), pltpu.SemaphoreType.DMA((3, 8))],
                us=2.0,
            )(received, factors, spec_weight, spectrum)

        return forward, backward

    legendre, lat_total = factors, factors.shape[2]
    quad_weight = grid_tables(lat_total)[1]
    orders = first_order + 2 * jnp.arange(own, dtype=jnp.int32)
    order_weight = jnp.where(orders == 0, 1.0, 2.0).astype(f32)[None, None, :, None]
    quad_column = quad_weight[:, None, None, None]
    dot = functools.partial(jnp.einsum, precision=highest)

    def forward(received):
        spectrum = plain_gather(received, parts, own)
        mixed = dot("jpmc,cd->jpmd", spectrum, spec_weight) * quad_column
        degree = dot("lmj,jpmd->lpmd", legendre, mixed) * degree_gain[:, None, None, :]
        synthesis = dot("lmj,lpmd->jpmd", legendre, degree) * order_weight
        return spectrum, plain_scatter(synthesis, parts)

    def backward(received, spectrum):
        error = plain_gather(received, parts, own) * order_weight
        gained = dot("lmj,jpmd->lpmd", legendre, error) * degree_gain[:, None, None, :]
        back = dot("lmj,lpmd->jpmd", legendre, gained) * quad_column
        sent = plain_scatter(dot("jpmd,cd->jpmc", back, spec_weight), parts)
        weight_part = dot("jpmc,jpmd->cd", spectrum, back)
        shares = weight_part.reshape(sent.shape[0], -1, weight_part.shape[1])
        return jnp.concatenate([sent, shares], axis=1)

    return forward, backward


def filter_coefficients(filters, disco_weight, band_start, band_reach):
    coefficient = jnp.einsum("ikrt,kc->irtc", filters, disco_weight, precision=highest)
    window = jnp.arange(WIN, dtype=jnp.int32)
    coefficient = jnp.where(
        (window[None, :] < band_reach[:, None])[:, :, None, None], coefficient, 0.0
    )
    offset = jnp.arange(-HMAX, HMAX + 1, dtype=jnp.int32)
    lands = offset[None, :, None] == band_start[:, None, None] + window[None, None, :]
    by_offset = jnp.sum(
        jnp.where(lands[:, :, :, None, None], coefficient[:, None], 0.0), axis=2
    )
    coef = by_offset.reshape(filters.shape[0], SPAN * KLON, LANES)
    return jnp.pad(coef, ((0, 0), (0, TAPS - SPAN * KLON), (0, 0)))


def swap_parts(x, axis):
    return lax.all_to_all(x, axis, split_axis=0, concat_axis=0, tiled=True)


def after(first, *later):
    return lax.optimization_barrier((first, *later))


def body(
    grid_field, filters, disco_weight, band_start, band_reach, spec_weight, degree_gain, cotangent
):
    band_rows, lon_local, chans = grid_field.shape
    bands, parts = lax.axis_size("lat"), lax.axis_size("chan")
    devices = bands * parts
    lat_total, lon_total = band_rows * bands, lon_local * parts
    own, share = M // devices, chans // devices
    assert band_rows == HMAX and chans == 2 * LANES and parts == 4
    band, part = lax.axis_index("lat"), lax.axis_index("chan")
    me, half, part_index = band * parts + part, part % 2, part[None]
    both_axes = ("lat", "chan")
    high, low = wave_tables(lon_total, own)
    high_t, low_t = (jnp.asarray(np.ascontiguousarray(t.T)) for t in (high, low))
    high, low = jnp.asarray(high), jnp.asarray(low)
    up = [(i, i + 1) for i in range(bands - 1)]
    down = [(i + 1, i) for i in range(bands - 1)]

    def halo(x):
        return lax.ppermute(x, "lat", up), x, lax.ppermute(x, "lat", down)

    def part_swap(x, distance):
        return lax.ppermute(x, "chan", [(i, i ^ distance) for i in range(parts)])

    def half_of(x, which):
        return lax.dynamic_slice_in_dim(x, which * LANES, LANES, axis=2)

    def edges(x):
        return part_swap(jnp.concatenate([x[:, :8], x[:, -8:]], axis=1), 2)

    def exchange(modes):
        return swap_parts(modes.reshape(devices, -1, modes.shape[-1]), both_axes)

    outgoing, cotangent, degree_gain, disco_weight, band_start = after(
        half_of(grid_field, 1 - half), cotangent, degree_gain, disco_weight, band_start
    )
    field_other = part_swap(outgoing, 1)
    first_order = owned_orders(me, devices)
    factors = mode_factors(first_order, own, lat_total, degree_gain)
    cot_out = half_of(cotangent, 1 - half)
    field_other, factors, cot_out = after(field_other, factors, cot_out)
    modes, field = analyze(part_index, lon_total, grid_field, field_other, high, low)

    modes, field_sent, cot_out, disco_weight, band_start = after(
        modes, field, cot_out, disco_weight, band_start
    )
    mine = lax.dynamic_slice_in_dim(disco_weight, half * LANES, LANES, axis=1)
    coef = filter_coefficients(filters, mine, band_start, band_reach)
    rows = halo(field_sent)
    cot_others = [part_swap(cot_out[row : row + 1], 1) for row in range(band_rows)]
    received, edge, cot_others[0] = after(exchange(modes), edges(field_sent), cot_others[0])
    forward, backward = mode_stages(first_order, own, parts, factors, degree_gain, spec_weight)
    spectrum, synthesis = forward(received)

    local, adjoint = local_filter(*rows, *halo(jnp.concatenate([edge, coef], axis=1)))
    error_modes, out_own, *out_sends, error = grid_stage(
        part_index, exchange(synthesis), field, local, cotangent, cot_others,
        (high, low, high_t, low_t),
    )

    out_others = [part_swap(x, 1) for x in out_sends]
    rows = list(halo(error))
    received, edge, out_others[0], rows[0] = after(
        exchange(error_modes), edges(error), out_others[0], rows[0]
    )
    sent = backward(received, spectrum)
    base = adjoint_filter(part_index, *rows, *halo(edge), adjoint, cotangent, cot_others)
    received = exchange(sent)
    if own % 8 == 0:
        grad_send, grad_own, shares = final_stage(
            part_index, lon_total, 2 * own, received, base, high_t, low_t
        )
    else:
        grad_send, grad_own, _ = final_stage(
            part_index, lon_total, 2 * own, received[:, : 2 * own], base, high_t, low_t
        )
        shares = jnp.sum(received[:, 2 * own :], axis=0, keepdims=True)
        shares = jnp.broadcast_to(shares, (devices,) + shares.shape[1:])
    grad_send, *out_others = after(grad_send, *out_others)
    output, shares = after(join(part_index, out_own, *out_others), shares)
    grad_input = join(part_index, grad_own, part_swap(grad_send, 1))
    grad_weight = swap_parts(shares, both_axes).reshape(chans, chans)
    return (output, grad_input, grad_weight)


def solution(mesh):
    in_specs = (
        P("lat", "chan", None),
        P("lat", None, None, None),
        P(),
        P("lat"),
        P("lat"),
        P(),
        P(),
        P("lat", "chan", None),
    )
    out_specs = (P("lat", "chan", None), P("lat", "chan", None), P())
    return jax.shard_map(body, mesh=mesh, in_specs=in_specs, out_specs=out_specs, check_vma=False)
```

```python
import functools
import math

import jax
import jax.numpy as jnp
import ml_dtypes
import numpy as np
from jax import lax
from jax.experimental import pallas as pl
from jax.experimental.pallas import tpu as pltpu
from jax.sharding import PartitionSpec as P

L = 360
M = 256
WIN = 3
HMAX = 2
KLON = 5
POLAR = 720
SPAN = 2 * HMAX + 1
TAPS = 32
EDGES = 16
LANES = 128
MIB = 2**20


highest = lax.Precision.HIGHEST
upper_bound = 2.0**32
lower_factor = 2.0 ** (-32)
log_step = 32.0 * math.log(2.0)

f32 = jnp.float32
bf16 = jnp.bfloat16
VMEM = pltpu.VMEM


@functools.lru_cache(maxsize=None)
def wave_tables(lon_total, own_count):
    orders = np.concatenate([np.arange(0, M, 2), np.arange(1, M, 2)]).reshape(-1, own_count)
    lons = np.arange(lon_total // 2)
    angle = (orders[:, :, None] * lons) % lon_total * (2.0 * np.pi / lon_total)
    table = np.stack([np.cos(angle), -np.sin(angle)], axis=1).reshape(2 * M, lon_total // 2)
    high = table.astype(ml_dtypes.bfloat16)
    low = (table - high.astype(np.float64)).astype(ml_dtypes.bfloat16)
    return high, low


def half_tables(table, depth):
    rows, lons = table.shape
    blocks = table.reshape(rows, 2, lons // 2).transpose(1, 0, 2)
    return np.pad(blocks, ((0, 0), (0, 0), (0, depth - lons // 2)))


def owned_orders(owner, devices):
    half = devices // 2
    return owner % half * (2 * (M // devices)) + owner // half


def grid_tables(lat_total):
    first_row = (POLAR - lat_total) // 2
    colatitude = math.pi * (jnp.arange(lat_total, dtype=f32) + float(first_row)) / POLAR
    quad_weight = 2.0 * math.pi * math.pi / POLAR * jnp.sin(colatitude)
    return (colatitude, quad_weight)


def log_norms(order_count):
    order_index = jnp.arange(order_count, dtype=f32)
    log_terms = jnp.where(
        order_index > 0.0,
        jnp.log((2.0 * order_index + 1.0) / jnp.maximum(2.0 * order_index, 1.0)),
        0.0,
    )
    return -0.5 * math.log(4.0 * math.pi) + 0.5 * jnp.cumsum(log_terms)


def split(x):
    high = x.astype(bf16)
    return high, (x - high.astype(f32)).astype(bf16)


def dot_split(a, b, dims):
    (ah, al), (bh, bl) = split(a), split(b)
    dot = lambda u, v: lax.dot_general(u, v, (dims, ((), ())), preferred_element_type=f32)
    return dot(ah, bh) + (dot(ah, bl) + dot(al, bh))


def cost(us):
    return pl.CostEstimate(flops=int(us * 1e9), bytes_accessed=int(us * 3e6), transcendentals=0)


def call(kernel, out_shape, in_specs, scratch=(), us=1.0, limit=16, out_spaces=None, aliases=None):
    run = pl.pallas_call(
        kernel,
        out_shape=out_shape,
        in_specs=[pl.BlockSpec(memory_space=space) for space, _ in in_specs],
        out_specs=jax.tree.map(
            lambda space: pl.BlockSpec(memory_space=space),
            out_spaces or jax.tree.map(lambda _: VMEM, out_shape),
        ),
        scratch_shapes=list(scratch),
        input_output_aliases=aliases or {},
        compiler_params=pltpu.CompilerParams(vmem_limit_bytes=limit * MIB),
        cost_estimate=cost(us),
    )
    keeps = [keep for _, keep in in_specs]
    return lambda *args: run(
        *[held(x) if keep else x for x, keep in zip(args, keeps, strict=True)]
    )


def held(x):
    return pltpu.with_memory_space_constraint(x, pltpu.HBM)


def vmem(count):
    return [(VMEM, False)] * count


def loaded(count):
    return [(VMEM, True)] * count


def hbm(count):
    return [(pltpu.HBM, True)] * count


smem = (pltpu.SMEM, False)


def struct(*shape, dtype=f32):
    return jax.ShapeDtypeStruct(shape, dtype)


def kept(*shape, dtype=f32):
    return pltpu.HBM(shape, dtype)


def own_half(part):
    return part % 2


def lane_half(x_ref, half):
    return x_ref.at[:, :, pl.ds(pl.multiple_of(half * LANES, LANES), LANES)]


def lon_half(x_ref, half):
    width = x_ref.shape[1] // 2
    return x_ref.at[:, pl.ds(pl.multiple_of(half * width, 8), width), :]


def pair_copies(half, own_hbm, other_hbms, target, sems):
    copies = [pltpu.make_async_copy(lane_half(own_hbm, half), lon_half(target, half), sems.at[0])]
    there = lon_half(target, 1 - half)
    for row, other_hbm in enumerate(other_hbms):
        copies.append(
            pltpu.make_async_copy(other_hbm, there.at[pl.ds(row, 1)], sems.at[1 + row])
        )
    for copy in copies:
        copy.start()
    return copies


def join_kernel(part_ref, own_ref, *refs):
    o_ref = refs[-1]
    half = own_half(part_ref[0])
    mine, theirs = (
        pl.ds(pl.multiple_of(place * LANES, LANES), LANES) for place in (half, 1 - half)
    )
    o_ref[:, :, mine] = own_ref[...]
    for row, other_ref in enumerate(refs[:-1]):
        o_ref[pl.ds(row, other_ref.shape[0]), :, theirs] = other_ref[...]


def join(part, own, *others):
    rows, lons, _ = own.shape
    return call(
        join_kernel, kept(rows, lons, 2 * LANES), [smem] + vmem(1 + len(others))
    )(part, own, *others)


def side_by_side(x):
    return jnp.concatenate([x[0], x[1]], axis=1)


def three(table_high, table_low, high, low):
    dot = lambda u, v: jnp.dot(u, v, preferred_element_type=f32)
    return dot(table_high, high) + (dot(table_high, low) + dot(table_low, high))


def fetches(sources, targets, sems, pieces):
    copies = []
    for index, (source, target) in enumerate(zip(sources, targets, strict=True)):
        tile = source.shape[0] // pieces
        copies.append(
            [
                pltpu.make_async_copy(
                    source.at[pl.ds(piece * tile, tile)],
                    target.at[pl.ds(piece * tile, tile)],
                    sems.at[index, piece],
                )
                for piece in range(pieces)
            ]
        )
    for piece in range(pieces):
        for group in copies:
            group[piece].start()
    return lambda index, piece: copies[index][piece].wait()


def analyze_rows(x, sign, high_ref, low_ref, wait, store):
    high, low = split(x)
    tile = high_ref.shape[0] // 2
    for parity in range(2):
        rows = pl.ds(parity * tile, tile)
        wait(0, parity)
        wait(1, parity)
        value = three(high_ref[rows, :], low_ref[rows, :], high, low)
        store(rows, value * sign if parity else value)


def compose_rows(modes, sign, thigh_ref, tlow_ref, wait, store):
    count = modes.shape[0] // 2
    high, low = split(jnp.concatenate([modes[:count], modes[count:] * sign], axis=0))
    tile = thigh_ref.shape[0] // 3
    for piece in range(3):
        rows = pl.ds(piece * tile, tile)
        wait(0, piece)
        wait(1, piece)
        store(rows, three(thigh_ref[rows, :], tlow_ref[rows, :], high, low))


def turn_sign(part):
    return (1 - 2 * (part // 2)).astype(f32)


def analyze_kernel(scale, part_ref, own_hbm, other_ref, high_hbm, low_hbm, o_ref, field_hbm,
                   x_ref, high_ref, low_ref, pair_sem, sems, out_sem):
    part = part_ref[0]
    half = own_half(part)
    mine = pltpu.make_async_copy(lane_half(own_hbm, half), lon_half(x_ref, half), pair_sem)
    mine.start()
    wait = fetches((high_hbm, low_hbm), (high_ref, low_ref), sems, 2)
    lon_half(x_ref, 1 - half)[...] = other_ref[...]
    mine.wait()
    out = pltpu.make_async_copy(x_ref, field_hbm, out_sem)
    out.start()

    def store(rows, value):
        o_ref[rows, :] = value * scale

    analyze_rows(side_by_side(x_ref[...]), turn_sign(part), high_ref, low_ref, wait, store)
    out.wait()


def analyze(part, lon_total, own, other, high, low):
    rows, lons, _ = own.shape
    field = (rows, 2 * lons, LANES)
    return call(
        functools.partial(analyze_kernel, 1.0 / lon_total),
        (struct(2 * M, rows * LANES), kept(*field)),
        [smem] + hbm(1) + vmem(1) + hbm(2),
        [VMEM(field, f32), VMEM(high.shape, bf16), VMEM(high.shape, bf16)]
        + [pltpu.SemaphoreType.DMA, pltpu.SemaphoreType.DMA((2, 2)), pltpu.SemaphoreType.DMA],
        us=3.0,
        out_spaces=(VMEM, pltpu.HBM),
    )(part, own, other, high, low)


def grid_kernel(part_ref, s_ref, field_hbm, local_hbm, cot_hbm, first_hbm, second_hbm,
                high_hbm, low_hbm, thigh_hbm, tlow_hbm,
                mode_ref, own_hbm, send_first_hbm, send_second_hbm, err_hbm,
                x_ref, local_ref, cot_ref, spec_ref, out_ref, err_ref,
                high_ref, low_ref, thigh_ref, tlow_ref,
                back_sems, sems, cot_sems, other_sems, out_sems):
    part = part_ref[0]
    half, sign = own_half(part), turn_sign(part)
    wait_back = fetches((thigh_hbm, tlow_hbm), (thigh_ref, tlow_ref), back_sems, 3)
    others = [
        pltpu.make_async_copy(source, target, other_sems.at[index])
        for index, (source, target) in enumerate(((local_hbm, local_ref), (field_hbm, x_ref)))
    ]
    for copy in others:
        copy.start()
    others += pair_copies(half, cot_hbm, (first_hbm, second_hbm), cot_ref, cot_sems)
    wait = fetches((high_hbm, low_hbm), (high_ref, low_ref), sems, 2)

    def store_spec(rows, value):
        spec_ref[rows, :] = value

    modes = s_ref[...].reshape(thigh_ref.shape[1], s_ref.shape[2])
    compose_rows(modes, sign, thigh_ref, tlow_ref, wait_back, store_spec)
    for copy in others:
        copy.wait()
    tile = x_ref.shape[1] // 6
    for row in range(x_ref.shape[0]):
        for piece in range(6):
            lons = pl.ds(piece * tile, tile)
            hidden = local_ref[row, lons, :] + spec_ref[lons, pl.ds(row * LANES, LANES)]
            gate = 1.0 / (1.0 + jnp.exp(-hidden))
            out_ref[row, lons, :] = x_ref[row, lons, :] + hidden * gate
            err_ref[row, lons, :] = cot_ref[row, lons, :] * (gate * (1.0 + hidden * (1.0 - gate)))
    there = lon_half(out_ref, 1 - half)
    outs = [
        pltpu.make_async_copy(source, target, out_sems.at[index])
        for index, (source, target) in enumerate(
            (
                (err_ref, err_hbm),
                (lon_half(out_ref, half), own_hbm),
                (there.at[pl.ds(0, 1)], send_first_hbm),
                (there.at[pl.ds(1, 1)], send_second_hbm),
            )
        )
    ]
    for copy in outs:
        copy.start()

    def store(rows, value):
        mode_ref[rows, :] = value

    analyze_rows(side_by_side(err_ref[...]), sign, high_ref, low_ref, wait, store)
    for copy in outs:
        copy.wait()


def grid_stage(part, synthesis, field, local, cotangent, others, tables):
    rows, lons, _ = field.shape
    block = (rows, lons // 2, LANES)
    grid = VMEM(field.shape, f32)
    return call(
        grid_kernel,
        (
            struct(2 * M, rows * LANES),
            kept(*block),
            kept(1, *block[1:]),
            kept(1, *block[1:]),
            kept(*field.shape),
        ),
        [smem] + vmem(1) + hbm(9),
        [grid, grid, grid, VMEM((lons, rows * LANES), f32), grid, grid]
        + [VMEM(table.shape, bf16) for table in tables]
        + [pltpu.SemaphoreType.DMA((2, 3)), pltpu.SemaphoreType.DMA((2, 2))]
        + [pltpu.SemaphoreType.DMA((count,)) for count in (3, 2, 4)],
        us=4.0,
        limit=32,
        out_spaces=(VMEM,) + (pltpu.HBM,) * 4,
    )(part, synthesis, field, local, cotangent, *others, *tables)


def final_kernel(scale, rows_own, theirs, part_ref, s_ref, base_hbm, thigh_hbm, tlow_hbm,
                 *refs):
    o_ref, base_ref, thigh_ref, tlow_ref, sems, base_sem = refs[-6:]
    out_hbm = refs[0]
    part = part_ref[0]
    half = 1 - own_half(part) if theirs else own_half(part)
    wait = fetches((thigh_hbm.at[half], tlow_hbm.at[half]), (thigh_ref, tlow_ref), sems, 3)
    base_copy = pltpu.make_async_copy(lon_half(base_hbm, half), base_ref, base_sem)
    base_copy.start()
    modes = s_ref[:, pl.ds(0, rows_own), :].reshape(thigh_ref.shape[1], s_ref.shape[2])
    total = o_ref.shape[1]

    def store(lons, value):
        count = min(lons.size, total - lons.start)
        for row in range(base_ref.shape[0]):
            lanes = slice(row * LANES, (row + 1) * LANES)
            o_ref[row, pl.ds(lons.start, count), :] = scale * value[:count, lanes]

    compose_rows(modes, turn_sign(part), thigh_ref, tlow_ref, wait, store)
    base_copy.wait()
    o_ref[...] = o_ref[...] + base_ref[...]
    if not theirs:
        out = pltpu.make_async_copy(o_ref, lane_half(out_hbm, half), base_sem)
        out.start()
        out.wait()


def final_stage(part, lon_total, rows_own, modes, base, high_t, low_t, theirs):
    rows, lons, _ = base.shape
    block = (rows, lons // 2, LANES)
    table = high_t.shape[1:]
    return call(
        functools.partial(final_kernel, 1.0 / lon_total, rows_own, theirs),
        struct(*block) if theirs else kept(rows, lons // 2, 2 * LANES),
        [smem] + vmem(1) + hbm(3),
        [VMEM(block, f32)] * (1 if theirs else 2)
        + [VMEM(table, bf16), VMEM(table, bf16)]
        + [pltpu.SemaphoreType.DMA((2, 3)), pltpu.SemaphoreType.DMA],
        us=2.0,
        out_spaces=VMEM if theirs else pltpu.HBM,
    )(part, modes, base, high_t, low_t)


def close_kernel(part_ref, held_hbm, other_ref, weight_ref, o_hbm, weight_hbm, sems):
    del held_hbm
    copies = (
        pltpu.make_async_copy(other_ref, lane_half(o_hbm, 1 - own_half(part_ref[0])), sems.at[0]),
        pltpu.make_async_copy(weight_ref, weight_hbm, sems.at[1]),
    )
    for copy in copies:
        copy.start()
    for copy in copies:
        copy.wait()


def close(part, held_half, other, weight):
    return call(
        close_kernel,
        (kept(*held_half.shape), kept(*weight.shape)),
        [smem] + hbm(1) + vmem(2),
        [pltpu.SemaphoreType.DMA((2,))],
        out_spaces=(pltpu.HBM, pltpu.HBM),
        aliases={1: 0},
    )(part, held_half, other, weight)


def shares_kernel(first, r_ref, o_ref):
    share = jnp.sum(r_ref[:, pl.ds(first, o_ref.shape[1]), :], axis=0)
    o_ref[...] = jnp.broadcast_to(share[None], o_ref.shape)


def spread_shares(received, first):
    devices, rows, chans = received.shape
    return call(
        functools.partial(shares_kernel, first), struct(devices, rows - first, chans), vmem(1)
    )(received)


def filter_sums(refs, edge_refs, coef_ref, finish, sums_ref):
    lons = refs[0].shape[1]
    tile = lons // 18
    sources = [(x_ref, row) for x_ref in refs for row in range(x_ref.shape[0])]
    for row in range(2):
        def add(values, rows, row=row):
            for tap in range(KLON):
                total = values[0] * coef_ref[row, pl.ds(tap, 1), :]
                for offset in range(1, SPAN):
                    total = total + values[offset] * coef_ref[row, pl.ds(offset * KLON + tap, 1), :]
                sums_ref[tap, rows, :] = total

        near = sources[row : row + SPAN]
        edges = [(edge_ref, k) for edge_ref in edge_refs for k in range(2)][row : row + SPAN]
        add([edge_ref[k, pl.ds(8, 8), :] for edge_ref, k in edges], pl.ds(0, 8))
        add([edge_ref[k, pl.ds(0, 8), :] for edge_ref, k in edges], pl.ds(lons + 8, 8))

        @pl.loop(0, 18)
        def _(piece, near=near, add=add):
            start = pl.multiple_of(piece * tile, 8)
            values = [x_ref[k, pl.ds(start, tile), :] for x_ref, k in near]
            add(values, pl.ds(pl.multiple_of(start + 8, 8), tile))

        for piece in range(18):
            total = None
            for tap in range(KLON):
                value = sums_ref[tap, pl.ds(piece * tile + 8 + tap - KLON // 2, tile), :]
                total = value if total is None else total + value
            finish(row, pl.ds(piece * tile, tile), total)


def filter_kernel(prev_ref, own_ref, next_ref, lower_ref, middle_ref, upper_ref, o_ref, adjoint_ref,
                  sums_ref):
    def finish(row, lons, value):
        o_ref[row, lons, :] = value

    taps = pl.ds(EDGES, TAPS)
    coef_refs = [ref.at[:, taps] for ref in (lower_ref, middle_ref, upper_ref)]
    filter_sums(
        (prev_ref, own_ref, next_ref), (lower_ref, middle_ref, upper_ref), coef_refs[1], finish, sums_ref
    )
    adjoint_ref[...] = jnp.zeros_like(adjoint_ref)
    sources = [(c_ref, row) for c_ref in coef_refs for row in range(2)]
    for row in range(2):
        for offset in range(SPAN):
            c_ref, k = sources[row + offset]
            for tap in range(KLON):
                mirrored = (SPAN - 1 - offset) * KLON + KLON - 1 - tap
                adjoint_ref[row, pl.ds(offset * KLON + tap, 1), :] = c_ref[k, pl.ds(mirrored, 1), :]


def adjoint_kernel(part_ref, first_ref, second_ref, own_ref, next_ref, lower_ref, middle_ref, upper_ref, coef_ref,
                   cot_hbm, first_hbm, second_hbm,
                   o_ref, sums_ref, cot_ref, cot_sems):
    copies = pair_copies(
        own_half(part_ref[0]), cot_hbm, (first_hbm, second_hbm), cot_ref, cot_sems
    )
    for copy in copies:
        copy.wait()

    def finish(row, lons, value):
        o_ref[row, lons, :] = cot_ref[row, lons, :] + value

    edge_refs = (lower_ref, middle_ref, upper_ref)
    filter_sums((first_ref, second_ref, own_ref, next_ref), edge_refs, coef_ref, finish, sums_ref)


def local_filter(prev, own, behind, *edges):
    return call(
        filter_kernel,
        (kept(*own.shape), kept(own.shape[0], TAPS, LANES)),
        loaded(3) + vmem(3),
        [VMEM((KLON, own.shape[1] + 16, LANES), f32)],
        us=4.0,
    )(prev, own, behind, *edges)


def adjoint_filter(part, first, second, own, behind, lower, middle, upper, coef, cotangent, others):
    return call(
        adjoint_kernel,
        kept(*own.shape),
        [smem] + loaded(4) + vmem(4) + hbm(3),
        [VMEM((KLON, own.shape[1] + 16, LANES), f32), VMEM(own.shape, f32)]
        + [pltpu.SemaphoreType.DMA((3,))],
        us=4.0,
    )(part, first, second, own, behind, lower, middle, upper, coef, cotangent, *others)


def coupling_kernel(lat_total, first_ref, gain_ref, o_hbm, step_ref, back_ref, start_ref, leg_ref,
                    scale_ref, padded_ref, column_ref, o_ref, out_sems):
    degree_count, chans = gain_ref.shape
    depth = padded_ref.shape[0]
    own = LANES // lat_total
    first_row = float((POLAR - lat_total) // 2)
    lane = lax.broadcasted_iota(jnp.int32, (1, LANES), 1)
    order = 2 * (lane % own) + first_ref[0]
    colatitude = math.pi * ((lane // own).astype(f32) + first_row) / POLAR
    cosine, log_sine = jnp.cos(colatitude), jnp.log(jnp.sin(colatitude))
    k = lax.broadcasted_iota(jnp.int32, (M, LANES), 0)
    k_f = k.astype(f32)
    log_terms = jnp.log((2.0 * k_f + 1.0) / jnp.maximum(2.0 * k_f, 1.0))
    log_norm = -0.5 * math.log(4.0 * math.pi) + 0.5 * jnp.sum(
        jnp.where((k > 0) & (k <= order), log_terms, 0.0), axis=0, keepdims=True
    )
    norm_start = jnp.exp(log_norm)
    degree = lax.broadcasted_iota(jnp.int32, (degree_count, LANES), 0)
    degree_f, order_f = degree.astype(f32), order.astype(f32)
    step = jnp.where(
        degree > order,
        jnp.sqrt(
            jnp.maximum(4.0 * degree_f * degree_f - 1.0, 0.0)
            / jnp.maximum(degree_f * degree_f - order_f * order_f, 1.0)
        ),
        0.0,
    )
    lower = degree_f - 1.0
    back = jnp.sqrt(
        jnp.maximum(lower * lower - order_f * order_f, 0.0) / (4.0 * lower * lower - 1.0)
    )
    step_ref[...] = step * cosine
    back_ref[...] = step * back
    start_ref[...] = jnp.where(degree == order, norm_start, 0.0)
    zeros = jnp.zeros((1, LANES), f32)

    def block(index, carry):
        previous, second, log_scale = carry
        first = pl.multiple_of(index * 8, 8)
        scale_ref[pl.ds(first, 8), :] = jnp.broadcast_to(log_scale, (8, LANES))
        for offset in range(8):
            row = pl.ds(first + offset, 1)
            rest = start_ref[row, :] - back_ref[row, :] * second
            current = step_ref[row, :] * previous + rest
            leg_ref[row, :] = current
            second, previous = previous, current
        too_large = jnp.abs(previous) > upper_bound
        second = jnp.where(too_large, second * lower_factor, second)
        previous = jnp.where(too_large, previous * lower_factor, previous)
        return previous, second, jnp.where(too_large, log_scale + log_step, log_scale)

    lax.fori_loop(0, degree_count // 8, block, (zeros, zeros, order_f * log_sine))
    leg_ref[pl.ds(0, degree_count), :] = leg_ref[pl.ds(0, degree_count), :] * jnp.exp(scale_ref[...])
    rest = depth - degree_count
    leg_ref[pl.ds(degree_count, rest), :] = jnp.zeros((rest, LANES), f32)
    padded_ref[pl.ds(0, degree_count), :] = gain_ref[...]
    padded_ref[pl.ds(degree_count, rest), :] = jnp.zeros((rest, chans), f32)
    column_ref[...] = leg_ref[...].T

    high, low = split(padded_ref[...])
    row = lax.broadcasted_iota(jnp.int32, (LANES, LANES), 0)
    quad = 2.0 * math.pi * math.pi / POLAR * jnp.sin(
        math.pi * ((row // own).astype(f32) + first_row) / POLAR
    )
    weight = quad * jnp.where(row % own + first_ref[0] == 0, 1.0, 2.0)
    weight = jnp.concatenate([weight] * (chans // LANES), axis=1)
    group = lat_total // out_sems.shape[0]
    copies = []
    for piece in range(out_sems.shape[0]):
        both = jnp.concatenate(
            [
                column_ref[...]
                * jnp.concatenate([column_ref[pl.ds(j * own, own), :]] * lat_total, axis=0)
                for j in range(piece * group, (piece + 1) * group)
            ],
            axis=0,
        )
        total = three(*split(both), high, low)
        for j in range(group):
            o_ref[piece * group + j] = (total[j * LANES : (j + 1) * LANES] * weight).reshape(
                lat_total, own, chans
            )
        block_of = pl.ds(piece * group, group)
        copies.append(
            pltpu.make_async_copy(o_ref.at[block_of], o_hbm.at[block_of], out_sems.at[piece])
        )
        copies[-1].start()
    for copy in copies:
        copy.wait()


def coupling(first_order, degree_gain, lat_total):
    degrees, chans = degree_gain.shape
    own = LANES // lat_total
    depth = (degrees + LANES - 1) // LANES * LANES
    table = (lat_total, lat_total, own, chans)
    rows = VMEM((degrees, LANES), f32)
    return call(
        functools.partial(coupling_kernel, lat_total),
        kept(*table),
        [smem] + loaded(1),
        [rows, rows, rows, VMEM((depth, LANES), f32), rows]
        + [VMEM((depth, chans), f32), VMEM((LANES, depth), f32), VMEM(table, f32)]
        + [pltpu.SemaphoreType.DMA((4,))],
        us=6.0,
        out_spaces=pltpu.HBM,
    )(first_order, degree_gain)


def gather_modes(r_ref, write, parts):
    for band in range(r_ref.shape[0] // parts):
        for half in range(2):
            both = r_ref[band * parts + half]
            for other in range(half + 2, parts, 2):
                both = both + r_ref[band * parts + other]
            for row in range(2):
                lanes = slice(row * LANES, (row + 1) * LANES)
                write(2 * band + row, pl.ds(half * LANES, LANES), both[:, lanes])


def scatter_modes(read, s_ref, parts, rows):
    for band in range(s_ref.shape[0] // parts):
        for part in range(parts):
            for row in range(2):
                lanes = pl.ds(row * LANES, LANES)
                value = read(2 * band + row, pl.ds(part % 2 * LANES, LANES))
                s_ref[band * parts + part, pl.ds(0, rows), lanes] = value


def forward_modes_kernel(parts, r_ref, coupling_hbm, w_hbm, x_ref, s_ref, y_ref, z_ref,
                         coupling_ref, w_ref, sems):
    wait_w = fetches((w_hbm,), (w_ref,), sems.at[pl.ds(0, 1)], 2)
    wait = fetches((coupling_hbm,), (coupling_ref,), sems.at[pl.ds(1, 1)], 8)

    def write(j, lanes, value):
        x_ref[j, :, lanes] = value

    gather_modes(r_ref, write, parts)
    lats, rows, chans = x_ref.shape
    own = rows // 2
    for piece in range(2):
        wait_w(0, piece)
    y_ref[...] = dot_split(
        x_ref[...].reshape(lats * rows, chans), w_ref[...], ((1,), (0,))
    ).reshape(lats, rows, chans)
    for piece in range(8):
        wait(0, piece)

        @pl.loop(piece * (lats // 8), (piece + 1) * (lats // 8))
        def _(j):
            totals = [jnp.zeros((own, chans), f32)] * 2
            for other in range(lats):
                factor = coupling_ref[j, other]
                for p in range(2):
                    totals[p] = totals[p] + factor * y_ref[other, pl.ds(p * own, own), :]
            for p in range(2):
                z_ref[j, pl.ds(p * own, own), :] = totals[p]

    scatter_modes(lambda j, lanes: z_ref[j, :, lanes], s_ref, parts, rows)


def backward_modes_kernel(parts, r_ref, coupling_hbm, w_hbm, x_hbm, s_hbm, s_ref, e_ref, v_ref,
                          coupling_ref, w_ref, x_ref, sems, out_sems):
    wait = fetches((coupling_hbm,), (coupling_ref,), sems.at[pl.ds(0, 1)], 8)
    wait_rest = fetches((w_hbm, x_hbm), (w_ref, x_ref), sems.at[pl.ds(1, 2)], 2)

    def write(j, lanes, value):
        e_ref[j, :, lanes] = value

    gather_modes(r_ref, write, parts)
    lats, rows, chans = x_ref.shape
    own = rows // 2
    for piece in range(8):
        wait(0, piece)

    @pl.loop(0, lats)
    def _(j):
        totals = [jnp.zeros((own, chans), f32)] * 2
        for other in range(lats):
            factor = coupling_ref[other, j]
            for p in range(2):
                totals[p] = totals[p] + factor * e_ref[other, pl.ds(p * own, own), :]
        for p in range(2):
            v_ref[j, pl.ds(p * own, own), :] = totals[p]

    for piece in range(2):
        for index in range(2):
            wait_rest(index, piece)
    v = v_ref[...].reshape(lats * rows, chans)
    e_ref[...] = dot_split(v, w_ref[...], ((1,), (1,))).reshape(lats, rows, chans)
    scatter_modes(lambda j, lanes: e_ref[j, :, lanes], s_ref, parts, rows)
    sent = pltpu.make_async_copy(
        s_ref.at[:, pl.ds(0, rows), :], s_hbm.at[:, pl.ds(0, rows), :], out_sems.at[0]
    )
    sent.start()
    weight_part = dot_split(x_ref[...].reshape(lats * rows, chans), v, ((0,), (0,)))
    share = chans // s_ref.shape[0]
    s_ref[:, pl.ds(rows, share), :] = weight_part.reshape(s_ref.shape[0], share, chans)
    shares = pltpu.make_async_copy(
        s_ref.at[:, pl.ds(rows, share), :], s_hbm.at[:, pl.ds(rows, share), :], out_sems.at[1]
    )
    shares.start()
    sent.wait()
    shares.wait()


def legendre_orders(colatitude, orders, log_norm, degree_count):
    cosine = jnp.cos(colatitude)[None, :]
    log_sine = jnp.log(jnp.sin(colatitude))[None, :]
    order_f = orders.astype(f32)[:, None]
    norm_start = jnp.exp(log_norm)[:, None] + jnp.zeros_like(cosine)
    zeros_state = jnp.zeros((orders.shape[0], colatitude.shape[0]), f32)

    def advance(carry, degree):
        previous, second, log_scale = carry
        degree_f = degree.astype(f32)
        step_factor = jnp.where(
            degree > orders[:, None],
            jnp.sqrt(
                jnp.maximum(4.0 * degree_f * degree_f - 1.0, 0.0)
                / jnp.maximum(degree_f * degree_f - order_f * order_f, 1.0)
            ),
            0.0,
        )
        lower_degree = degree_f - 1.0
        back_factor = jnp.sqrt(
            jnp.maximum(lower_degree * lower_degree - order_f * order_f, 0.0)
            / (4.0 * lower_degree * lower_degree - 1.0)
        )
        current = jnp.where(
            degree == orders[:, None],
            norm_start,
            step_factor * (cosine * previous - back_factor * second),
        )
        too_large = jnp.abs(current) > upper_bound
        current = jnp.where(too_large, current * lower_factor, current)
        previous = jnp.where(too_large, previous * lower_factor, previous)
        log_scale = jnp.where(too_large, log_scale + log_step, log_scale)
        return ((current, previous, log_scale), current * jnp.exp(log_scale))

    start_state = (zeros_state, zeros_state, order_f * log_sine)
    _, tables = lax.scan(advance, start_state, jnp.arange(degree_count, dtype=jnp.int32), unroll=8)
    return tables


def plain_gather(received, parts, own):
    bands = received.shape[0] // parts
    blocks = received.reshape(bands, parts // 2, 2, 2, own, 2, LANES).sum(axis=1)
    return blocks.transpose(0, 4, 2, 3, 1, 5).reshape(2 * bands, 2, own, 2 * LANES)


def plain_scatter(modes, parts):
    lats, _, own, _ = modes.shape
    bands = lats // 2
    blocks = modes.reshape(bands, 2, 2, own, 2, LANES).transpose(0, 4, 2, 3, 1, 5)
    blocks = jnp.broadcast_to(blocks[:, None], (bands, parts // 2) + blocks.shape[1:])
    return blocks.reshape(bands * parts, 2 * own, 2 * LANES)


def mode_factors(first_order, own, lat_total, degree_gain):
    if own % 8 == 0 and own * lat_total == LANES and degree_gain.shape[0] % 8 == 0:
        return coupling(first_order[None], degree_gain, lat_total)
    orders = first_order + 2 * jnp.arange(own, dtype=jnp.int32)
    log_norm = jnp.take(log_norms(M), orders)
    return legendre_orders(grid_tables(lat_total)[0], orders, log_norm, degree_gain.shape[0])


def mode_stages(first_order, own, parts, factors, degree_gain, spec_weight):
    if factors.ndim == 4:
        chans = spec_weight.shape[0]
        shape = (factors.shape[0], 2 * own, chans)

        def forward(received):
            return call(
                functools.partial(forward_modes_kernel, parts),
                (kept(*shape), struct(*received.shape)),
                vmem(1) + hbm(2),
                [VMEM(shape, f32), VMEM(shape, f32), VMEM(factors.shape, f32)]
                + [VMEM(spec_weight.shape, f32), pltpu.SemaphoreType.DMA((2, 8))],
                us=2.0,
            )(received, factors, spec_weight)

        def backward(received, spectrum):
            sent = (received.shape[0], 2 * own + chans // received.shape[0], chans)
            return call(
                functools.partial(backward_modes_kernel, parts),
                kept(*sent),
                vmem(1) + hbm(3),
                [VMEM(sent, f32), VMEM(shape, f32), VMEM(shape, f32), VMEM(factors.shape, f32)]
                + [VMEM(spec_weight.shape, f32), VMEM(shape, f32)]
                + [pltpu.SemaphoreType.DMA((3, 8)), pltpu.SemaphoreType.DMA((2,))],
                us=2.0,
                out_spaces=pltpu.HBM,
            )(received, factors, spec_weight, spectrum)

        return forward, backward

    legendre, lat_total = factors, factors.shape[2]
    quad_weight = grid_tables(lat_total)[1]
    orders = first_order + 2 * jnp.arange(own, dtype=jnp.int32)
    order_weight = jnp.where(orders == 0, 1.0, 2.0).astype(f32)[None, None, :, None]
    quad_column = quad_weight[:, None, None, None]
    dot = functools.partial(jnp.einsum, precision=highest)

    def forward(received):
        spectrum = plain_gather(received, parts, own)
        mixed = dot("jpmc,cd->jpmd", spectrum, spec_weight) * quad_column
        degree = dot("lmj,jpmd->lpmd", legendre, mixed) * degree_gain[:, None, None, :]
        synthesis = dot("lmj,lpmd->jpmd", legendre, degree) * order_weight
        return spectrum, plain_scatter(synthesis, parts)

    def backward(received, spectrum):
        error = plain_gather(received, parts, own) * order_weight
        gained = dot("lmj,jpmd->lpmd", legendre, error) * degree_gain[:, None, None, :]
        back = dot("lmj,lpmd->jpmd", legendre, gained) * quad_column
        sent = plain_scatter(dot("jpmd,cd->jpmc", back, spec_weight), parts)
        weight_part = dot("jpmc,jpmd->cd", spectrum, back)
        shares = weight_part.reshape(sent.shape[0], -1, weight_part.shape[1])
        return jnp.concatenate([sent, shares], axis=1)

    return forward, backward


def filter_coefficients(filters, disco_weight, band_start, band_reach):
    coefficient = jnp.einsum("ikrt,kc->irtc", filters, disco_weight, precision=highest)
    window = jnp.arange(WIN, dtype=jnp.int32)
    coefficient = jnp.where(
        (window[None, :] < band_reach[:, None])[:, :, None, None], coefficient, 0.0
    )
    offset = jnp.arange(-HMAX, HMAX + 1, dtype=jnp.int32)
    lands = offset[None, :, None] == band_start[:, None, None] + window[None, None, :]
    by_offset = jnp.sum(
        jnp.where(lands[:, :, :, None, None], coefficient[:, None], 0.0), axis=2
    )
    coef = by_offset.reshape(filters.shape[0], SPAN * KLON, LANES)
    return jnp.pad(coef, ((0, 0), (0, TAPS - SPAN * KLON), (0, 0)))


def swap_parts(x, axis):
    return lax.all_to_all(x, axis, split_axis=0, concat_axis=0, tiled=True)


def after(first, *later):
    return lax.optimization_barrier((first, *later))


def body(
    grid_field, filters, disco_weight, band_start, band_reach, spec_weight, degree_gain, cotangent
):
    band_rows, lon_local, chans = grid_field.shape
    bands, parts = lax.axis_size("lat"), lax.axis_size("chan")
    devices = bands * parts
    lat_total, lon_total = band_rows * bands, lon_local * parts
    own, share = M // devices, chans // devices
    assert band_rows == HMAX and chans == 2 * LANES and parts == 4
    band, part = lax.axis_index("lat"), lax.axis_index("chan")
    me, half, part_index = band * parts + part, part % 2, part[None]
    both_axes = ("lat", "chan")
    high, low = wave_tables(lon_total, own)
    depth = (lon_local + LANES - 1) // LANES * LANES
    apart_t = [
        jnp.asarray(np.ascontiguousarray(half_tables(table, depth).transpose(0, 2, 1)))
        for table in (high, low)
    ]
    high_t, low_t = (jnp.asarray(np.ascontiguousarray(t.T)) for t in (high, low))
    high, low = jnp.asarray(high), jnp.asarray(low)
    up = [(i, i + 1) for i in range(bands - 1)]
    down = [(i + 1, i) for i in range(bands - 1)]

    def halo(x):
        return lax.ppermute(x, "lat", up), x, lax.ppermute(x, "lat", down)

    def part_swap(x, distance):
        return lax.ppermute(x, "chan", [(i, i ^ distance) for i in range(parts)])

    def half_of(x, which):
        return lax.dynamic_slice_in_dim(x, which * LANES, LANES, axis=2)

    def edges(x):
        return part_swap(jnp.concatenate([x[:, :8], x[:, -8:]], axis=1), 2)

    def exchange(modes):
        return swap_parts(modes.reshape(devices, -1, modes.shape[-1]), both_axes)

    outgoing, cotangent, degree_gain, disco_weight, band_start = after(
        half_of(grid_field, 1 - half), cotangent, degree_gain, disco_weight, band_start
    )
    field_other = part_swap(outgoing, 1)
    first_order = owned_orders(me, devices)
    factors = mode_factors(first_order, own, lat_total, degree_gain)
    cot_out = half_of(cotangent, 1 - half)
    field_other, factors, cot_out = after(field_other, factors, cot_out)
    modes, field = analyze(part_index, lon_total, grid_field, field_other, high, low)

    cot_others = [part_swap(cot_out[:1], 1)]
    modes, field_sent, cot_others[0], cot_out, disco_weight, band_start = after(
        modes, field, cot_others[0], cot_out, disco_weight, band_start
    )
    mine = lax.dynamic_slice_in_dim(disco_weight, half * LANES, LANES, axis=1)
    coef = filter_coefficients(filters, mine, band_start, band_reach)
    rows = halo(field_sent)
    cot_others.append(part_swap(cot_out[1:], 1))
    forward, backward = mode_stages(first_order, own, parts, factors, degree_gain, spec_weight)
    spectrum, synthesis = forward(exchange(modes))
    synthesis, edge, cot_others[1] = after(synthesis, edges(field_sent), cot_others[1])

    local, adjoint = local_filter(*rows, *halo(jnp.concatenate([edge, coef], axis=1)))
    error_modes, out_own, *out_sends, error = grid_stage(
        part_index, exchange(synthesis), field, local, cotangent, cot_others,
        (high, low, high_t, low_t),
    )

    out_others = [part_swap(x, 1) for x in out_sends]
    rows = [lax.ppermute(error[row : row + 1], "lat", up) for row in range(band_rows)]
    rows += [error, lax.ppermute(error, "lat", down)]
    sent = backward(exchange(error_modes), spectrum)
    sent, edge, out_others[0], rows[0], rows[3] = after(
        sent, edges(error), out_others[0], rows[0], rows[3]
    )
    base = adjoint_filter(part_index, *rows, *halo(edge), adjoint, cotangent, cot_others)
    received = exchange(sent)
    if own % 8 == 0 and share % 8 == 0:
        shares = spread_shares(received, 2 * own)
    else:
        shares = jnp.sum(received[:, 2 * own :], axis=0, keepdims=True)
        shares = jnp.broadcast_to(shares, (devices,) + shares.shape[1:])
        received = received[:, : 2 * own]
    grad_weight = swap_parts(shares, both_axes).reshape(chans, chans)
    grad_send, grad_own = (
        final_stage(part_index, lon_total, 2 * own, received, base, *apart_t, theirs)
        for theirs in (True, False)
    )
    grad_send, *out_others = after(grad_send, *out_others)
    output = join(part_index, out_own, *out_others)
    grad_input, grad_weight = close(part_index, grad_own, part_swap(grad_send, 1), grad_weight)
    return (output, grad_input, grad_weight)


def solution(mesh):
    in_specs = (
        P("lat", "chan", None),
        P("lat", None, None, None),
        P(),
        P("lat"),
        P("lat"),
        P(),
        P(),
        P("lat", "chan", None),
    )
    out_specs = (P("lat", "chan", None), P("lat", "chan", None), P())
    return jax.shard_map(body, mesh=mesh, in_specs=in_specs, out_specs=out_specs, check_vma=False)
```

```python
import functools
import math

import jax
import jax.numpy as jnp
import ml_dtypes
import numpy as np
from jax import lax
from jax.experimental import pallas as pl
from jax.experimental.pallas import tpu as pltpu
from jax.sharding import PartitionSpec as P

L = 360
M = 256
WIN = 3
HMAX = 2
KLON = 5
POLAR = 720
SPAN = 2 * HMAX + 1
TAPS = 32
EDGES = 16
LANES = 128
MIB = 2**20


highest = lax.Precision.HIGHEST
upper_bound = 2.0**32
lower_factor = 2.0 ** (-32)
log_step = 32.0 * math.log(2.0)

f32 = jnp.float32
bf16 = jnp.bfloat16
VMEM = pltpu.VMEM


@functools.lru_cache(maxsize=None)
def wave_tables(lon_total, own_count):
    orders = np.concatenate([np.arange(0, M, 2), np.arange(1, M, 2)]).reshape(-1, own_count)
    lons = np.arange(lon_total // 2)
    angle = (orders[:, :, None] * lons) % lon_total * (2.0 * np.pi / lon_total)
    table = np.stack([np.cos(angle), -np.sin(angle)], axis=1).reshape(2 * M, lon_total // 2)
    high = table.astype(ml_dtypes.bfloat16)
    low = (table - high.astype(np.float64)).astype(ml_dtypes.bfloat16)
    return high, low


def half_tables(table, depth):
    rows, lons = table.shape
    blocks = table.reshape(rows, 2, lons // 2).transpose(1, 0, 2)
    return np.pad(blocks, ((0, 0), (0, 0), (0, depth - lons // 2)))


def owned_orders(owner, devices):
    half = devices // 2
    return owner % half * (2 * (M // devices)) + owner // half


def grid_tables(lat_total):
    first_row = (POLAR - lat_total) // 2
    colatitude = math.pi * (jnp.arange(lat_total, dtype=f32) + float(first_row)) / POLAR
    quad_weight = 2.0 * math.pi * math.pi / POLAR * jnp.sin(colatitude)
    return (colatitude, quad_weight)


def log_norms(order_count):
    order_index = jnp.arange(order_count, dtype=f32)
    log_terms = jnp.where(
        order_index > 0.0,
        jnp.log((2.0 * order_index + 1.0) / jnp.maximum(2.0 * order_index, 1.0)),
        0.0,
    )
    return -0.5 * math.log(4.0 * math.pi) + 0.5 * jnp.cumsum(log_terms)


def split(x):
    high = x.astype(bf16)
    return high, (x - high.astype(f32)).astype(bf16)


def dot_split(a, b, dims):
    (ah, al), (bh, bl) = split(a), split(b)
    dot = lambda u, v: lax.dot_general(u, v, (dims, ((), ())), preferred_element_type=f32)
    return dot(ah, bh) + (dot(ah, bl) + dot(al, bh))


def cost(us):
    return pl.CostEstimate(flops=int(us * 1e9), bytes_accessed=int(us * 3e6), transcendentals=0)


def call(kernel, out_shape, in_specs, scratch=(), us=1.0, limit=16, out_spaces=None, aliases=None):
    run = pl.pallas_call(
        kernel,
        out_shape=out_shape,
        in_specs=[pl.BlockSpec(memory_space=space) for space, _ in in_specs],
        out_specs=jax.tree.map(
            lambda space: pl.BlockSpec(memory_space=space),
            out_spaces or jax.tree.map(lambda _: VMEM, out_shape),
        ),
        scratch_shapes=list(scratch),
        input_output_aliases=aliases or {},
        compiler_params=pltpu.CompilerParams(vmem_limit_bytes=limit * MIB),
        cost_estimate=cost(us),
    )
    keeps = [keep for _, keep in in_specs]
    return lambda *args: run(
        *[held(x) if keep else x for x, keep in zip(args, keeps, strict=True)]
    )


def held(x):
    return pltpu.with_memory_space_constraint(x, pltpu.HBM)


def vmem(count):
    return [(VMEM, False)] * count


def loaded(count):
    return [(VMEM, True)] * count


def hbm(count):
    return [(pltpu.HBM, True)] * count


smem = (pltpu.SMEM, False)


def struct(*shape, dtype=f32):
    return jax.ShapeDtypeStruct(shape, dtype)


def kept(*shape, dtype=f32):
    return pltpu.HBM(shape, dtype)


def own_half(part):
    return part % 2


def lane_half(x_ref, half):
    return x_ref.at[:, :, pl.ds(pl.multiple_of(half * LANES, LANES), LANES)]


def lon_half(x_ref, half):
    width = x_ref.shape[1] // 2
    return x_ref.at[:, pl.ds(pl.multiple_of(half * width, 8), width), :]


def pair_copies(half, own_hbm, other_hbms, target, sems):
    copies = [pltpu.make_async_copy(lane_half(own_hbm, half), lon_half(target, half), sems.at[0])]
    there = lon_half(target, 1 - half)
    for row, other_hbm in enumerate(other_hbms):
        copies.append(
            pltpu.make_async_copy(other_hbm, there.at[pl.ds(row, 1)], sems.at[1 + row])
        )
    for copy in copies:
        copy.start()
    return copies


def join_kernel(part_ref, own_ref, *refs):
    o_ref = refs[-1]
    half = own_half(part_ref[0])
    mine, theirs = (
        pl.ds(pl.multiple_of(place * LANES, LANES), LANES) for place in (half, 1 - half)
    )
    o_ref[:, :, mine] = own_ref[...]
    for row, other_ref in enumerate(refs[:-1]):
        o_ref[pl.ds(row, other_ref.shape[0]), :, theirs] = other_ref[...]


def join(part, own, *others):
    rows, lons, _ = own.shape
    return call(
        join_kernel, kept(rows, lons, 2 * LANES), [smem] + vmem(1 + len(others))
    )(part, own, *others)


def side_by_side(x):
    return jnp.concatenate([x[0], x[1]], axis=1)


def three(table_high, table_low, high, low):
    dot = lambda u, v: jnp.dot(u, v, preferred_element_type=f32)
    return dot(table_high, high) + (dot(table_high, low) + dot(table_low, high))


def fetches(sources, targets, sems, pieces):
    copies = []
    for index, (source, target) in enumerate(zip(sources, targets, strict=True)):
        tile = source.shape[0] // pieces
        copies.append(
            [
                pltpu.make_async_copy(
                    source.at[pl.ds(piece * tile, tile)],
                    target.at[pl.ds(piece * tile, tile)],
                    sems.at[index, piece],
                )
                for piece in range(pieces)
            ]
        )
    for piece in range(pieces):
        for group in copies:
            group[piece].start()
    return lambda index, piece: copies[index][piece].wait()


def analyze_rows(x, sign, high_ref, low_ref, wait, store):
    high, low = split(x)
    wait(0, 0)
    wait(1, 0)
    value = three(high_ref[...], low_ref[...], high, low)
    count = value.shape[0] // 2
    store(pl.ds(0, count), value[:count])
    store(pl.ds(count, count), value[count:] * sign)


def compose_rows(modes, sign, thigh_ref, tlow_ref, wait, store, pieces):
    count = modes.shape[0] // 2
    high, low = split(jnp.concatenate([modes[:count], modes[count:] * sign], axis=0))
    tile = thigh_ref.shape[0] // pieces
    for piece in range(pieces):
        rows = pl.ds(piece * tile, tile)
        wait(0, piece)
        wait(1, piece)
        store(rows, three(thigh_ref[rows, :], tlow_ref[rows, :], high, low))


def turn_sign(part):
    return (1 - 2 * (part // 2)).astype(f32)


def analyze_kernel(scale, part_ref, own_hbm, other_ref, high_hbm, low_hbm, o_ref, field_hbm,
                   x_ref, high_ref, low_ref, pair_sem, sems, out_sem):
    part = part_ref[0]
    half = own_half(part)
    mine = pltpu.make_async_copy(lane_half(own_hbm, half), lon_half(x_ref, half), pair_sem)
    mine.start()
    wait = fetches((high_hbm, low_hbm), (high_ref, low_ref), sems, 1)
    lon_half(x_ref, 1 - half)[...] = other_ref[...]
    mine.wait()
    out = pltpu.make_async_copy(x_ref, field_hbm, out_sem)
    out.start()

    def store(rows, value):
        o_ref[rows, :] = value * scale

    analyze_rows(side_by_side(x_ref[...]), turn_sign(part), high_ref, low_ref, wait, store)
    out.wait()


def analyze(part, lon_total, own, other, high, low):
    rows, lons, _ = own.shape
    field = (rows, 2 * lons, LANES)
    return call(
        functools.partial(analyze_kernel, 1.0 / lon_total),
        (struct(2 * M, rows * LANES), kept(*field)),
        [smem] + hbm(1) + vmem(1) + hbm(2),
        [VMEM(field, f32), VMEM(high.shape, bf16), VMEM(high.shape, bf16)]
        + [pltpu.SemaphoreType.DMA, pltpu.SemaphoreType.DMA((2, 1)), pltpu.SemaphoreType.DMA],
        us=3.0,
        out_spaces=(VMEM, pltpu.HBM),
    )(part, own, other, high, low)


def grid_kernel(part_ref, s_ref, field_hbm, local_hbm, cot_hbm, first_hbm, second_hbm,
                high_hbm, low_hbm, thigh_hbm, tlow_hbm,
                mode_ref, own_hbm, send_first_hbm, send_second_hbm, err_hbm,
                x_ref, local_ref, cot_ref, spec_ref, out_ref, err_ref,
                high_ref, low_ref, thigh_ref, tlow_ref,
                back_sems, sems, cot_sems, other_sems, out_sems):
    part = part_ref[0]
    half, sign = own_half(part), turn_sign(part)
    wait_back = fetches((thigh_hbm, tlow_hbm), (thigh_ref, tlow_ref), back_sems, 3)
    others = [
        pltpu.make_async_copy(source, target, other_sems.at[index])
        for index, (source, target) in enumerate(((local_hbm, local_ref), (field_hbm, x_ref)))
    ]
    for copy in others:
        copy.start()
    others += pair_copies(half, cot_hbm, (first_hbm, second_hbm), cot_ref, cot_sems)
    wait = fetches((high_hbm, low_hbm), (high_ref, low_ref), sems, 1)

    def store_spec(rows, value):
        spec_ref[rows, :] = value

    modes = s_ref[...].reshape(thigh_ref.shape[1], s_ref.shape[2])
    compose_rows(modes, sign, thigh_ref, tlow_ref, wait_back, store_spec, 3)
    for copy in others:
        copy.wait()
    tile = x_ref.shape[1] // 6
    for row in range(x_ref.shape[0]):
        for piece in range(6):
            lons = pl.ds(piece * tile, tile)
            hidden = local_ref[row, lons, :] + spec_ref[lons, pl.ds(row * LANES, LANES)]
            gate = 1.0 / (1.0 + jnp.exp(-hidden))
            out_ref[row, lons, :] = x_ref[row, lons, :] + hidden * gate
            err_ref[row, lons, :] = cot_ref[row, lons, :] * (gate * (1.0 + hidden * (1.0 - gate)))
    there = lon_half(out_ref, 1 - half)
    outs = [
        pltpu.make_async_copy(source, target, out_sems.at[index])
        for index, (source, target) in enumerate(
            (
                (err_ref, err_hbm),
                (lon_half(out_ref, half), own_hbm),
                (there.at[pl.ds(0, 1)], send_first_hbm),
                (there.at[pl.ds(1, 1)], send_second_hbm),
            )
        )
    ]
    for copy in outs:
        copy.start()

    def store(rows, value):
        mode_ref[rows, :] = value

    analyze_rows(side_by_side(err_ref[...]), sign, high_ref, low_ref, wait, store)
    for copy in outs:
        copy.wait()


def grid_stage(part, synthesis, field, local, cotangent, others, tables):
    rows, lons, _ = field.shape
    block = (rows, lons // 2, LANES)
    grid = VMEM(field.shape, f32)
    return call(
        grid_kernel,
        (
            struct(2 * M, rows * LANES),
            kept(*block),
            kept(1, *block[1:]),
            kept(1, *block[1:]),
            kept(*field.shape),
        ),
        [smem] + vmem(1) + hbm(9),
        [grid, grid, grid, VMEM((lons, rows * LANES), f32), grid, grid]
        + [VMEM(table.shape, bf16) for table in tables]
        + [pltpu.SemaphoreType.DMA((2, 3)), pltpu.SemaphoreType.DMA((2, 1))]
        + [pltpu.SemaphoreType.DMA((count,)) for count in (3, 2, 4)],
        us=4.0,
        limit=32,
        out_spaces=(VMEM,) + (pltpu.HBM,) * 4,
    )(part, synthesis, field, local, cotangent, *others, *tables)


def final_kernel(scale, rows_own, theirs, part_ref, s_ref, base_hbm, thigh_hbm, tlow_hbm,
                 *refs):
    o_ref, base_ref, thigh_ref, tlow_ref, sems, base_sem = refs[-6:]
    out_hbm = refs[0]
    part = part_ref[0]
    half = 1 - own_half(part) if theirs else own_half(part)
    wait = fetches((thigh_hbm.at[half], tlow_hbm.at[half]), (thigh_ref, tlow_ref), sems, 1)
    base_copy = pltpu.make_async_copy(lon_half(base_hbm, half), base_ref, base_sem)
    base_copy.start()
    modes = s_ref[:, pl.ds(0, rows_own), :].reshape(thigh_ref.shape[1], s_ref.shape[2])
    total = o_ref.shape[1]

    def store(lons, value):
        count = min(lons.size, total - lons.start)
        for row in range(base_ref.shape[0]):
            lanes = slice(row * LANES, (row + 1) * LANES)
            o_ref[row, pl.ds(lons.start, count), :] = scale * value[:count, lanes]

    compose_rows(modes, turn_sign(part), thigh_ref, tlow_ref, wait, store, 1)
    base_copy.wait()
    o_ref[...] = o_ref[...] + base_ref[...]
    if not theirs:
        out = pltpu.make_async_copy(o_ref, lane_half(out_hbm, half), base_sem)
        out.start()
        out.wait()


def final_stage(part, lon_total, rows_own, modes, base, high_t, low_t, theirs):
    rows, lons, _ = base.shape
    block = (rows, lons // 2, LANES)
    table = high_t.shape[1:]
    return call(
        functools.partial(final_kernel, 1.0 / lon_total, rows_own, theirs),
        struct(*block) if theirs else kept(rows, lons // 2, 2 * LANES),
        [smem] + vmem(1) + hbm(3),
        [VMEM(block, f32)] * (1 if theirs else 2)
        + [VMEM(table, bf16), VMEM(table, bf16)]
        + [pltpu.SemaphoreType.DMA((2, 1)), pltpu.SemaphoreType.DMA],
        us=2.0,
        out_spaces=VMEM if theirs else pltpu.HBM,
    )(part, modes, base, high_t, low_t)


def close_kernel(part_ref, held_hbm, other_ref, o_hbm, sem):
    del held_hbm
    copy = pltpu.make_async_copy(other_ref, lane_half(o_hbm, 1 - own_half(part_ref[0])), sem)
    copy.start()
    copy.wait()


def close(part, held_half, other):
    return call(
        close_kernel,
        kept(*held_half.shape),
        [smem] + hbm(1) + vmem(1),
        [pltpu.SemaphoreType.DMA],
        us=8.0,
        out_spaces=pltpu.HBM,
        aliases={1: 0},
    )(part, held_half, other)


def shares_kernel(first, r_ref, o_ref):
    share = jnp.sum(r_ref[:, pl.ds(first, o_ref.shape[1]), :], axis=0)
    o_ref[...] = jnp.broadcast_to(share[None], o_ref.shape)


def spread_shares(received, first):
    devices, rows, chans = received.shape
    return call(
        functools.partial(shares_kernel, first), struct(devices, rows - first, chans), vmem(1)
    )(received)


def filter_sums(refs, edge_refs, coef_ref, finish, sums_ref):
    lons = refs[0].shape[1]
    tile = lons // 18
    sources = [(x_ref, row) for x_ref in refs for row in range(x_ref.shape[0])]
    for row in range(2):
        def add(values, rows, row=row):
            for tap in range(KLON):
                total = values[0] * coef_ref[row, pl.ds(tap, 1), :]
                for offset in range(1, SPAN):
                    total = total + values[offset] * coef_ref[row, pl.ds(offset * KLON + tap, 1), :]
                sums_ref[tap, rows, :] = total

        near = sources[row : row + SPAN]
        edges = [(edge_ref, k) for edge_ref in edge_refs for k in range(2)][row : row + SPAN]
        add([edge_ref[k, pl.ds(8, 8), :] for edge_ref, k in edges], pl.ds(0, 8))
        add([edge_ref[k, pl.ds(0, 8), :] for edge_ref, k in edges], pl.ds(lons + 8, 8))

        @pl.loop(0, 18)
        def _(piece, near=near, add=add):
            start = pl.multiple_of(piece * tile, 8)
            values = [x_ref[k, pl.ds(start, tile), :] for x_ref, k in near]
            add(values, pl.ds(pl.multiple_of(start + 8, 8), tile))

        for piece in range(18):
            total = None
            for tap in range(KLON):
                value = sums_ref[tap, pl.ds(piece * tile + 8 + tap - KLON // 2, tile), :]
                total = value if total is None else total + value
            finish(row, pl.ds(piece * tile, tile), total)


def filter_kernel(prev_ref, own_ref, next_ref, lower_ref, middle_ref, upper_ref, o_ref, adjoint_ref,
                  sums_ref):
    def finish(row, lons, value):
        o_ref[row, lons, :] = value

    taps = pl.ds(EDGES, TAPS)
    coef_refs = [ref.at[:, taps] for ref in (lower_ref, middle_ref, upper_ref)]
    filter_sums(
        (prev_ref, own_ref, next_ref), (lower_ref, middle_ref, upper_ref), coef_refs[1], finish, sums_ref
    )
    adjoint_ref[...] = jnp.zeros_like(adjoint_ref)
    sources = [(c_ref, row) for c_ref in coef_refs for row in range(2)]
    for row in range(2):
        for offset in range(SPAN):
            c_ref, k = sources[row + offset]
            for tap in range(KLON):
                mirrored = (SPAN - 1 - offset) * KLON + KLON - 1 - tap
                adjoint_ref[row, pl.ds(offset * KLON + tap, 1), :] = c_ref[k, pl.ds(mirrored, 1), :]


def adjoint_kernel(part_ref, first_ref, second_ref, own_ref, next_ref, lower_ref, middle_ref, upper_ref, coef_ref,
                   cot_hbm, first_hbm, second_hbm,
                   o_ref, sums_ref, cot_ref, cot_sems):
    copies = pair_copies(
        own_half(part_ref[0]), cot_hbm, (first_hbm, second_hbm), cot_ref, cot_sems
    )
    for copy in copies:
        copy.wait()

    def finish(row, lons, value):
        o_ref[row, lons, :] = cot_ref[row, lons, :] + value

    edge_refs = (lower_ref, middle_ref, upper_ref)
    filter_sums((first_ref, second_ref, own_ref, next_ref), edge_refs, coef_ref, finish, sums_ref)


def local_filter(prev, own, behind, *edges):
    return call(
        filter_kernel,
        (kept(*own.shape), kept(own.shape[0], TAPS, LANES)),
        loaded(3) + vmem(3),
        [VMEM((KLON, own.shape[1] + 16, LANES), f32)],
        us=4.0,
    )(prev, own, behind, *edges)


def adjoint_filter(part, first, second, own, behind, lower, middle, upper, coef, cotangent, others):
    return call(
        adjoint_kernel,
        kept(*own.shape),
        [smem] + loaded(4) + vmem(4) + hbm(3),
        [VMEM((KLON, own.shape[1] + 16, LANES), f32), VMEM(own.shape, f32)]
        + [pltpu.SemaphoreType.DMA((3,))],
        us=4.0,
    )(part, first, second, own, behind, lower, middle, upper, coef, cotangent, *others)


def coupling_kernel(lat_total, first_ref, gain_ref, o_hbm, step_ref, back_ref, start_ref, leg_ref,
                    scale_ref, padded_ref, column_ref, o_ref, out_sems):
    degree_count, chans = gain_ref.shape
    depth = padded_ref.shape[0]
    own = LANES // lat_total
    first_row = float((POLAR - lat_total) // 2)
    lane = lax.broadcasted_iota(jnp.int32, (1, LANES), 1)
    order = 2 * (lane % own) + first_ref[0]
    colatitude = math.pi * ((lane // own).astype(f32) + first_row) / POLAR
    cosine, log_sine = jnp.cos(colatitude), jnp.log(jnp.sin(colatitude))
    k = lax.broadcasted_iota(jnp.int32, (M, LANES), 0)
    k_f = k.astype(f32)
    log_terms = jnp.log((2.0 * k_f + 1.0) / jnp.maximum(2.0 * k_f, 1.0))
    log_norm = -0.5 * math.log(4.0 * math.pi) + 0.5 * jnp.sum(
        jnp.where((k > 0) & (k <= order), log_terms, 0.0), axis=0, keepdims=True
    )
    norm_start = jnp.exp(log_norm)
    degree = lax.broadcasted_iota(jnp.int32, (degree_count, LANES), 0)
    degree_f, order_f = degree.astype(f32), order.astype(f32)
    step = jnp.where(
        degree > order,
        jnp.sqrt(
            jnp.maximum(4.0 * degree_f * degree_f - 1.0, 0.0)
            / jnp.maximum(degree_f * degree_f - order_f * order_f, 1.0)
        ),
        0.0,
    )
    lower = degree_f - 1.0
    back = jnp.sqrt(
        jnp.maximum(lower * lower - order_f * order_f, 0.0) / (4.0 * lower * lower - 1.0)
    )
    step_ref[...] = step * cosine
    back_ref[...] = step * back
    start_ref[...] = jnp.where(degree == order, norm_start, 0.0)
    zeros = jnp.zeros((1, LANES), f32)

    def block(index, carry):
        previous, second, log_scale = carry
        first = pl.multiple_of(index * 8, 8)
        scale_ref[pl.ds(first, 8), :] = jnp.broadcast_to(log_scale, (8, LANES))
        for offset in range(8):
            row = pl.ds(first + offset, 1)
            rest = start_ref[row, :] - back_ref[row, :] * second
            current = step_ref[row, :] * previous + rest
            leg_ref[row, :] = current
            second, previous = previous, current
        too_large = jnp.abs(previous) > upper_bound
        second = jnp.where(too_large, second * lower_factor, second)
        previous = jnp.where(too_large, previous * lower_factor, previous)
        return previous, second, jnp.where(too_large, log_scale + log_step, log_scale)

    lax.fori_loop(0, degree_count // 8, block, (zeros, zeros, order_f * log_sine))
    leg_ref[pl.ds(0, degree_count), :] = leg_ref[pl.ds(0, degree_count), :] * jnp.exp(scale_ref[...])
    rest = depth - degree_count
    leg_ref[pl.ds(degree_count, rest), :] = jnp.zeros((rest, LANES), f32)
    padded_ref[pl.ds(0, degree_count), :] = gain_ref[...]
    padded_ref[pl.ds(degree_count, rest), :] = jnp.zeros((rest, chans), f32)
    column_ref[...] = leg_ref[...].T

    high, low = split(padded_ref[...])
    row = lax.broadcasted_iota(jnp.int32, (LANES, LANES), 0)
    quad = 2.0 * math.pi * math.pi / POLAR * jnp.sin(
        math.pi * ((row // own).astype(f32) + first_row) / POLAR
    )
    weight = quad * jnp.where(row % own + first_ref[0] == 0, 1.0, 2.0)
    weight = jnp.concatenate([weight] * (chans // LANES), axis=1)
    group = lat_total // out_sems.shape[0]
    copies = []
    for piece in range(out_sems.shape[0]):
        both = jnp.concatenate(
            [
                column_ref[...]
                * jnp.concatenate([column_ref[pl.ds(j * own, own), :]] * lat_total, axis=0)
                for j in range(piece * group, (piece + 1) * group)
            ],
            axis=0,
        )
        total = three(*split(both), high, low)
        for j in range(group):
            o_ref[piece * group + j] = (total[j * LANES : (j + 1) * LANES] * weight).reshape(
                lat_total, own, chans
            )
        block_of = pl.ds(piece * group, group)
        copies.append(
            pltpu.make_async_copy(o_ref.at[block_of], o_hbm.at[block_of], out_sems.at[piece])
        )
        copies[-1].start()
    for copy in copies:
        copy.wait()


def coupling(first_order, degree_gain, lat_total):
    degrees, chans = degree_gain.shape
    own = LANES // lat_total
    depth = (degrees + LANES - 1) // LANES * LANES
    table = (lat_total, lat_total, own, chans)
    rows = VMEM((degrees, LANES), f32)
    return call(
        functools.partial(coupling_kernel, lat_total),
        kept(*table),
        [smem] + loaded(1),
        [rows, rows, rows, VMEM((depth, LANES), f32), rows]
        + [VMEM((depth, chans), f32), VMEM((LANES, depth), f32), VMEM(table, f32)]
        + [pltpu.SemaphoreType.DMA((4,))],
        us=6.0,
        out_spaces=pltpu.HBM,
    )(first_order, degree_gain)


def gather_modes(r_ref, write, parts):
    for band in range(r_ref.shape[0] // parts):
        for half in range(2):
            both = r_ref[band * parts + half]
            for other in range(half + 2, parts, 2):
                both = both + r_ref[band * parts + other]
            for row in range(2):
                lanes = slice(row * LANES, (row + 1) * LANES)
                write(2 * band + row, pl.ds(half * LANES, LANES), both[:, lanes])


def scatter_modes(read, s_ref, parts, rows):
    for band in range(s_ref.shape[0] // parts):
        for part in range(parts):
            for row in range(2):
                lanes = pl.ds(row * LANES, LANES)
                value = read(2 * band + row, pl.ds(part % 2 * LANES, LANES))
                s_ref[band * parts + part, pl.ds(0, rows), lanes] = value


def forward_modes_kernel(parts, r_ref, coupling_hbm, w_hbm, x_ref, s_ref, y_ref, z_ref,
                         coupling_ref, w_ref, sems):
    wait_w = fetches((w_hbm,), (w_ref,), sems.at[pl.ds(0, 1)], 2)
    wait = fetches((coupling_hbm,), (coupling_ref,), sems.at[pl.ds(1, 1)], 8)

    def write(j, lanes, value):
        x_ref[j, :, lanes] = value

    gather_modes(r_ref, write, parts)
    lats, rows, chans = x_ref.shape
    own = rows // 2
    for piece in range(2):
        wait_w(0, piece)
    y_ref[...] = dot_split(
        x_ref[...].reshape(lats * rows, chans), w_ref[...], ((1,), (0,))
    ).reshape(lats, rows, chans)
    for piece in range(8):
        wait(0, piece)

        @pl.loop(piece * (lats // 8), (piece + 1) * (lats // 8))
        def _(j):
            totals = [jnp.zeros((own, chans), f32)] * 2
            for other in range(lats):
                factor = coupling_ref[j, other]
                for p in range(2):
                    totals[p] = totals[p] + factor * y_ref[other, pl.ds(p * own, own), :]
            for p in range(2):
                z_ref[j, pl.ds(p * own, own), :] = totals[p]

    scatter_modes(lambda j, lanes: z_ref[j, :, lanes], s_ref, parts, rows)


def backward_modes_kernel(parts, r_ref, coupling_hbm, w_hbm, x_hbm, s_hbm, s_ref, e_ref, v_ref,
                          coupling_ref, w_ref, x_ref, sems, out_sems):
    wait = fetches((coupling_hbm,), (coupling_ref,), sems.at[pl.ds(0, 1)], 8)
    wait_rest = fetches((w_hbm, x_hbm), (w_ref, x_ref), sems.at[pl.ds(1, 2)], 2)

    def write(j, lanes, value):
        e_ref[j, :, lanes] = value

    gather_modes(r_ref, write, parts)
    lats, rows, chans = x_ref.shape
    own = rows // 2
    for piece in range(8):
        wait(0, piece)

    @pl.loop(0, lats)
    def _(j):
        totals = [jnp.zeros((own, chans), f32)] * 2
        for other in range(lats):
            factor = coupling_ref[other, j]
            for p in range(2):
                totals[p] = totals[p] + factor * e_ref[other, pl.ds(p * own, own), :]
        for p in range(2):
            v_ref[j, pl.ds(p * own, own), :] = totals[p]

    for piece in range(2):
        for index in range(2):
            wait_rest(index, piece)
    v = v_ref[...].reshape(lats * rows, chans)
    e_ref[...] = dot_split(v, w_ref[...], ((1,), (1,))).reshape(lats, rows, chans)
    scatter_modes(lambda j, lanes: e_ref[j, :, lanes], s_ref, parts, rows)
    sent = pltpu.make_async_copy(
        s_ref.at[:, pl.ds(0, rows), :], s_hbm.at[:, pl.ds(0, rows), :], out_sems.at[0]
    )
    sent.start()
    weight_part = dot_split(x_ref[...].reshape(lats * rows, chans), v, ((0,), (0,)))
    share = chans // s_ref.shape[0]
    s_ref[:, pl.ds(rows, share), :] = weight_part.reshape(s_ref.shape[0], share, chans)
    shares = pltpu.make_async_copy(
        s_ref.at[:, pl.ds(rows, share), :], s_hbm.at[:, pl.ds(rows, share), :], out_sems.at[1]
    )
    shares.start()
    sent.wait()
    shares.wait()


def legendre_orders(colatitude, orders, log_norm, degree_count):
    cosine = jnp.cos(colatitude)[None, :]
    log_sine = jnp.log(jnp.sin(colatitude))[None, :]
    order_f = orders.astype(f32)[:, None]
    norm_start = jnp.exp(log_norm)[:, None] + jnp.zeros_like(cosine)
    zeros_state = jnp.zeros((orders.shape[0], colatitude.shape[0]), f32)

    def advance(carry, degree):
        previous, second, log_scale = carry
        degree_f = degree.astype(f32)
        step_factor = jnp.where(
            degree > orders[:, None],
            jnp.sqrt(
                jnp.maximum(4.0 * degree_f * degree_f - 1.0, 0.0)
                / jnp.maximum(degree_f * degree_f - order_f * order_f, 1.0)
            ),
            0.0,
        )
        lower_degree = degree_f - 1.0
        back_factor = jnp.sqrt(
            jnp.maximum(lower_degree * lower_degree - order_f * order_f, 0.0)
            / (4.0 * lower_degree * lower_degree - 1.0)
        )
        current = jnp.where(
            degree == orders[:, None],
            norm_start,
            step_factor * (cosine * previous - back_factor * second),
        )
        too_large = jnp.abs(current) > upper_bound
        current = jnp.where(too_large, current * lower_factor, current)
        previous = jnp.where(too_large, previous * lower_factor, previous)
        log_scale = jnp.where(too_large, log_scale + log_step, log_scale)
        return ((current, previous, log_scale), current * jnp.exp(log_scale))

    start_state = (zeros_state, zeros_state, order_f * log_sine)
    _, tables = lax.scan(advance, start_state, jnp.arange(degree_count, dtype=jnp.int32), unroll=8)
    return tables


def plain_gather(received, parts, own):
    bands = received.shape[0] // parts
    blocks = received.reshape(bands, parts // 2, 2, 2, own, 2, LANES).sum(axis=1)
    return blocks.transpose(0, 4, 2, 3, 1, 5).reshape(2 * bands, 2, own, 2 * LANES)


def plain_scatter(modes, parts):
    lats, _, own, _ = modes.shape
    bands = lats // 2
    blocks = modes.reshape(bands, 2, 2, own, 2, LANES).transpose(0, 4, 2, 3, 1, 5)
    blocks = jnp.broadcast_to(blocks[:, None], (bands, parts // 2) + blocks.shape[1:])
    return blocks.reshape(bands * parts, 2 * own, 2 * LANES)


def mode_factors(first_order, own, lat_total, degree_gain):
    if own % 8 == 0 and own * lat_total == LANES and degree_gain.shape[0] % 8 == 0:
        return coupling(first_order[None], degree_gain, lat_total)
    orders = first_order + 2 * jnp.arange(own, dtype=jnp.int32)
    log_norm = jnp.take(log_norms(M), orders)
    return legendre_orders(grid_tables(lat_total)[0], orders, log_norm, degree_gain.shape[0])


def mode_stages(first_order, own, parts, factors, degree_gain, spec_weight):
    if factors.ndim == 4:
        chans = spec_weight.shape[0]
        shape = (factors.shape[0], 2 * own, chans)

        def forward(received):
            return call(
                functools.partial(forward_modes_kernel, parts),
                (kept(*shape), struct(*received.shape)),
                vmem(1) + hbm(2),
                [VMEM(shape, f32), VMEM(shape, f32), VMEM(factors.shape, f32)]
                + [VMEM(spec_weight.shape, f32), pltpu.SemaphoreType.DMA((2, 8))],
                us=2.0,
            )(received, factors, spec_weight)

        def backward(received, spectrum):
            sent = (received.shape[0], 2 * own + chans // received.shape[0], chans)
            return call(
                functools.partial(backward_modes_kernel, parts),
                kept(*sent),
                vmem(1) + hbm(3),
                [VMEM(sent, f32), VMEM(shape, f32), VMEM(shape, f32), VMEM(factors.shape, f32)]
                + [VMEM(spec_weight.shape, f32), VMEM(shape, f32)]
                + [pltpu.SemaphoreType.DMA((3, 8)), pltpu.SemaphoreType.DMA((2,))],
                us=2.0,
                out_spaces=pltpu.HBM,
            )(received, factors, spec_weight, spectrum)

        return forward, backward

    legendre, lat_total = factors, factors.shape[2]
    quad_weight = grid_tables(lat_total)[1]
    orders = first_order + 2 * jnp.arange(own, dtype=jnp.int32)
    order_weight = jnp.where(orders == 0, 1.0, 2.0).astype(f32)[None, None, :, None]
    quad_column = quad_weight[:, None, None, None]
    dot = functools.partial(jnp.einsum, precision=highest)

    def forward(received):
        spectrum = plain_gather(received, parts, own)
        mixed = dot("jpmc,cd->jpmd", spectrum, spec_weight) * quad_column
        degree = dot("lmj,jpmd->lpmd", legendre, mixed) * degree_gain[:, None, None, :]
        synthesis = dot("lmj,lpmd->jpmd", legendre, degree) * order_weight
        return spectrum, plain_scatter(synthesis, parts)

    def backward(received, spectrum):
        error = plain_gather(received, parts, own) * order_weight
        gained = dot("lmj,jpmd->lpmd", legendre, error) * degree_gain[:, None, None, :]
        back = dot("lmj,lpmd->jpmd", legendre, gained) * quad_column
        sent = plain_scatter(dot("jpmd,cd->jpmc", back, spec_weight), parts)
        weight_part = dot("jpmc,jpmd->cd", spectrum, back)
        shares = weight_part.reshape(sent.shape[0], -1, weight_part.shape[1])
        return jnp.concatenate([sent, shares], axis=1)

    return forward, backward


def filter_coefficients(filters, disco_weight, band_start, band_reach):
    coefficient = jnp.einsum("ikrt,kc->irtc", filters, disco_weight, precision=highest)
    window = jnp.arange(WIN, dtype=jnp.int32)
    coefficient = jnp.where(
        (window[None, :] < band_reach[:, None])[:, :, None, None], coefficient, 0.0
    )
    offset = jnp.arange(-HMAX, HMAX + 1, dtype=jnp.int32)
    lands = offset[None, :, None] == band_start[:, None, None] + window[None, None, :]
    by_offset = jnp.sum(
        jnp.where(lands[:, :, :, None, None], coefficient[:, None], 0.0), axis=2
    )
    coef = by_offset.reshape(filters.shape[0], SPAN * KLON, LANES)
    return jnp.pad(coef, ((0, 0), (0, TAPS - SPAN * KLON), (0, 0)))


def swap_parts(x, axis):
    return lax.all_to_all(x, axis, split_axis=0, concat_axis=0, tiled=True)


def after(first, *later):
    return lax.optimization_barrier((first, *later))


def body(
    grid_field, filters, disco_weight, band_start, band_reach, spec_weight, degree_gain, cotangent
):
    band_rows, lon_local, chans = grid_field.shape
    bands, parts = lax.axis_size("lat"), lax.axis_size("chan")
    devices = bands * parts
    lat_total, lon_total = band_rows * bands, lon_local * parts
    own, share = M // devices, chans // devices
    assert band_rows == HMAX and chans == 2 * LANES and parts == 4
    band, part = lax.axis_index("lat"), lax.axis_index("chan")
    me, half, part_index = band * parts + part, part % 2, part[None]
    both_axes = ("lat", "chan")
    high, low = wave_tables(lon_total, own)
    depth = (lon_local + LANES - 1) // LANES * LANES
    apart_t = [
        jnp.asarray(np.ascontiguousarray(half_tables(table, depth).transpose(0, 2, 1)))
        for table in (high, low)
    ]
    high_t, low_t = (jnp.asarray(np.ascontiguousarray(t.T)) for t in (high, low))
    high, low = jnp.asarray(high), jnp.asarray(low)
    up = [(i, i + 1) for i in range(bands - 1)]
    down = [(i + 1, i) for i in range(bands - 1)]

    def halo(x):
        return lax.ppermute(x, "lat", up), x, lax.ppermute(x, "lat", down)

    def part_swap(x, distance):
        return lax.ppermute(x, "chan", [(i, i ^ distance) for i in range(parts)])

    def half_of(x, which):
        return lax.dynamic_slice_in_dim(x, which * LANES, LANES, axis=2)

    def edges(x):
        return part_swap(jnp.concatenate([x[:, :8], x[:, -8:]], axis=1), 2)

    def exchange(modes):
        return swap_parts(modes.reshape(devices, -1, modes.shape[-1]), both_axes)

    outgoing, cotangent, degree_gain, disco_weight, band_start = after(
        half_of(grid_field, 1 - half), cotangent, degree_gain, disco_weight, band_start
    )
    field_other = part_swap(outgoing, 1)
    first_order = owned_orders(me, devices)
    factors = mode_factors(first_order, own, lat_total, degree_gain)
    cot_out = half_of(cotangent, 1 - half)
    field_other, factors, cot_out = after(field_other, factors, cot_out)
    modes, field = analyze(part_index, lon_total, grid_field, field_other, high, low)

    modes, field_sent, cot_out, disco_weight, band_start = after(
        modes, field, cot_out, disco_weight, band_start
    )
    mine = lax.dynamic_slice_in_dim(disco_weight, half * LANES, LANES, axis=1)
    coef = filter_coefficients(filters, mine, band_start, band_reach)
    rows = halo(field_sent)
    cot_others = [part_swap(cot_out[row : row + 1], 1) for row in range(band_rows)]
    forward, backward = mode_stages(first_order, own, parts, factors, degree_gain, spec_weight)
    spectrum, synthesis = forward(exchange(modes))
    synthesis, edge, cot_others[0] = after(synthesis, edges(field_sent), cot_others[0])

    local, adjoint = local_filter(*rows, *halo(jnp.concatenate([edge, coef], axis=1)))
    error_modes, out_own, *out_sends, error = grid_stage(
        part_index, exchange(synthesis), field, local, cotangent, cot_others,
        (high, low, high_t, low_t),
    )

    out_others = [part_swap(x, 1) for x in out_sends]
    rows = [lax.ppermute(error[row : row + 1], "lat", up) for row in range(band_rows)]
    rows += [error, lax.ppermute(error, "lat", down)]
    sent = backward(exchange(error_modes), spectrum)
    sent, edge, out_others[0], rows[0], rows[3] = after(
        sent, edges(error), out_others[0], rows[0], rows[3]
    )
    base = adjoint_filter(part_index, *rows, *halo(edge), adjoint, cotangent, cot_others)
    received = exchange(sent)
    modes = received if own % 8 == 0 else received[:, : 2 * own]
    grad_send = final_stage(part_index, lon_total, 2 * own, modes, base, *apart_t, True)
    grad_send, received, *out_others = after(grad_send, received, *out_others)
    grad_other = part_swap(grad_send, 1)
    if own % 8 == 0 and share % 8 == 0:
        shares = spread_shares(received, 2 * own)
    else:
        shares = jnp.sum(received[:, 2 * own :], axis=0, keepdims=True)
        shares = jnp.broadcast_to(shares, (devices,) + shares.shape[1:])
    grad_weight = swap_parts(shares, both_axes).reshape(chans, chans)
    grad_own = final_stage(part_index, lon_total, 2 * own, modes, base, *apart_t, False)
    output = join(part_index, out_own, *out_others)
    grad_input, grad_weight = after(close(part_index, grad_own, grad_other), grad_weight)
    return (output, grad_input, grad_weight)


def solution(mesh):
    in_specs = (
        P("lat", "chan", None),
        P("lat", None, None, None),
        P(),
        P("lat"),
        P("lat"),
        P(),
        P(),
        P("lat", "chan", None),
    )
    out_specs = (P("lat", "chan", None), P("lat", "chan", None), P())
    return jax.shard_map(body, mesh=mesh, in_specs=in_specs, out_specs=out_specs, check_vma=False)
```

```python
import functools
import math

import jax
import jax.numpy as jnp
import ml_dtypes
import numpy as np
from jax import lax
from jax.experimental import pallas as pl
from jax.experimental.pallas import tpu as pltpu
from jax.sharding import PartitionSpec as P

L = 360
M = 256
WIN = 3
HMAX = 2
KLON = 5
POLAR = 720
SPAN = 2 * HMAX + 1
TAPS = 32
EDGES = 16
LANES = 128
MIB = 2**20


highest = lax.Precision.HIGHEST
upper_bound = 2.0**32
lower_factor = 2.0 ** (-32)
log_step = 32.0 * math.log(2.0)

f32 = jnp.float32
bf16 = jnp.bfloat16
VMEM = pltpu.VMEM


@functools.lru_cache(maxsize=None)
def wave_tables(lon_total, own_count):
    orders = np.concatenate([np.arange(0, M, 2), np.arange(1, M, 2)]).reshape(-1, own_count)
    lons = np.arange(lon_total // 2)
    angle = (orders[:, :, None] * lons) % lon_total * (2.0 * np.pi / lon_total)
    table = np.stack([np.cos(angle), -np.sin(angle)], axis=1).reshape(2 * M, lon_total // 2)
    high = table.astype(ml_dtypes.bfloat16)
    low = (table - high.astype(np.float64)).astype(ml_dtypes.bfloat16)
    return high, low


def half_tables(table, depth):
    rows, lons = table.shape
    blocks = table.reshape(rows, 2, lons // 2).transpose(1, 0, 2)
    return np.pad(blocks, ((0, 0), (0, 0), (0, depth - lons // 2)))


def owned_orders(owner, devices):
    half = devices // 2
    return owner % half * (2 * (M // devices)) + owner // half


def grid_tables(lat_total):
    first_row = (POLAR - lat_total) // 2
    colatitude = math.pi * (jnp.arange(lat_total, dtype=f32) + float(first_row)) / POLAR
    quad_weight = 2.0 * math.pi * math.pi / POLAR * jnp.sin(colatitude)
    return (colatitude, quad_weight)


def log_norms(order_count):
    order_index = jnp.arange(order_count, dtype=f32)
    log_terms = jnp.where(
        order_index > 0.0,
        jnp.log((2.0 * order_index + 1.0) / jnp.maximum(2.0 * order_index, 1.0)),
        0.0,
    )
    return -0.5 * math.log(4.0 * math.pi) + 0.5 * jnp.cumsum(log_terms)


def split(x):
    high = x.astype(bf16)
    return high, (x - high.astype(f32)).astype(bf16)


def dot_split(a, b, dims):
    (ah, al), (bh, bl) = split(a), split(b)
    dot = lambda u, v: lax.dot_general(u, v, (dims, ((), ())), preferred_element_type=f32)
    return dot(ah, bh) + (dot(ah, bl) + dot(al, bh))


def cost(us):
    return pl.CostEstimate(flops=int(us * 1e9), bytes_accessed=int(us * 3e6), transcendentals=0)


def call(kernel, out_shape, in_specs, scratch=(), us=1.0, limit=16, out_spaces=None, aliases=None):
    run = pl.pallas_call(
        kernel,
        out_shape=out_shape,
        in_specs=[pl.BlockSpec(memory_space=space) for space, _ in in_specs],
        out_specs=jax.tree.map(
            lambda space: pl.BlockSpec(memory_space=space),
            out_spaces or jax.tree.map(lambda _: VMEM, out_shape),
        ),
        scratch_shapes=list(scratch),
        input_output_aliases=aliases or {},
        compiler_params=pltpu.CompilerParams(vmem_limit_bytes=limit * MIB),
        cost_estimate=cost(us),
    )
    keeps = [keep for _, keep in in_specs]
    return lambda *args: run(
        *[held(x, keep) if keep else x for x, keep in zip(args, keeps, strict=True)]
    )


def held(x, space):
    return pltpu.with_memory_space_constraint(x, space)


def vmem(count):
    return [(VMEM, None)] * count


def resident(count):
    return [(VMEM, VMEM)] * count


def loaded(count):
    return [(VMEM, pltpu.HBM)] * count


def hbm(count):
    return [(pltpu.HBM, pltpu.HBM)] * count


smem = (pltpu.SMEM, None)


def struct(*shape, dtype=f32):
    return jax.ShapeDtypeStruct(shape, dtype)


def near(*shape, dtype=f32):
    return pltpu.VMEM(shape, dtype)


def kept(*shape, dtype=f32):
    return pltpu.HBM(shape, dtype)


def own_half(part):
    return part % 2


def lane_half(x_ref, half):
    return x_ref.at[:, :, pl.ds(pl.multiple_of(half * LANES, LANES), LANES)]


def lon_half(x_ref, half):
    width = x_ref.shape[1] // 2
    return x_ref.at[:, pl.ds(pl.multiple_of(half * width, 8), width), :]


def pair_copies(half, own_hbm, other_hbms, target, sems):
    copies = [pltpu.make_async_copy(lane_half(own_hbm, half), lon_half(target, half), sems.at[0])]
    there = lon_half(target, 1 - half)
    for row, other_hbm in enumerate(other_hbms):
        copies.append(
            pltpu.make_async_copy(other_hbm, there.at[pl.ds(row, 1)], sems.at[1 + row])
        )
    for copy in copies:
        copy.start()
    return copies


def join_kernel(part_ref, own_ref, *refs):
    o_ref = refs[-1]
    half = own_half(part_ref[0])
    mine, theirs = (
        pl.ds(pl.multiple_of(place * LANES, LANES), LANES) for place in (half, 1 - half)
    )
    o_ref[:, :, mine] = own_ref[...]
    for row, other_ref in enumerate(refs[:-1]):
        o_ref[pl.ds(row, other_ref.shape[0]), :, theirs] = other_ref[...]


def join(part, own, *others):
    rows, lons, _ = own.shape
    return call(
        join_kernel, kept(rows, lons, 2 * LANES), [smem] + vmem(1 + len(others))
    )(part, own, *others)


def side_by_side(x):
    return jnp.concatenate([x[0], x[1]], axis=1)


def three(table_high, table_low, high, low):
    dot = lambda u, v: jnp.dot(u, v, preferred_element_type=f32)
    return dot(table_high, high) + (dot(table_high, low) + dot(table_low, high))


def fetches(sources, targets, sems, pieces):
    copies = []
    for index, (source, target) in enumerate(zip(sources, targets, strict=True)):
        tile = source.shape[0] // pieces
        copies.append(
            [
                pltpu.make_async_copy(
                    source.at[pl.ds(piece * tile, tile)],
                    target.at[pl.ds(piece * tile, tile)],
                    sems.at[index, piece],
                )
                for piece in range(pieces)
            ]
        )
    for piece in range(pieces):
        for group in copies:
            group[piece].start()
    return lambda index, piece: copies[index][piece].wait()


def bring_kernel(views, part_ref, *refs):
    sources, targets, sems = refs[: len(views)], refs[len(views) : -1], refs[-1]
    copies = [
        pltpu.make_async_copy(view(source, part_ref[0]), target, sems.at[index])
        for index, (view, source, target) in enumerate(zip(views, sources, targets, strict=True))
    ]
    for copy in copies:
        copy.start()
    for copy in copies:
        copy.wait()


def bring(part, sources, view=None):
    views = [view or (lambda ref, part: ref)] * len(sources)
    shapes = [x.shape[1:] if view else x.shape for x in sources]
    return call(
        functools.partial(bring_kernel, views),
        [near(*shape, dtype=x.dtype) for shape, x in zip(shapes, sources, strict=True)],
        [smem] + hbm(len(sources)),
        [pltpu.SemaphoreType.DMA((len(sources),))],
        us=2.0,
        limit=8,
    )(part, *sources)


def there_already(index, piece):
    del index, piece


def analyze_rows(x, sign, high_ref, low_ref, wait, store):
    high, low = split(x)
    wait(0, 0)
    wait(1, 0)
    value = three(high_ref[...], low_ref[...], high, low)
    count = value.shape[0] // 2
    store(pl.ds(0, count), value[:count])
    store(pl.ds(count, count), value[count:] * sign)


def compose_rows(modes, sign, thigh_ref, tlow_ref, wait, store, pieces):
    count = modes.shape[0] // 2
    high, low = split(jnp.concatenate([modes[:count], modes[count:] * sign], axis=0))
    tile = thigh_ref.shape[0] // pieces
    for piece in range(pieces):
        rows = pl.ds(piece * tile, tile)
        wait(0, piece)
        wait(1, piece)
        store(rows, three(thigh_ref[rows, :], tlow_ref[rows, :], high, low))


def turn_sign(part):
    return (1 - 2 * (part // 2)).astype(f32)


def analyze_kernel(scale, part_ref, own_hbm, other_ref, high_ref, low_ref, o_ref, field_hbm,
                   x_ref, pair_sem, out_sem):
    part = part_ref[0]
    half = own_half(part)
    mine = pltpu.make_async_copy(lane_half(own_hbm, half), lon_half(x_ref, half), pair_sem)
    mine.start()
    lon_half(x_ref, 1 - half)[...] = other_ref[...]
    mine.wait()
    out = pltpu.make_async_copy(x_ref, field_hbm, out_sem)
    out.start()

    def store(rows, value):
        o_ref[rows, :] = value * scale

    analyze_rows(side_by_side(x_ref[...]), turn_sign(part), high_ref, low_ref, there_already, store)
    out.wait()


def analyze(part, lon_total, own, other, high, low):
    rows, lons, _ = own.shape
    field = (rows, 2 * lons, LANES)
    return call(
        functools.partial(analyze_kernel, 1.0 / lon_total),
        (struct(2 * M, rows * LANES), kept(*field)),
        [smem] + hbm(1) + vmem(1) + resident(2),
        [VMEM(field, f32), pltpu.SemaphoreType.DMA, pltpu.SemaphoreType.DMA],
        us=3.0,
        out_spaces=(VMEM, pltpu.HBM),
    )(part, own, other, high, low)


def grid_kernel(part_ref, s_ref, field_hbm, local_hbm, cot_hbm, first_hbm, second_hbm,
                high_hbm, low_hbm, thigh_hbm, tlow_hbm,
                mode_ref, own_hbm, send_first_hbm, send_second_hbm, err_hbm,
                x_ref, local_ref, cot_ref, spec_ref, out_ref, err_ref,
                high_ref, low_ref, thigh_ref, tlow_ref,
                back_sems, sems, cot_sems, other_sems, out_sems):
    part = part_ref[0]
    half, sign = own_half(part), turn_sign(part)
    wait_back = fetches((thigh_hbm, tlow_hbm), (thigh_ref, tlow_ref), back_sems, 3)
    others = [
        pltpu.make_async_copy(source, target, other_sems.at[index])
        for index, (source, target) in enumerate(((local_hbm, local_ref), (field_hbm, x_ref)))
    ]
    for copy in others:
        copy.start()
    others += pair_copies(half, cot_hbm, (first_hbm, second_hbm), cot_ref, cot_sems)
    wait = fetches((high_hbm, low_hbm), (high_ref, low_ref), sems, 1)

    def store_spec(rows, value):
        spec_ref[rows, :] = value

    modes = s_ref[...].reshape(thigh_ref.shape[1], s_ref.shape[2])
    compose_rows(modes, sign, thigh_ref, tlow_ref, wait_back, store_spec, 3)
    for copy in others:
        copy.wait()
    tile = x_ref.shape[1] // 6
    for row in range(x_ref.shape[0]):
        for piece in range(6):
            lons = pl.ds(piece * tile, tile)
            hidden = local_ref[row, lons, :] + spec_ref[lons, pl.ds(row * LANES, LANES)]
            gate = 1.0 / (1.0 + jnp.exp(-hidden))
            out_ref[row, lons, :] = x_ref[row, lons, :] + hidden * gate
            err_ref[row, lons, :] = cot_ref[row, lons, :] * (gate * (1.0 + hidden * (1.0 - gate)))
    there = lon_half(out_ref, 1 - half)
    outs = [
        pltpu.make_async_copy(source, target, out_sems.at[index])
        for index, (source, target) in enumerate(
            (
                (err_ref, err_hbm),
                (lon_half(out_ref, half), own_hbm),
                (there.at[pl.ds(0, 1)], send_first_hbm),
                (there.at[pl.ds(1, 1)], send_second_hbm),
            )
        )
    ]
    for copy in outs:
        copy.start()

    def store(rows, value):
        mode_ref[rows, :] = value

    analyze_rows(side_by_side(err_ref[...]), sign, high_ref, low_ref, wait, store)
    for copy in outs:
        copy.wait()


def grid_stage(part, synthesis, field, local, cotangent, others, tables):
    rows, lons, _ = field.shape
    block = (rows, lons // 2, LANES)
    grid = VMEM(field.shape, f32)
    return call(
        grid_kernel,
        (
            struct(2 * M, rows * LANES),
            kept(*block),
            kept(1, *block[1:]),
            kept(1, *block[1:]),
            kept(*field.shape),
        ),
        [smem] + vmem(1) + hbm(9),
        [grid, grid, grid, VMEM((lons, rows * LANES), f32), grid, grid]
        + [VMEM(table.shape, bf16) for table in tables]
        + [pltpu.SemaphoreType.DMA((2, 3)), pltpu.SemaphoreType.DMA((2, 1))]
        + [pltpu.SemaphoreType.DMA((count,)) for count in (3, 2, 4)],
        us=4.0,
        limit=32,
        out_spaces=(VMEM,) + (pltpu.HBM,) * 4,
    )(part, synthesis, field, local, cotangent, *others, *tables)


def final_kernel(scale, rows_own, theirs, part_ref, s_ref, base_hbm, *refs):
    part = part_ref[0]
    half = 1 - own_half(part) if theirs else own_half(part)
    if theirs:
        thigh_ref, tlow_ref, o_ref, *shares_ref, base_ref, base_sem = refs
        wait = there_already
        if shares_ref:
            share = jnp.sum(s_ref[:, pl.ds(rows_own, shares_ref[0].shape[1]), :], axis=0)
            shares_ref[0][...] = jnp.broadcast_to(share[None], shares_ref[0].shape)
    else:
        thigh_hbm, tlow_hbm, out_hbm, o_ref, base_ref, thigh_ref, tlow_ref, sems, base_sem = refs
        wait = fetches((thigh_hbm.at[half], tlow_hbm.at[half]), (thigh_ref, tlow_ref), sems, 1)
    base_copy = pltpu.make_async_copy(lon_half(base_hbm, half), base_ref, base_sem)
    base_copy.start()
    modes = s_ref[:, pl.ds(0, rows_own), :].reshape(thigh_ref.shape[1], s_ref.shape[2])
    total = o_ref.shape[1]

    def store(lons, value):
        count = min(lons.size, total - lons.start)
        for row in range(base_ref.shape[0]):
            lanes = slice(row * LANES, (row + 1) * LANES)
            o_ref[row, pl.ds(lons.start, count), :] = scale * value[:count, lanes]

    compose_rows(modes, turn_sign(part), thigh_ref, tlow_ref, wait, store, 1)
    base_copy.wait()
    o_ref[...] = o_ref[...] + base_ref[...]
    if not theirs:
        out = pltpu.make_async_copy(o_ref, lane_half(out_hbm, half), base_sem)
        out.start()
        out.wait()


def final_stage(part, lon_total, rows_own, modes, base, high_t, low_t, theirs):
    rows, lons, _ = base.shape
    block = (rows, lons // 2, LANES)
    scratch = [VMEM(block, f32)]
    out_shape = [struct(*block)]
    share = modes.shape[1] - rows_own
    if share:
        out_shape.append(struct(modes.shape[0], share, modes.shape[2]))
    if not theirs:
        out_shape = kept(rows, lons // 2, 2 * LANES)
        table = VMEM(high_t.shape[1:], bf16)
        scratch = [VMEM(block, f32)] * 2 + [table, table, pltpu.SemaphoreType.DMA((2, 1))]
    return call(
        functools.partial(final_kernel, 1.0 / lon_total, rows_own, theirs),
        out_shape,
        [smem] + vmem(1) + hbm(1) + (resident(2) if theirs else hbm(2)),
        scratch + [pltpu.SemaphoreType.DMA],
        us=2.0,
        out_spaces=None if theirs else pltpu.HBM,
    )(part, modes, base, high_t, low_t)


def close_kernel(part_ref, held_hbm, other_ref, o_hbm, sem):
    del held_hbm
    copy = pltpu.make_async_copy(other_ref, lane_half(o_hbm, 1 - own_half(part_ref[0])), sem)
    copy.start()
    copy.wait()


def close(part, held_half, other):
    return call(
        close_kernel,
        kept(*held_half.shape),
        [smem] + hbm(1) + vmem(1),
        [pltpu.SemaphoreType.DMA],
        us=8.0,
        out_spaces=pltpu.HBM,
        aliases={1: 0},
    )(part, held_half, other)


def filter_sums(refs, edge_refs, coef_ref, finish, sums_ref):
    lons = refs[0].shape[1]
    tile = lons // 18
    sources = [(x_ref, row) for x_ref in refs for row in range(x_ref.shape[0])]
    for row in range(2):
        def add(values, rows, row=row):
            for tap in range(KLON):
                total = values[0] * coef_ref[row, pl.ds(tap, 1), :]
                for offset in range(1, SPAN):
                    total = total + values[offset] * coef_ref[row, pl.ds(offset * KLON + tap, 1), :]
                sums_ref[tap, rows, :] = total

        near = sources[row : row + SPAN]
        edges = [(edge_ref, k) for edge_ref in edge_refs for k in range(2)][row : row + SPAN]
        add([edge_ref[k, pl.ds(8, 8), :] for edge_ref, k in edges], pl.ds(0, 8))
        add([edge_ref[k, pl.ds(0, 8), :] for edge_ref, k in edges], pl.ds(lons + 8, 8))

        @pl.loop(0, 18)
        def _(piece, near=near, add=add):
            start = pl.multiple_of(piece * tile, 8)
            values = [x_ref[k, pl.ds(start, tile), :] for x_ref, k in near]
            add(values, pl.ds(pl.multiple_of(start + 8, 8), tile))

        for piece in range(18):
            total = None
            for tap in range(KLON):
                value = sums_ref[tap, pl.ds(piece * tile + 8 + tap - KLON // 2, tile), :]
                total = value if total is None else total + value
            finish(row, pl.ds(piece * tile, tile), total)


def filter_kernel(prev_ref, own_ref, next_ref, lower_ref, middle_ref, upper_ref, o_ref, adjoint_ref,
                  sums_ref):
    def finish(row, lons, value):
        o_ref[row, lons, :] = value

    taps = pl.ds(EDGES, TAPS)
    coef_refs = [ref.at[:, taps] for ref in (lower_ref, middle_ref, upper_ref)]
    filter_sums(
        (prev_ref, own_ref, next_ref), (lower_ref, middle_ref, upper_ref), coef_refs[1], finish, sums_ref
    )
    adjoint_ref[...] = jnp.zeros_like(adjoint_ref)
    sources = [(c_ref, row) for c_ref in coef_refs for row in range(2)]
    for row in range(2):
        for offset in range(SPAN):
            c_ref, k = sources[row + offset]
            for tap in range(KLON):
                mirrored = (SPAN - 1 - offset) * KLON + KLON - 1 - tap
                adjoint_ref[row, pl.ds(offset * KLON + tap, 1), :] = c_ref[k, pl.ds(mirrored, 1), :]


def adjoint_kernel(part_ref, first_ref, second_ref, own_ref, next_ref, lower_ref, middle_ref, upper_ref, coef_ref,
                   cot_hbm, first_hbm, second_hbm,
                   o_ref, sums_ref, cot_ref, cot_sems):
    copies = pair_copies(
        own_half(part_ref[0]), cot_hbm, (first_hbm, second_hbm), cot_ref, cot_sems
    )
    for copy in copies:
        copy.wait()

    def finish(row, lons, value):
        o_ref[row, lons, :] = cot_ref[row, lons, :] + value

    edge_refs = (lower_ref, middle_ref, upper_ref)
    filter_sums((first_ref, second_ref, own_ref, next_ref), edge_refs, coef_ref, finish, sums_ref)


def local_filter(prev, own, behind, *edges):
    return call(
        filter_kernel,
        (kept(*own.shape), kept(own.shape[0], TAPS, LANES)),
        loaded(3) + vmem(3),
        [VMEM((KLON, own.shape[1] + 16, LANES), f32)],
        us=4.0,
    )(prev, own, behind, *edges)


def adjoint_filter(part, first, second, own, behind, lower, middle, upper, coef, cotangent, others):
    return call(
        adjoint_kernel,
        kept(*own.shape),
        [smem] + loaded(4) + vmem(4) + hbm(3),
        [VMEM((KLON, own.shape[1] + 16, LANES), f32), VMEM(own.shape, f32)]
        + [pltpu.SemaphoreType.DMA((3,))],
        us=4.0,
    )(part, first, second, own, behind, lower, middle, upper, coef, cotangent, *others)


def coupling_kernel(lat_total, first_ref, gain_ref, o_hbm, step_ref, back_ref, start_ref, leg_ref,
                    scale_ref, padded_ref, column_ref, o_ref, out_sems):
    degree_count, chans = gain_ref.shape
    depth = padded_ref.shape[0]
    own = LANES // lat_total
    first_row = float((POLAR - lat_total) // 2)
    lane = lax.broadcasted_iota(jnp.int32, (1, LANES), 1)
    order = 2 * (lane % own) + first_ref[0]
    colatitude = math.pi * ((lane // own).astype(f32) + first_row) / POLAR
    cosine, log_sine = jnp.cos(colatitude), jnp.log(jnp.sin(colatitude))
    k = lax.broadcasted_iota(jnp.int32, (M, LANES), 0)
    k_f = k.astype(f32)
    log_terms = jnp.log((2.0 * k_f + 1.0) / jnp.maximum(2.0 * k_f, 1.0))
    log_norm = -0.5 * math.log(4.0 * math.pi) + 0.5 * jnp.sum(
        jnp.where((k > 0) & (k <= order), log_terms, 0.0), axis=0, keepdims=True
    )
    norm_start = jnp.exp(log_norm)
    degree = lax.broadcasted_iota(jnp.int32, (degree_count, LANES), 0)
    degree_f, order_f = degree.astype(f32), order.astype(f32)
    step = jnp.where(
        degree > order,
        jnp.sqrt(
            jnp.maximum(4.0 * degree_f * degree_f - 1.0, 0.0)
            / jnp.maximum(degree_f * degree_f - order_f * order_f, 1.0)
        ),
        0.0,
    )
    lower = degree_f - 1.0
    back = jnp.sqrt(
        jnp.maximum(lower * lower - order_f * order_f, 0.0) / (4.0 * lower * lower - 1.0)
    )
    step_ref[...] = step * cosine
    back_ref[...] = step * back
    start_ref[...] = jnp.where(degree == order, norm_start, 0.0)
    zeros = jnp.zeros((1, LANES), f32)

    def block(index, carry):
        previous, second, log_scale = carry
        first = pl.multiple_of(index * 8, 8)
        scale_ref[pl.ds(first, 8), :] = jnp.broadcast_to(log_scale, (8, LANES))
        for offset in range(8):
            row = pl.ds(first + offset, 1)
            rest = start_ref[row, :] - back_ref[row, :] * second
            current = step_ref[row, :] * previous + rest
            leg_ref[row, :] = current
            second, previous = previous, current
        too_large = jnp.abs(previous) > upper_bound
        second = jnp.where(too_large, second * lower_factor, second)
        previous = jnp.where(too_large, previous * lower_factor, previous)
        return previous, second, jnp.where(too_large, log_scale + log_step, log_scale)

    lax.fori_loop(0, degree_count // 8, block, (zeros, zeros, order_f * log_sine))
    leg_ref[pl.ds(0, degree_count), :] = leg_ref[pl.ds(0, degree_count), :] * jnp.exp(scale_ref[...])
    rest = depth - degree_count
    leg_ref[pl.ds(degree_count, rest), :] = jnp.zeros((rest, LANES), f32)
    padded_ref[pl.ds(0, degree_count), :] = gain_ref[...]
    padded_ref[pl.ds(degree_count, rest), :] = jnp.zeros((rest, chans), f32)
    column_ref[...] = leg_ref[...].T

    high, low = split(padded_ref[...])
    row = lax.broadcasted_iota(jnp.int32, (LANES, LANES), 0)
    quad = 2.0 * math.pi * math.pi / POLAR * jnp.sin(
        math.pi * ((row // own).astype(f32) + first_row) / POLAR
    )
    weight = quad * jnp.where(row % own + first_ref[0] == 0, 1.0, 2.0)
    weight = jnp.concatenate([weight] * (chans // LANES), axis=1)
    group = lat_total // out_sems.shape[0]
    copies = []
    for piece in range(out_sems.shape[0]):
        both = jnp.concatenate(
            [
                column_ref[...]
                * jnp.concatenate([column_ref[pl.ds(j * own, own), :]] * lat_total, axis=0)
                for j in range(piece * group, (piece + 1) * group)
            ],
            axis=0,
        )
        total = three(*split(both), high, low)
        for j in range(group):
            o_ref[piece * group + j] = (total[j * LANES : (j + 1) * LANES] * weight).reshape(
                lat_total, own, chans
            )
        block_of = pl.ds(piece * group, group)
        copies.append(
            pltpu.make_async_copy(o_ref.at[block_of], o_hbm.at[block_of], out_sems.at[piece])
        )
        copies[-1].start()
    for copy in copies:
        copy.wait()


def coupling(first_order, degree_gain, lat_total):
    degrees, chans = degree_gain.shape
    own = LANES // lat_total
    depth = (degrees + LANES - 1) // LANES * LANES
    table = (lat_total, lat_total, own, chans)
    rows = VMEM((degrees, LANES), f32)
    return call(
        functools.partial(coupling_kernel, lat_total),
        kept(*table),
        [smem] + loaded(1),
        [rows, rows, rows, VMEM((depth, LANES), f32), rows]
        + [VMEM((depth, chans), f32), VMEM((LANES, depth), f32), VMEM(table, f32)]
        + [pltpu.SemaphoreType.DMA((4,))],
        us=6.0,
        out_spaces=pltpu.HBM,
    )(first_order, degree_gain)


def gather_modes(r_ref, write, parts):
    for band in range(r_ref.shape[0] // parts):
        for half in range(2):
            both = r_ref[band * parts + half]
            for other in range(half + 2, parts, 2):
                both = both + r_ref[band * parts + other]
            for row in range(2):
                lanes = slice(row * LANES, (row + 1) * LANES)
                write(2 * band + row, pl.ds(half * LANES, LANES), both[:, lanes])


def scatter_modes(read, s_ref, parts, rows):
    for band in range(s_ref.shape[0] // parts):
        for part in range(parts):
            for row in range(2):
                lanes = pl.ds(row * LANES, LANES)
                value = read(2 * band + row, pl.ds(part % 2 * LANES, LANES))
                s_ref[band * parts + part, pl.ds(0, rows), lanes] = value


def forward_modes_kernel(parts, r_ref, coupling_hbm, w_hbm, x_ref, s_ref, y_ref, z_ref,
                         coupling_ref, w_ref, sems):
    wait_w = fetches((w_hbm,), (w_ref,), sems.at[pl.ds(0, 1)], 2)
    wait = fetches((coupling_hbm,), (coupling_ref,), sems.at[pl.ds(1, 1)], 8)

    def write(j, lanes, value):
        x_ref[j, :, lanes] = value

    gather_modes(r_ref, write, parts)
    lats, rows, chans = x_ref.shape
    own = rows // 2
    for piece in range(2):
        wait_w(0, piece)
    y_ref[...] = dot_split(
        x_ref[...].reshape(lats * rows, chans), w_ref[...], ((1,), (0,))
    ).reshape(lats, rows, chans)
    for piece in range(8):
        wait(0, piece)

        @pl.loop(piece * (lats // 8), (piece + 1) * (lats // 8))
        def _(j):
            totals = [jnp.zeros((own, chans), f32)] * 2
            for other in range(lats):
                factor = coupling_ref[j, other]
                for p in range(2):
                    totals[p] = totals[p] + factor * y_ref[other, pl.ds(p * own, own), :]
            for p in range(2):
                z_ref[j, pl.ds(p * own, own), :] = totals[p]

    scatter_modes(lambda j, lanes: z_ref[j, :, lanes], s_ref, parts, rows)


def backward_modes_kernel(parts, r_ref, coupling_hbm, w_hbm, x_hbm, s_hbm, s_ref, e_ref, v_ref,
                          coupling_ref, w_ref, x_ref, sems, out_sems):
    wait = fetches((coupling_hbm,), (coupling_ref,), sems.at[pl.ds(0, 1)], 8)
    wait_rest = fetches((w_hbm, x_hbm), (w_ref, x_ref), sems.at[pl.ds(1, 2)], 2)

    def write(j, lanes, value):
        e_ref[j, :, lanes] = value

    gather_modes(r_ref, write, parts)
    lats, rows, chans = x_ref.shape
    own = rows // 2
    for piece in range(8):
        wait(0, piece)

    @pl.loop(0, lats)
    def _(j):
        totals = [jnp.zeros((own, chans), f32)] * 2
        for other in range(lats):
            factor = coupling_ref[other, j]
            for p in range(2):
                totals[p] = totals[p] + factor * e_ref[other, pl.ds(p * own, own), :]
        for p in range(2):
            v_ref[j, pl.ds(p * own, own), :] = totals[p]

    for piece in range(2):
        for index in range(2):
            wait_rest(index, piece)
    v = v_ref[...].reshape(lats * rows, chans)
    e_ref[...] = dot_split(v, w_ref[...], ((1,), (1,))).reshape(lats, rows, chans)
    scatter_modes(lambda j, lanes: e_ref[j, :, lanes], s_ref, parts, rows)
    sent = pltpu.make_async_copy(
        s_ref.at[:, pl.ds(0, rows), :], s_hbm.at[:, pl.ds(0, rows), :], out_sems.at[0]
    )
    sent.start()
    weight_part = dot_split(x_ref[...].reshape(lats * rows, chans), v, ((0,), (0,)))
    share = chans // s_ref.shape[0]
    s_ref[:, pl.ds(rows, share), :] = weight_part.reshape(s_ref.shape[0], share, chans)
    shares = pltpu.make_async_copy(
        s_ref.at[:, pl.ds(rows, share), :], s_hbm.at[:, pl.ds(rows, share), :], out_sems.at[1]
    )
    shares.start()
    sent.wait()
    shares.wait()


def legendre_orders(colatitude, orders, log_norm, degree_count):
    cosine = jnp.cos(colatitude)[None, :]
    log_sine = jnp.log(jnp.sin(colatitude))[None, :]
    order_f = orders.astype(f32)[:, None]
    norm_start = jnp.exp(log_norm)[:, None] + jnp.zeros_like(cosine)
    zeros_state = jnp.zeros((orders.shape[0], colatitude.shape[0]), f32)

    def advance(carry, degree):
        previous, second, log_scale = carry
        degree_f = degree.astype(f32)
        step_factor = jnp.where(
            degree > orders[:, None],
            jnp.sqrt(
                jnp.maximum(4.0 * degree_f * degree_f - 1.0, 0.0)
                / jnp.maximum(degree_f * degree_f - order_f * order_f, 1.0)
            ),
            0.0,
        )
        lower_degree = degree_f - 1.0
        back_factor = jnp.sqrt(
            jnp.maximum(lower_degree * lower_degree - order_f * order_f, 0.0)
            / (4.0 * lower_degree * lower_degree - 1.0)
        )
        current = jnp.where(
            degree == orders[:, None],
            norm_start,
            step_factor * (cosine * previous - back_factor * second),
        )
        too_large = jnp.abs(current) > upper_bound
        current = jnp.where(too_large, current * lower_factor, current)
        previous = jnp.where(too_large, previous * lower_factor, previous)
        log_scale = jnp.where(too_large, log_scale + log_step, log_scale)
        return ((current, previous, log_scale), current * jnp.exp(log_scale))

    start_state = (zeros_state, zeros_state, order_f * log_sine)
    _, tables = lax.scan(advance, start_state, jnp.arange(degree_count, dtype=jnp.int32), unroll=8)
    return tables


def plain_gather(received, parts, own):
    bands = received.shape[0] // parts
    blocks = received.reshape(bands, parts // 2, 2, 2, own, 2, LANES).sum(axis=1)
    return blocks.transpose(0, 4, 2, 3, 1, 5).reshape(2 * bands, 2, own, 2 * LANES)


def plain_scatter(modes, parts):
    lats, _, own, _ = modes.shape
    bands = lats // 2
    blocks = modes.reshape(bands, 2, 2, own, 2, LANES).transpose(0, 4, 2, 3, 1, 5)
    blocks = jnp.broadcast_to(blocks[:, None], (bands, parts // 2) + blocks.shape[1:])
    return blocks.reshape(bands * parts, 2 * own, 2 * LANES)


def mode_factors(first_order, own, lat_total, degree_gain):
    if own % 8 == 0 and own * lat_total == LANES and degree_gain.shape[0] % 8 == 0:
        return coupling(first_order[None], degree_gain, lat_total)
    orders = first_order + 2 * jnp.arange(own, dtype=jnp.int32)
    log_norm = jnp.take(log_norms(M), orders)
    return legendre_orders(grid_tables(lat_total)[0], orders, log_norm, degree_gain.shape[0])


def mode_stages(first_order, own, parts, factors, degree_gain, spec_weight):
    if factors.ndim == 4:
        chans = spec_weight.shape[0]
        shape = (factors.shape[0], 2 * own, chans)

        def forward(received):
            return call(
                functools.partial(forward_modes_kernel, parts),
                (kept(*shape), struct(*received.shape)),
                vmem(1) + hbm(2),
                [VMEM(shape, f32), VMEM(shape, f32), VMEM(factors.shape, f32)]
                + [VMEM(spec_weight.shape, f32), pltpu.SemaphoreType.DMA((2, 8))],
                us=2.0,
            )(received, factors, spec_weight)

        def backward(received, spectrum):
            sent = (received.shape[0], 2 * own + chans // received.shape[0], chans)
            return call(
                functools.partial(backward_modes_kernel, parts),
                kept(*sent),
                vmem(1) + hbm(3),
                [VMEM(sent, f32), VMEM(shape, f32), VMEM(shape, f32), VMEM(factors.shape, f32)]
                + [VMEM(spec_weight.shape, f32), VMEM(shape, f32)]
                + [pltpu.SemaphoreType.DMA((3, 8)), pltpu.SemaphoreType.DMA((2,))],
                us=2.0,
                out_spaces=pltpu.HBM,
            )(received, factors, spec_weight, spectrum)

        return forward, backward

    legendre, lat_total = factors, factors.shape[2]
    quad_weight = grid_tables(lat_total)[1]
    orders = first_order + 2 * jnp.arange(own, dtype=jnp.int32)
    order_weight = jnp.where(orders == 0, 1.0, 2.0).astype(f32)[None, None, :, None]
    quad_column = quad_weight[:, None, None, None]
    dot = functools.partial(jnp.einsum, precision=highest)

    def forward(received):
        spectrum = plain_gather(received, parts, own)
        mixed = dot("jpmc,cd->jpmd", spectrum, spec_weight) * quad_column
        degree = dot("lmj,jpmd->lpmd", legendre, mixed) * degree_gain[:, None, None, :]
        synthesis = dot("lmj,lpmd->jpmd", legendre, degree) * order_weight
        return spectrum, plain_scatter(synthesis, parts)

    def backward(received, spectrum):
        error = plain_gather(received, parts, own) * order_weight
        gained = dot("lmj,jpmd->lpmd", legendre, error) * degree_gain[:, None, None, :]
        back = dot("lmj,lpmd->jpmd", legendre, gained) * quad_column
        sent = plain_scatter(dot("jpmd,cd->jpmc", back, spec_weight), parts)
        weight_part = dot("jpmc,jpmd->cd", spectrum, back)
        shares = weight_part.reshape(sent.shape[0], -1, weight_part.shape[1])
        return jnp.concatenate([sent, shares], axis=1)

    return forward, backward


def filter_coefficients(filters, disco_weight, band_start, band_reach):
    coefficient = jnp.einsum("ikrt,kc->irtc", filters, disco_weight, precision=highest)
    window = jnp.arange(WIN, dtype=jnp.int32)
    coefficient = jnp.where(
        (window[None, :] < band_reach[:, None])[:, :, None, None], coefficient, 0.0
    )
    offset = jnp.arange(-HMAX, HMAX + 1, dtype=jnp.int32)
    lands = offset[None, :, None] == band_start[:, None, None] + window[None, None, :]
    by_offset = jnp.sum(
        jnp.where(lands[:, :, :, None, None], coefficient[:, None], 0.0), axis=2
    )
    coef = by_offset.reshape(filters.shape[0], SPAN * KLON, LANES)
    return jnp.pad(coef, ((0, 0), (0, TAPS - SPAN * KLON), (0, 0)))


def swap_parts(x, axis):
    return lax.all_to_all(x, axis, split_axis=0, concat_axis=0, tiled=True)


def after(first, *later):
    return lax.optimization_barrier((first, *later))


def body(
    grid_field, filters, disco_weight, band_start, band_reach, spec_weight, degree_gain, cotangent
):
    band_rows, lon_local, chans = grid_field.shape
    bands, parts = lax.axis_size("lat"), lax.axis_size("chan")
    devices = bands * parts
    lat_total, lon_total = band_rows * bands, lon_local * parts
    own, share = M // devices, chans // devices
    assert band_rows == HMAX and chans == 2 * LANES and parts == 4
    band, part = lax.axis_index("lat"), lax.axis_index("chan")
    me, half, part_index = band * parts + part, part % 2, part[None]
    both_axes = ("lat", "chan")
    high, low = wave_tables(lon_total, own)
    depth = (lon_local + LANES - 1) // LANES * LANES
    apart_t = [
        jnp.asarray(np.ascontiguousarray(half_tables(table, depth).transpose(0, 2, 1)))
        for table in (high, low)
    ]
    high_t, low_t = (jnp.asarray(np.ascontiguousarray(t.T)) for t in (high, low))
    high, low = jnp.asarray(high), jnp.asarray(low)
    up = [(i, i + 1) for i in range(bands - 1)]
    down = [(i + 1, i) for i in range(bands - 1)]

    def halo(x):
        return lax.ppermute(x, "lat", up), x, lax.ppermute(x, "lat", down)

    def part_swap(x, distance):
        return lax.ppermute(x, "chan", [(i, i ^ distance) for i in range(parts)])

    def half_of(x, which):
        return lax.dynamic_slice_in_dim(x, which * LANES, LANES, axis=2)

    def edges(x):
        return part_swap(jnp.concatenate([x[:, :8], x[:, -8:]], axis=1), 2)

    def exchange(modes):
        return swap_parts(modes.reshape(devices, -1, modes.shape[-1]), both_axes)

    outgoing, cotangent, degree_gain, disco_weight, band_start, tied = after(
        half_of(grid_field, 1 - half), cotangent, degree_gain, disco_weight, band_start, part_index
    )
    field_other = part_swap(outgoing, 1)
    first_order = owned_orders(me, devices)
    factors = mode_factors(first_order, own, lat_total, degree_gain)
    cot_out = half_of(cotangent, 1 - half)
    field_other, factors, cot_out = after(field_other, factors, cot_out)
    tables = bring(tied, [high, low])
    modes, field = analyze(part_index, lon_total, grid_field, field_other, *tables)

    modes, field_sent, cot_out, disco_weight, band_start = after(
        modes, field, cot_out, disco_weight, band_start
    )
    mine = lax.dynamic_slice_in_dim(disco_weight, half * LANES, LANES, axis=1)
    coef = filter_coefficients(filters, mine, band_start, band_reach)
    rows = halo(field_sent)
    cot_others = [part_swap(cot_out[row : row + 1], 1) for row in range(band_rows)]
    forward, backward = mode_stages(first_order, own, parts, factors, degree_gain, spec_weight)
    spectrum, synthesis = forward(exchange(modes))
    synthesis, edge, cot_others[0] = after(synthesis, edges(field_sent), cot_others[0])

    local, adjoint = local_filter(*rows, *halo(jnp.concatenate([edge, coef], axis=1)))
    error_modes, out_own, *out_sends, error = grid_stage(
        part_index, exchange(synthesis), field, local, cotangent, cot_others,
        (high, low, high_t, low_t),
    )

    out_others = [part_swap(x, 1) for x in out_sends]
    rows = [lax.ppermute(error[row : row + 1], "lat", up) for row in range(band_rows)]
    rows += [error, lax.ppermute(error, "lat", down)]
    sent = backward(exchange(error_modes), spectrum)
    sent, edge, out_others[0], rows[0], rows[3], tied = after(
        sent, edges(error), out_others[0], rows[0], rows[3], part_index
    )
    base = adjoint_filter(part_index, *rows, *halo(edge), adjoint, cotangent, cot_others)
    received = exchange(sent)
    modes = received if own % 8 == 0 else received[:, : 2 * own]
    tables = bring(tied, apart_t, lambda ref, part: ref.at[1 - own_half(part)])
    grad_send, *shares = final_stage(part_index, lon_total, 2 * own, modes, base, *tables, True)
    if shares:
        grad_send, shares, *out_others = after(grad_send, shares[0], *out_others)
    else:
        shares = jnp.sum(received[:, 2 * own :], axis=0, keepdims=True)
        shares = jnp.broadcast_to(shares, (devices,) + shares.shape[1:])
    grad_other = part_swap(grad_send, 1)
    grad_weight = swap_parts(shares, both_axes).reshape(chans, chans)
    grad_own = final_stage(part_index, lon_total, 2 * own, modes, base, *apart_t, False)
    output = join(part_index, out_own, *out_others)
    grad_input, grad_weight = after(close(part_index, grad_own, grad_other), grad_weight)
    return (output, grad_input, grad_weight)


def solution(mesh):
    in_specs = (
        P("lat", "chan", None),
        P("lat", None, None, None),
        P(),
        P("lat"),
        P("lat"),
        P(),
        P(),
        P("lat", "chan", None),
    )
    out_specs = (P("lat", "chan", None), P("lat", "chan", None), P())
    return jax.shard_map(body, mesh=mesh, in_specs=in_specs, out_specs=out_specs, check_vma=False)
```

```python
import functools
import math

import jax
import jax.numpy as jnp
import ml_dtypes
import numpy as np
from jax import lax
from jax.experimental import pallas as pl
from jax.experimental.pallas import tpu as pltpu
from jax.sharding import PartitionSpec as P

L = 360
M = 256
WIN = 3
HMAX = 2
KLON = 5
POLAR = 720
SPAN = 2 * HMAX + 1
TAPS = 32
EDGES = 16
LANES = 128
MIB = 2**20


highest = lax.Precision.HIGHEST
upper_bound = 2.0**32
lower_factor = 2.0 ** (-32)
log_step = 32.0 * math.log(2.0)

f32 = jnp.float32
bf16 = jnp.bfloat16
VMEM = pltpu.VMEM


@functools.lru_cache(maxsize=None)
def wave_tables(lon_total, own_count):
    orders = np.concatenate([np.arange(0, M, 2), np.arange(1, M, 2)]).reshape(-1, own_count)
    lons = np.arange(lon_total // 2)
    angle = (orders[:, :, None] * lons) % lon_total * (2.0 * np.pi / lon_total)
    table = np.stack([np.cos(angle), -np.sin(angle)], axis=1).reshape(2 * M, lon_total // 2)
    high = table.astype(ml_dtypes.bfloat16)
    low = (table - high.astype(np.float64)).astype(ml_dtypes.bfloat16)
    return high, low


def half_tables(table, depth):
    rows, lons = table.shape
    blocks = table.reshape(rows, 2, lons // 2).transpose(1, 0, 2)
    return np.pad(blocks, ((0, 0), (0, 0), (0, depth - lons // 2)))


def owned_orders(owner, devices):
    half = devices // 2
    return owner % half * (2 * (M // devices)) + owner // half


def grid_tables(lat_total):
    first_row = (POLAR - lat_total) // 2
    colatitude = math.pi * (jnp.arange(lat_total, dtype=f32) + float(first_row)) / POLAR
    quad_weight = 2.0 * math.pi * math.pi / POLAR * jnp.sin(colatitude)
    return (colatitude, quad_weight)


def log_norms(order_count):
    order_index = jnp.arange(order_count, dtype=f32)
    log_terms = jnp.where(
        order_index > 0.0,
        jnp.log((2.0 * order_index + 1.0) / jnp.maximum(2.0 * order_index, 1.0)),
        0.0,
    )
    return -0.5 * math.log(4.0 * math.pi) + 0.5 * jnp.cumsum(log_terms)


def split(x):
    high = x.astype(bf16)
    return high, (x - high.astype(f32)).astype(bf16)


def dot_split(a, b, dims):
    (ah, al), (bh, bl) = split(a), split(b)
    dot = lambda u, v: lax.dot_general(u, v, (dims, ((), ())), preferred_element_type=f32)
    return dot(ah, bh) + (dot(ah, bl) + dot(al, bh))


def cost(us):
    return pl.CostEstimate(flops=int(us * 1e9), bytes_accessed=int(us * 3e6), transcendentals=0)


def call(kernel, out_shape, in_specs, scratch=(), us=1.0, limit=16, out_spaces=None, aliases=None):
    run = pl.pallas_call(
        kernel,
        out_shape=out_shape,
        in_specs=[pl.BlockSpec(memory_space=space) for space, _ in in_specs],
        out_specs=jax.tree.map(
            lambda space: pl.BlockSpec(memory_space=space),
            out_spaces or jax.tree.map(lambda _: VMEM, out_shape),
        ),
        scratch_shapes=list(scratch),
        input_output_aliases=aliases or {},
        compiler_params=pltpu.CompilerParams(vmem_limit_bytes=limit * MIB),
        cost_estimate=cost(us),
    )
    keeps = [keep for _, keep in in_specs]
    return lambda *args: run(
        *[held(x, keep) if keep else x for x, keep in zip(args, keeps, strict=True)]
    )


def held(x, space):
    return pltpu.with_memory_space_constraint(x, space)


def vmem(count):
    return [(VMEM, None)] * count


def resident(count):
    return [(VMEM, VMEM)] * count


def loaded(count):
    return [(VMEM, pltpu.HBM)] * count


def hbm(count):
    return [(pltpu.HBM, pltpu.HBM)] * count


smem = (pltpu.SMEM, None)


def struct(*shape, dtype=f32):
    return jax.ShapeDtypeStruct(shape, dtype)


def near(*shape, dtype=f32):
    return pltpu.VMEM(shape, dtype)


def kept(*shape, dtype=f32):
    return pltpu.HBM(shape, dtype)


def own_half(part):
    return part % 2


def lane_half(x_ref, half):
    return x_ref.at[:, :, pl.ds(pl.multiple_of(half * LANES, LANES), LANES)]


def lon_half(x_ref, half):
    width = x_ref.shape[1] // 2
    return x_ref.at[:, pl.ds(pl.multiple_of(half * width, 8), width), :]


def pair_copies(half, own_hbm, other_hbms, target, sems):
    copies = [pltpu.make_async_copy(lane_half(own_hbm, half), lon_half(target, half), sems.at[0])]
    there = lon_half(target, 1 - half)
    for row, other_hbm in enumerate(other_hbms):
        copies.append(
            pltpu.make_async_copy(other_hbm, there.at[pl.ds(row, 1)], sems.at[1 + row])
        )
    for copy in copies:
        copy.start()
    return copies


def join_kernel(part_ref, field_ref, own_ref, *refs):
    o_ref = refs[-1]
    half = own_half(part_ref[0])
    mine, theirs = (
        pl.ds(pl.multiple_of(place * LANES, LANES), LANES) for place in (half, 1 - half)
    )
    o_ref[:, :, mine] = field_ref[:, :, mine] + own_ref[...]
    for row, other_ref in enumerate(refs[:-1]):
        this = pl.ds(row, 1)
        o_ref[this, :, theirs] = field_ref[this, :, theirs] + other_ref[...]


def join(part, field, own, *others):
    return call(
        join_kernel, kept(*field.shape), [smem] + loaded(2) + vmem(len(others))
    )(part, field, own, *others)


def side_by_side(x):
    return jnp.concatenate([x[0], x[1]], axis=1)


def three(table_high, table_low, high, low):
    dot = lambda u, v: jnp.dot(u, v, preferred_element_type=f32)
    return dot(table_high, high) + (dot(table_high, low) + dot(table_low, high))


def fetches(sources, targets, sems, pieces):
    copies = []
    for index, (source, target) in enumerate(zip(sources, targets, strict=True)):
        tile = source.shape[0] // pieces
        copies.append(
            [
                pltpu.make_async_copy(
                    source.at[pl.ds(piece * tile, tile)],
                    target.at[pl.ds(piece * tile, tile)],
                    sems.at[index, piece],
                )
                for piece in range(pieces)
            ]
        )
    for piece in range(pieces):
        for group in copies:
            group[piece].start()
    return lambda index, piece: copies[index][piece].wait()


def bring_kernel(views, part_ref, *refs):
    sources, targets, sems = refs[: len(views)], refs[len(views) : -1], refs[-1]
    copies = [
        pltpu.make_async_copy(view(source, part_ref[0]), target, sems.at[index])
        for index, (view, source, target) in enumerate(zip(views, sources, targets, strict=True))
    ]
    for copy in copies:
        copy.start()
    for copy in copies:
        copy.wait()


def bring(part, sources, view=None, us=2.0):
    views = [view or (lambda ref, part: ref)] * len(sources)
    shapes = [x.shape[1:] if view else x.shape for x in sources]
    return call(
        functools.partial(bring_kernel, views),
        [near(*shape, dtype=x.dtype) for shape, x in zip(shapes, sources, strict=True)],
        [smem] + hbm(len(sources)),
        [pltpu.SemaphoreType.DMA((len(sources),))],
        us=us,
        limit=8,
    )(part, *sources)


def there_already(index, piece):
    del index, piece


def analyze_rows(x, sign, high_ref, low_ref, wait, store):
    high, low = split(x)
    wait(0, 0)
    wait(1, 0)
    value = three(high_ref[...], low_ref[...], high, low)
    count = value.shape[0] // 2
    store(pl.ds(0, count), value[:count])
    store(pl.ds(count, count), value[count:] * sign)


def compose_rows(modes, sign, thigh_ref, tlow_ref, wait, store, pieces):
    count = modes.shape[0] // 2
    high, low = split(jnp.concatenate([modes[:count], modes[count:] * sign], axis=0))
    tile = thigh_ref.shape[0] // pieces
    for piece in range(pieces):
        rows = pl.ds(piece * tile, tile)
        wait(0, piece)
        wait(1, piece)
        store(rows, three(thigh_ref[rows, :], tlow_ref[rows, :], high, low))


def turn_sign(part):
    return (1 - 2 * (part // 2)).astype(f32)


def analyze_kernel(scale, part_ref, own_hbm, other_ref, high_ref, low_ref, o_ref, field_hbm,
                   x_ref, pair_sem, out_sem):
    part = part_ref[0]
    half = own_half(part)
    mine = pltpu.make_async_copy(lane_half(own_hbm, half), lon_half(x_ref, half), pair_sem)
    mine.start()
    lon_half(x_ref, 1 - half)[...] = other_ref[...]
    mine.wait()
    out = pltpu.make_async_copy(x_ref, field_hbm, out_sem)
    out.start()

    def store(rows, value):
        o_ref[rows, :] = value * scale

    analyze_rows(side_by_side(x_ref[...]), turn_sign(part), high_ref, low_ref, there_already, store)
    out.wait()


def analyze(part, lon_total, own, other, high, low):
    rows, lons, _ = own.shape
    field = (rows, 2 * lons, LANES)
    return call(
        functools.partial(analyze_kernel, 1.0 / lon_total),
        (struct(2 * M, rows * LANES), kept(*field)),
        [smem] + hbm(1) + vmem(1) + resident(2),
        [VMEM(field, f32), pltpu.SemaphoreType.DMA, pltpu.SemaphoreType.DMA],
        us=3.0,
        out_spaces=(VMEM, pltpu.HBM),
    )(part, own, other, high, low)


def grid_kernel(part_ref, s_ref, first_ref, second_ref, thigh_ref, tlow_ref, local_hbm, cot_hbm,
                high_hbm, low_hbm,
                mode_ref, own_hbm, send_first_hbm, send_second_hbm, err_hbm,
                local_ref, cot_ref, spec_ref, out_ref, err_ref,
                high_ref, low_ref, sems, other_sems, out_sems):
    part = part_ref[0]
    half, sign = own_half(part), turn_sign(part)
    others = [
        pltpu.make_async_copy(local_hbm, local_ref, other_sems.at[0]),
        pltpu.make_async_copy(lane_half(cot_hbm, half), lon_half(cot_ref, half), other_sems.at[1]),
    ]
    for copy in others:
        copy.start()
    wait = fetches((high_hbm, low_hbm), (high_ref, low_ref), sems, 1)
    there = lon_half(cot_ref, 1 - half)
    for row, other_ref in enumerate((first_ref, second_ref)):
        there[pl.ds(row, 1)] = other_ref[...]

    def store_spec(rows, value):
        spec_ref[rows, :] = value

    modes = s_ref[...].reshape(thigh_ref.shape[1], s_ref.shape[2])
    compose_rows(modes, sign, thigh_ref, tlow_ref, there_already, store_spec, 1)
    for copy in others:
        copy.wait()
    tile = cot_ref.shape[1] // 6
    for row in range(cot_ref.shape[0]):
        for piece in range(6):
            lons = pl.ds(piece * tile, tile)
            hidden = local_ref[row, lons, :] + spec_ref[lons, pl.ds(row * LANES, LANES)]
            gate = 1.0 / (1.0 + jnp.exp(-hidden))
            out_ref[row, lons, :] = hidden * gate
            err_ref[row, lons, :] = cot_ref[row, lons, :] * (gate * (1.0 + hidden * (1.0 - gate)))
    there = lon_half(out_ref, 1 - half)
    outs = [
        pltpu.make_async_copy(source, target, out_sems.at[index])
        for index, (source, target) in enumerate(
            (
                (err_ref, err_hbm),
                (lon_half(out_ref, half), own_hbm),
                (there.at[pl.ds(0, 1)], send_first_hbm),
                (there.at[pl.ds(1, 1)], send_second_hbm),
            )
        )
    ]
    for copy in outs:
        copy.start()

    def store(rows, value):
        mode_ref[rows, :] = value

    analyze_rows(side_by_side(err_ref[...]), sign, high_ref, low_ref, wait, store)
    for copy in outs:
        copy.wait()


def grid_stage(part, synthesis, local, cotangent, others, tables):
    rows, lons, _ = local.shape
    block = (rows, lons // 2, LANES)
    grid = VMEM(local.shape, f32)
    return call(
        grid_kernel,
        (
            struct(2 * M, rows * LANES),
            kept(*block),
            kept(1, *block[1:]),
            kept(1, *block[1:]),
            kept(*local.shape),
        ),
        [smem] + vmem(3) + resident(2) + hbm(4),
        [grid, grid, VMEM((lons, rows * LANES), f32), grid, grid]
        + [VMEM(table.shape, bf16) for table in tables[:2]]
        + [pltpu.SemaphoreType.DMA((2, 1))]
        + [pltpu.SemaphoreType.DMA((count,)) for count in (2, 4)],
        us=4.0,
        limit=32,
        out_spaces=(VMEM,) + (pltpu.HBM,) * 4,
    )(part, synthesis, *others, *tables[2:], local, cotangent, *tables[:2])


def final_kernel(scale, rows_own, theirs, part_ref, s_ref, base_hbm, *refs):
    part = part_ref[0]
    half = 1 - own_half(part) if theirs else own_half(part)
    if theirs:
        thigh_ref, tlow_ref, o_ref, *shares_ref, base_ref, base_sem = refs
        wait = there_already
        if shares_ref:
            share = jnp.sum(s_ref[:, pl.ds(rows_own, shares_ref[0].shape[1]), :], axis=0)
            shares_ref[0][...] = jnp.broadcast_to(share[None], shares_ref[0].shape)
    else:
        thigh_hbm, tlow_hbm, out_hbm, o_ref, base_ref, thigh_ref, tlow_ref, sems, base_sem = refs
        wait = fetches((thigh_hbm.at[half], tlow_hbm.at[half]), (thigh_ref, tlow_ref), sems, 1)
    base_copy = pltpu.make_async_copy(lon_half(base_hbm, half), base_ref, base_sem)
    base_copy.start()
    modes = s_ref[:, pl.ds(0, rows_own), :].reshape(thigh_ref.shape[1], s_ref.shape[2])
    total = o_ref.shape[1]

    def store(lons, value):
        count = min(lons.size, total - lons.start)
        for row in range(base_ref.shape[0]):
            lanes = slice(row * LANES, (row + 1) * LANES)
            o_ref[row, pl.ds(lons.start, count), :] = scale * value[:count, lanes]

    compose_rows(modes, turn_sign(part), thigh_ref, tlow_ref, wait, store, 1)
    base_copy.wait()
    o_ref[...] = o_ref[...] + base_ref[...]
    if not theirs:
        out = pltpu.make_async_copy(o_ref, lane_half(out_hbm, half), base_sem)
        out.start()
        out.wait()


def final_stage(part, lon_total, rows_own, modes, base, high_t, low_t, theirs):
    rows, lons, _ = base.shape
    block = (rows, lons // 2, LANES)
    scratch = [VMEM(block, f32)]
    out_shape = [struct(*block)]
    share = modes.shape[1] - rows_own
    if share:
        out_shape.append(struct(modes.shape[0], share, modes.shape[2]))
    if not theirs:
        out_shape = kept(rows, lons // 2, 2 * LANES)
        table = VMEM(high_t.shape[1:], bf16)
        scratch = [VMEM(block, f32)] * 2 + [table, table, pltpu.SemaphoreType.DMA((2, 1))]
    return call(
        functools.partial(final_kernel, 1.0 / lon_total, rows_own, theirs),
        out_shape,
        [smem] + vmem(1) + hbm(1) + (resident(2) if theirs else hbm(2)),
        scratch + [pltpu.SemaphoreType.DMA],
        us=2.0,
        out_spaces=None if theirs else pltpu.HBM,
    )(part, modes, base, high_t, low_t)


def close_kernel(part_ref, held_hbm, other_ref, o_hbm, sem):
    del held_hbm
    copy = pltpu.make_async_copy(other_ref, lane_half(o_hbm, 1 - own_half(part_ref[0])), sem)
    copy.start()
    copy.wait()


def close(part, held_half, other):
    return call(
        close_kernel,
        kept(*held_half.shape),
        [smem] + hbm(1) + vmem(1),
        [pltpu.SemaphoreType.DMA],
        us=8.0,
        out_spaces=pltpu.HBM,
        aliases={1: 0},
    )(part, held_half, other)


def filter_sums(refs, edge_refs, coef_ref, finish, sums_ref):
    lons = refs[0].shape[1]
    tile = lons // 18
    sources = [(x_ref, row) for x_ref in refs for row in range(x_ref.shape[0])]
    for row in range(2):
        def add(values, rows, row=row):
            for tap in range(KLON):
                total = values[0] * coef_ref[row, pl.ds(tap, 1), :]
                for offset in range(1, SPAN):
                    total = total + values[offset] * coef_ref[row, pl.ds(offset * KLON + tap, 1), :]
                sums_ref[tap, rows, :] = total

        near = sources[row : row + SPAN]
        edges = [(edge_ref, k) for edge_ref in edge_refs for k in range(2)][row : row + SPAN]
        add([edge_ref[k, pl.ds(8, 8), :] for edge_ref, k in edges], pl.ds(0, 8))
        add([edge_ref[k, pl.ds(0, 8), :] for edge_ref, k in edges], pl.ds(lons + 8, 8))

        @pl.loop(0, 18)
        def _(piece, near=near, add=add):
            start = pl.multiple_of(piece * tile, 8)
            values = [x_ref[k, pl.ds(start, tile), :] for x_ref, k in near]
            add(values, pl.ds(pl.multiple_of(start + 8, 8), tile))

        for piece in range(18):
            total = None
            for tap in range(KLON):
                value = sums_ref[tap, pl.ds(piece * tile + 8 + tap - KLON // 2, tile), :]
                total = value if total is None else total + value
            finish(row, pl.ds(piece * tile, tile), total)


def filter_kernel(prev_ref, own_ref, next_ref, lower_ref, middle_ref, upper_ref, o_ref, adjoint_ref,
                  sums_ref):
    def finish(row, lons, value):
        o_ref[row, lons, :] = value

    taps = pl.ds(EDGES, TAPS)
    coef_refs = [ref.at[:, taps] for ref in (lower_ref, middle_ref, upper_ref)]
    filter_sums(
        (prev_ref, own_ref, next_ref), (lower_ref, middle_ref, upper_ref), coef_refs[1], finish, sums_ref
    )
    adjoint_ref[...] = jnp.zeros_like(adjoint_ref)
    sources = [(c_ref, row) for c_ref in coef_refs for row in range(2)]
    for row in range(2):
        for offset in range(SPAN):
            c_ref, k = sources[row + offset]
            for tap in range(KLON):
                mirrored = (SPAN - 1 - offset) * KLON + KLON - 1 - tap
                adjoint_ref[row, pl.ds(offset * KLON + tap, 1), :] = c_ref[k, pl.ds(mirrored, 1), :]


def adjoint_kernel(part_ref, first_ref, second_ref, own_ref, next_ref, lower_ref, middle_ref, upper_ref, coef_ref,
                   cot_hbm, first_hbm, second_hbm,
                   o_ref, sums_ref, cot_ref, cot_sems):
    copies = pair_copies(
        own_half(part_ref[0]), cot_hbm, (first_hbm, second_hbm), cot_ref, cot_sems
    )
    for copy in copies:
        copy.wait()

    def finish(row, lons, value):
        o_ref[row, lons, :] = cot_ref[row, lons, :] + value

    edge_refs = (lower_ref, middle_ref, upper_ref)
    filter_sums((first_ref, second_ref, own_ref, next_ref), edge_refs, coef_ref, finish, sums_ref)


def local_filter(prev, own, behind, *edges):
    return call(
        filter_kernel,
        (kept(*own.shape), kept(own.shape[0], TAPS, LANES)),
        loaded(3) + vmem(3),
        [VMEM((KLON, own.shape[1] + 16, LANES), f32)],
        us=4.0,
    )(prev, own, behind, *edges)


def adjoint_filter(part, first, second, own, behind, lower, middle, upper, coef, cotangent, others):
    return call(
        adjoint_kernel,
        kept(*own.shape),
        [smem] + loaded(4) + vmem(4) + hbm(3),
        [VMEM((KLON, own.shape[1] + 16, LANES), f32), VMEM(own.shape, f32)]
        + [pltpu.SemaphoreType.DMA((3,))],
        us=4.0,
    )(part, first, second, own, behind, lower, middle, upper, coef, cotangent, *others)


def coupling_kernel(lat_total, first_ref, gain_ref, o_hbm, step_ref, back_ref, start_ref, leg_ref,
                    scale_ref, padded_ref, column_ref, o_ref, out_sems):
    degree_count, chans = gain_ref.shape
    depth = padded_ref.shape[0]
    own = LANES // lat_total
    first_row = float((POLAR - lat_total) // 2)
    lane = lax.broadcasted_iota(jnp.int32, (1, LANES), 1)
    order = 2 * (lane % own) + first_ref[0]
    colatitude = math.pi * ((lane // own).astype(f32) + first_row) / POLAR
    cosine, log_sine = jnp.cos(colatitude), jnp.log(jnp.sin(colatitude))
    k = lax.broadcasted_iota(jnp.int32, (M, LANES), 0)
    k_f = k.astype(f32)
    log_terms = jnp.log((2.0 * k_f + 1.0) / jnp.maximum(2.0 * k_f, 1.0))
    log_norm = -0.5 * math.log(4.0 * math.pi) + 0.5 * jnp.sum(
        jnp.where((k > 0) & (k <= order), log_terms, 0.0), axis=0, keepdims=True
    )
    norm_start = jnp.exp(log_norm)
    degree = lax.broadcasted_iota(jnp.int32, (degree_count, LANES), 0)
    degree_f, order_f = degree.astype(f32), order.astype(f32)
    step = jnp.where(
        degree > order,
        jnp.sqrt(
            jnp.maximum(4.0 * degree_f * degree_f - 1.0, 0.0)
            / jnp.maximum(degree_f * degree_f - order_f * order_f, 1.0)
        ),
        0.0,
    )
    lower = degree_f - 1.0
    back = jnp.sqrt(
        jnp.maximum(lower * lower - order_f * order_f, 0.0) / (4.0 * lower * lower - 1.0)
    )
    step_ref[...] = step * cosine
    back_ref[...] = step * back
    start_ref[...] = jnp.where(degree == order, norm_start, 0.0)
    zeros = jnp.zeros((1, LANES), f32)

    def block(index, carry):
        previous, second, log_scale = carry
        first = pl.multiple_of(index * 8, 8)
        scale_ref[pl.ds(first, 8), :] = jnp.broadcast_to(log_scale, (8, LANES))
        for offset in range(8):
            row = pl.ds(first + offset, 1)
            rest = start_ref[row, :] - back_ref[row, :] * second
            current = step_ref[row, :] * previous + rest
            leg_ref[row, :] = current
            second, previous = previous, current
        too_large = jnp.abs(previous) > upper_bound
        second = jnp.where(too_large, second * lower_factor, second)
        previous = jnp.where(too_large, previous * lower_factor, previous)
        return previous, second, jnp.where(too_large, log_scale + log_step, log_scale)

    lax.fori_loop(0, degree_count // 8, block, (zeros, zeros, order_f * log_sine))
    leg_ref[pl.ds(0, degree_count), :] = leg_ref[pl.ds(0, degree_count), :] * jnp.exp(scale_ref[...])
    rest = depth - degree_count
    leg_ref[pl.ds(degree_count, rest), :] = jnp.zeros((rest, LANES), f32)
    padded_ref[pl.ds(0, degree_count), :] = gain_ref[...]
    padded_ref[pl.ds(degree_count, rest), :] = jnp.zeros((rest, chans), f32)
    column_ref[...] = leg_ref[...].T

    high, low = split(padded_ref[...])
    row = lax.broadcasted_iota(jnp.int32, (LANES, LANES), 0)
    quad = 2.0 * math.pi * math.pi / POLAR * jnp.sin(
        math.pi * ((row // own).astype(f32) + first_row) / POLAR
    )
    weight = quad * jnp.where(row % own + first_ref[0] == 0, 1.0, 2.0)
    weight = jnp.concatenate([weight] * (chans // LANES), axis=1)
    group = lat_total // out_sems.shape[0]
    copies = []
    for piece in range(out_sems.shape[0]):
        both = jnp.concatenate(
            [
                column_ref[...]
                * jnp.concatenate([column_ref[pl.ds(j * own, own), :]] * lat_total, axis=0)
                for j in range(piece * group, (piece + 1) * group)
            ],
            axis=0,
        )
        total = three(*split(both), high, low)
        for j in range(group):
            o_ref[piece * group + j] = (total[j * LANES : (j + 1) * LANES] * weight).reshape(
                lat_total, own, chans
            )
        block_of = pl.ds(piece * group, group)
        copies.append(
            pltpu.make_async_copy(o_ref.at[block_of], o_hbm.at[block_of], out_sems.at[piece])
        )
        copies[-1].start()
    for copy in copies:
        copy.wait()


def coupling(first_order, degree_gain, lat_total):
    degrees, chans = degree_gain.shape
    own = LANES // lat_total
    depth = (degrees + LANES - 1) // LANES * LANES
    table = (lat_total, lat_total, own, chans)
    rows = VMEM((degrees, LANES), f32)
    return call(
        functools.partial(coupling_kernel, lat_total),
        kept(*table),
        [smem] + loaded(1),
        [rows, rows, rows, VMEM((depth, LANES), f32), rows]
        + [VMEM((depth, chans), f32), VMEM((LANES, depth), f32), VMEM(table, f32)]
        + [pltpu.SemaphoreType.DMA((4,))],
        us=6.0,
        out_spaces=pltpu.HBM,
    )(first_order, degree_gain)


def gather_modes(r_ref, write, parts):
    for band in range(r_ref.shape[0] // parts):
        for half in range(2):
            both = r_ref[band * parts + half]
            for other in range(half + 2, parts, 2):
                both = both + r_ref[band * parts + other]
            for row in range(2):
                lanes = slice(row * LANES, (row + 1) * LANES)
                write(2 * band + row, pl.ds(half * LANES, LANES), both[:, lanes])


def scatter_modes(read, s_ref, parts, rows):
    for band in range(s_ref.shape[0] // parts):
        for part in range(parts):
            for row in range(2):
                lanes = pl.ds(row * LANES, LANES)
                value = read(2 * band + row, pl.ds(part % 2 * LANES, LANES))
                s_ref[band * parts + part, pl.ds(0, rows), lanes] = value


def forward_modes_kernel(parts, r_ref, coupling_hbm, w_hbm, x_ref, s_ref, y_ref, z_ref,
                         coupling_ref, w_ref, sems):
    wait_w = fetches((w_hbm,), (w_ref,), sems.at[pl.ds(0, 1)], 2)
    wait = fetches((coupling_hbm,), (coupling_ref,), sems.at[pl.ds(1, 1)], 8)

    def write(j, lanes, value):
        x_ref[j, :, lanes] = value

    gather_modes(r_ref, write, parts)
    lats, rows, chans = x_ref.shape
    own = rows // 2
    for piece in range(2):
        wait_w(0, piece)
    y_ref[...] = dot_split(
        x_ref[...].reshape(lats * rows, chans), w_ref[...], ((1,), (0,))
    ).reshape(lats, rows, chans)
    for piece in range(8):
        wait(0, piece)

        @pl.loop(piece * (lats // 8), (piece + 1) * (lats // 8))
        def _(j):
            totals = [jnp.zeros((own, chans), f32)] * 2
            for other in range(lats):
                factor = coupling_ref[j, other]
                for p in range(2):
                    totals[p] = totals[p] + factor * y_ref[other, pl.ds(p * own, own), :]
            for p in range(2):
                z_ref[j, pl.ds(p * own, own), :] = totals[p]

    scatter_modes(lambda j, lanes: z_ref[j, :, lanes], s_ref, parts, rows)


def backward_modes_kernel(parts, r_ref, coupling_hbm, w_hbm, x_hbm, s_hbm, s_ref, e_ref, v_ref,
                          coupling_ref, w_ref, x_ref, sems, out_sems):
    wait = fetches((coupling_hbm,), (coupling_ref,), sems.at[pl.ds(0, 1)], 8)
    wait_rest = fetches((w_hbm, x_hbm), (w_ref, x_ref), sems.at[pl.ds(1, 2)], 2)

    def write(j, lanes, value):
        e_ref[j, :, lanes] = value

    gather_modes(r_ref, write, parts)
    lats, rows, chans = x_ref.shape
    own = rows // 2
    for piece in range(8):
        wait(0, piece)

    @pl.loop(0, lats)
    def _(j):
        totals = [jnp.zeros((own, chans), f32)] * 2
        for other in range(lats):
            factor = coupling_ref[other, j]
            for p in range(2):
                totals[p] = totals[p] + factor * e_ref[other, pl.ds(p * own, own), :]
        for p in range(2):
            v_ref[j, pl.ds(p * own, own), :] = totals[p]

    for piece in range(2):
        for index in range(2):
            wait_rest(index, piece)
    v = v_ref[...].reshape(lats * rows, chans)
    e_ref[...] = dot_split(v, w_ref[...], ((1,), (1,))).reshape(lats, rows, chans)
    scatter_modes(lambda j, lanes: e_ref[j, :, lanes], s_ref, parts, rows)
    sent = pltpu.make_async_copy(
        s_ref.at[:, pl.ds(0, rows), :], s_hbm.at[:, pl.ds(0, rows), :], out_sems.at[0]
    )
    sent.start()
    weight_part = dot_split(x_ref[...].reshape(lats * rows, chans), v, ((0,), (0,)))
    share = chans // s_ref.shape[0]
    s_ref[:, pl.ds(rows, share), :] = weight_part.reshape(s_ref.shape[0], share, chans)
    shares = pltpu.make_async_copy(
        s_ref.at[:, pl.ds(rows, share), :], s_hbm.at[:, pl.ds(rows, share), :], out_sems.at[1]
    )
    shares.start()
    sent.wait()
    shares.wait()


def legendre_orders(colatitude, orders, log_norm, degree_count):
    cosine = jnp.cos(colatitude)[None, :]
    log_sine = jnp.log(jnp.sin(colatitude))[None, :]
    order_f = orders.astype(f32)[:, None]
    norm_start = jnp.exp(log_norm)[:, None] + jnp.zeros_like(cosine)
    zeros_state = jnp.zeros((orders.shape[0], colatitude.shape[0]), f32)

    def advance(carry, degree):
        previous, second, log_scale = carry
        degree_f = degree.astype(f32)
        step_factor = jnp.where(
            degree > orders[:, None],
            jnp.sqrt(
                jnp.maximum(4.0 * degree_f * degree_f - 1.0, 0.0)
                / jnp.maximum(degree_f * degree_f - order_f * order_f, 1.0)
            ),
            0.0,
        )
        lower_degree = degree_f - 1.0
        back_factor = jnp.sqrt(
            jnp.maximum(lower_degree * lower_degree - order_f * order_f, 0.0)
            / (4.0 * lower_degree * lower_degree - 1.0)
        )
        current = jnp.where(
            degree == orders[:, None],
            norm_start,
            step_factor * (cosine * previous - back_factor * second),
        )
        too_large = jnp.abs(current) > upper_bound
        current = jnp.where(too_large, current * lower_factor, current)
        previous = jnp.where(too_large, previous * lower_factor, previous)
        log_scale = jnp.where(too_large, log_scale + log_step, log_scale)
        return ((current, previous, log_scale), current * jnp.exp(log_scale))

    start_state = (zeros_state, zeros_state, order_f * log_sine)
    _, tables = lax.scan(advance, start_state, jnp.arange(degree_count, dtype=jnp.int32), unroll=8)
    return tables


def plain_gather(received, parts, own):
    bands = received.shape[0] // parts
    blocks = received.reshape(bands, parts // 2, 2, 2, own, 2, LANES).sum(axis=1)
    return blocks.transpose(0, 4, 2, 3, 1, 5).reshape(2 * bands, 2, own, 2 * LANES)


def plain_scatter(modes, parts):
    lats, _, own, _ = modes.shape
    bands = lats // 2
    blocks = modes.reshape(bands, 2, 2, own, 2, LANES).transpose(0, 4, 2, 3, 1, 5)
    blocks = jnp.broadcast_to(blocks[:, None], (bands, parts // 2) + blocks.shape[1:])
    return blocks.reshape(bands * parts, 2 * own, 2 * LANES)


def mode_factors(first_order, own, lat_total, degree_gain):
    if own % 8 == 0 and own * lat_total == LANES and degree_gain.shape[0] % 8 == 0:
        return coupling(first_order[None], degree_gain, lat_total)
    orders = first_order + 2 * jnp.arange(own, dtype=jnp.int32)
    log_norm = jnp.take(log_norms(M), orders)
    return legendre_orders(grid_tables(lat_total)[0], orders, log_norm, degree_gain.shape[0])


def mode_stages(first_order, own, parts, factors, degree_gain, spec_weight):
    if factors.ndim == 4:
        chans = spec_weight.shape[0]
        shape = (factors.shape[0], 2 * own, chans)

        def forward(received):
            return call(
                functools.partial(forward_modes_kernel, parts),
                (kept(*shape), struct(*received.shape)),
                vmem(1) + hbm(2),
                [VMEM(shape, f32), VMEM(shape, f32), VMEM(factors.shape, f32)]
                + [VMEM(spec_weight.shape, f32), pltpu.SemaphoreType.DMA((2, 8))],
                us=2.0,
            )(received, factors, spec_weight)

        def backward(received, spectrum):
            sent = (received.shape[0], 2 * own + chans // received.shape[0], chans)
            return call(
                functools.partial(backward_modes_kernel, parts),
                kept(*sent),
                vmem(1) + hbm(3),
                [VMEM(sent, f32), VMEM(shape, f32), VMEM(shape, f32), VMEM(factors.shape, f32)]
                + [VMEM(spec_weight.shape, f32), VMEM(shape, f32)]
                + [pltpu.SemaphoreType.DMA((3, 8)), pltpu.SemaphoreType.DMA((2,))],
                us=2.0,
                out_spaces=pltpu.HBM,
            )(received, factors, spec_weight, spectrum)

        return forward, backward

    legendre, lat_total = factors, factors.shape[2]
    quad_weight = grid_tables(lat_total)[1]
    orders = first_order + 2 * jnp.arange(own, dtype=jnp.int32)
    order_weight = jnp.where(orders == 0, 1.0, 2.0).astype(f32)[None, None, :, None]
    quad_column = quad_weight[:, None, None, None]
    dot = functools.partial(jnp.einsum, precision=highest)

    def forward(received):
        spectrum = plain_gather(received, parts, own)
        mixed = dot("jpmc,cd->jpmd", spectrum, spec_weight) * quad_column
        degree = dot("lmj,jpmd->lpmd", legendre, mixed) * degree_gain[:, None, None, :]
        synthesis = dot("lmj,lpmd->jpmd", legendre, degree) * order_weight
        return spectrum, plain_scatter(synthesis, parts)

    def backward(received, spectrum):
        error = plain_gather(received, parts, own) * order_weight
        gained = dot("lmj,jpmd->lpmd", legendre, error) * degree_gain[:, None, None, :]
        back = dot("lmj,lpmd->jpmd", legendre, gained) * quad_column
        sent = plain_scatter(dot("jpmd,cd->jpmc", back, spec_weight), parts)
        weight_part = dot("jpmc,jpmd->cd", spectrum, back)
        shares = weight_part.reshape(sent.shape[0], -1, weight_part.shape[1])
        return jnp.concatenate([sent, shares], axis=1)

    return forward, backward


def filter_coefficients(filters, disco_weight, band_start, band_reach):
    coefficient = jnp.einsum("ikrt,kc->irtc", filters, disco_weight, precision=highest)
    window = jnp.arange(WIN, dtype=jnp.int32)
    coefficient = jnp.where(
        (window[None, :] < band_reach[:, None])[:, :, None, None], coefficient, 0.0
    )
    offset = jnp.arange(-HMAX, HMAX + 1, dtype=jnp.int32)
    lands = offset[None, :, None] == band_start[:, None, None] + window[None, None, :]
    by_offset = jnp.sum(
        jnp.where(lands[:, :, :, None, None], coefficient[:, None], 0.0), axis=2
    )
    coef = by_offset.reshape(filters.shape[0], SPAN * KLON, LANES)
    return jnp.pad(coef, ((0, 0), (0, TAPS - SPAN * KLON), (0, 0)))


def swap_parts(x, axis):
    return lax.all_to_all(x, axis, split_axis=0, concat_axis=0, tiled=True)


def after(first, *later):
    return lax.optimization_barrier((first, *later))


def body(
    grid_field, filters, disco_weight, band_start, band_reach, spec_weight, degree_gain, cotangent
):
    band_rows, lon_local, chans = grid_field.shape
    bands, parts = lax.axis_size("lat"), lax.axis_size("chan")
    devices = bands * parts
    lat_total, lon_total = band_rows * bands, lon_local * parts
    own, share = M // devices, chans // devices
    assert band_rows == HMAX and chans == 2 * LANES and parts == 4
    band, part = lax.axis_index("lat"), lax.axis_index("chan")
    me, half, part_index = band * parts + part, part % 2, part[None]
    both_axes = ("lat", "chan")
    high, low = wave_tables(lon_total, own)
    depth = (lon_local + LANES - 1) // LANES * LANES
    apart_t = [
        jnp.asarray(np.ascontiguousarray(half_tables(table, depth).transpose(0, 2, 1)))
        for table in (high, low)
    ]
    high_t, low_t = (jnp.asarray(np.ascontiguousarray(t.T)) for t in (high, low))
    high, low = jnp.asarray(high), jnp.asarray(low)
    up = [(i, i + 1) for i in range(bands - 1)]
    down = [(i + 1, i) for i in range(bands - 1)]

    def halo(x):
        return lax.ppermute(x, "lat", up), x, lax.ppermute(x, "lat", down)

    def part_swap(x, distance):
        return lax.ppermute(x, "chan", [(i, i ^ distance) for i in range(parts)])

    def half_of(x, which):
        return lax.dynamic_slice_in_dim(x, which * LANES, LANES, axis=2)

    def edges(x):
        return part_swap(jnp.concatenate([x[:, :8], x[:, -8:]], axis=1), 2)

    def exchange(modes):
        return swap_parts(modes.reshape(devices, -1, modes.shape[-1]), both_axes)

    outgoing, cotangent, degree_gain, disco_weight, band_start, tied = after(
        half_of(grid_field, 1 - half), cotangent, degree_gain, disco_weight, band_start, part_index
    )
    field_other = part_swap(outgoing, 1)
    first_order = owned_orders(me, devices)
    factors = mode_factors(first_order, own, lat_total, degree_gain)
    cot_out = half_of(cotangent, 1 - half)
    field_other, factors, cot_out = after(field_other, factors, cot_out)
    tables = bring(tied, [high, low])
    modes, field = analyze(part_index, lon_total, grid_field, field_other, *tables)

    modes, field_sent, cot_out, disco_weight, band_start = after(
        modes, field, cot_out, disco_weight, band_start
    )
    mine = lax.dynamic_slice_in_dim(disco_weight, half * LANES, LANES, axis=1)
    coef = filter_coefficients(filters, mine, band_start, band_reach)
    rows = halo(field_sent)
    cot_others = [part_swap(cot_out[row : row + 1], 1) for row in range(band_rows)]
    forward, backward = mode_stages(first_order, own, parts, factors, degree_gain, spec_weight)
    spectrum, synthesis = forward(exchange(modes))
    synthesis, edge, cot_others[0] = after(synthesis, edges(field_sent), cot_others[0])

    local, adjoint = local_filter(*rows, *halo(jnp.concatenate([edge, coef], axis=1)))
    local, tied = after(local, part_index)
    error_modes, out_own, *out_sends, error = grid_stage(
        part_index, exchange(synthesis), local, cotangent, cot_others,
        (high, low, *bring(tied, [high_t, low_t], us=0.1)),
    )

    out_others = [part_swap(x, 1) for x in out_sends]
    rows = [lax.ppermute(error[row : row + 1], "lat", up) for row in range(band_rows)]
    rows += [error, lax.ppermute(error, "lat", down)]
    sent = backward(exchange(error_modes), spectrum)
    sent, edge, out_others[0], rows[0], rows[3], tied = after(
        sent, edges(error), out_others[0], rows[0], rows[3], part_index
    )
    base = adjoint_filter(part_index, *rows, *halo(edge), adjoint, cotangent, cot_others)
    received = exchange(sent)
    modes = received if own % 8 == 0 else received[:, : 2 * own]
    tables = bring(tied, apart_t, lambda ref, part: ref.at[1 - own_half(part)])
    grad_send, *shares = final_stage(part_index, lon_total, 2 * own, modes, base, *tables, True)
    if shares:
        grad_send, shares, *out_others = after(grad_send, shares[0], *out_others)
    else:
        shares = jnp.sum(received[:, 2 * own :], axis=0, keepdims=True)
        shares = jnp.broadcast_to(shares, (devices,) + shares.shape[1:])
    grad_other = part_swap(grad_send, 1)
    grad_weight = swap_parts(shares, both_axes).reshape(chans, chans)
    grad_own = final_stage(part_index, lon_total, 2 * own, modes, base, *apart_t, False)
    output = join(part_index, grid_field, out_own, *out_others)
    grad_input, grad_weight = after(close(part_index, grad_own, grad_other), grad_weight)
    return (output, grad_input, grad_weight)


def solution(mesh):
    in_specs = (
        P("lat", "chan", None),
        P("lat", None, None, None),
        P(),
        P("lat"),
        P("lat"),
        P(),
        P(),
        P("lat", "chan", None),
    )
    out_specs = (P("lat", "chan", None), P("lat", "chan", None), P())
    return jax.shard_map(body, mesh=mesh, in_specs=in_specs, out_specs=out_specs, check_vma=False)
```

```python
import functools
import math

import jax
import jax.numpy as jnp
import ml_dtypes
import numpy as np
from jax import lax
from jax.experimental import pallas as pl
from jax.experimental.pallas import tpu as pltpu
from jax.sharding import PartitionSpec as P

L = 360
M = 256
WIN = 3
HMAX = 2
KLON = 5
POLAR = 720
SPAN = 2 * HMAX + 1
TAPS = 32
EDGES = 16
LANES = 128
MIB = 2**20


highest = lax.Precision.HIGHEST
upper_bound = 2.0**32
lower_factor = 2.0 ** (-32)
log_step = 32.0 * math.log(2.0)

f32 = jnp.float32
bf16 = jnp.bfloat16
VMEM = pltpu.VMEM


@functools.lru_cache(maxsize=None)
def wave_tables(lon_total, own_count):
    orders = np.concatenate([np.arange(0, M, 2), np.arange(1, M, 2)]).reshape(-1, own_count)
    lons = np.arange(lon_total // 2)
    angle = (orders[:, :, None] * lons) % lon_total * (2.0 * np.pi / lon_total)
    table = np.stack([np.cos(angle), -np.sin(angle)], axis=1).reshape(2 * M, lon_total // 2)
    high = table.astype(ml_dtypes.bfloat16)
    low = (table - high.astype(np.float64)).astype(ml_dtypes.bfloat16)
    return high, low


def half_tables(table, depth):
    rows, lons = table.shape
    blocks = table.reshape(rows, 2, lons // 2).transpose(1, 0, 2)
    return np.pad(blocks, ((0, 0), (0, 0), (0, depth - lons // 2)))


def owned_orders(owner, devices):
    half = devices // 2
    return owner % half * (2 * (M // devices)) + owner // half


def grid_tables(lat_total):
    first_row = (POLAR - lat_total) // 2
    colatitude = math.pi * (jnp.arange(lat_total, dtype=f32) + float(first_row)) / POLAR
    quad_weight = 2.0 * math.pi * math.pi / POLAR * jnp.sin(colatitude)
    return (colatitude, quad_weight)


def log_norms(order_count):
    order_index = jnp.arange(order_count, dtype=f32)
    log_terms = jnp.where(
        order_index > 0.0,
        jnp.log((2.0 * order_index + 1.0) / jnp.maximum(2.0 * order_index, 1.0)),
        0.0,
    )
    return -0.5 * math.log(4.0 * math.pi) + 0.5 * jnp.cumsum(log_terms)


def split(x):
    high = x.astype(bf16)
    return high, (x - high.astype(f32)).astype(bf16)


def dot_split(a, b, dims):
    (ah, al), (bh, bl) = split(a), split(b)
    dot = lambda u, v: lax.dot_general(u, v, (dims, ((), ())), preferred_element_type=f32)
    return dot(ah, bh) + (dot(ah, bl) + dot(al, bh))


def cost(us):
    return pl.CostEstimate(flops=int(us * 1e9), bytes_accessed=int(us * 3e6), transcendentals=0)


def call(kernel, out_shape, in_specs, scratch=(), us=1.0, limit=16, out_spaces=None, aliases=None):
    run = pl.pallas_call(
        kernel,
        out_shape=out_shape,
        in_specs=[pl.BlockSpec(memory_space=space) for space, _ in in_specs],
        out_specs=jax.tree.map(
            lambda space: pl.BlockSpec(memory_space=space),
            out_spaces or jax.tree.map(lambda _: VMEM, out_shape),
        ),
        scratch_shapes=list(scratch),
        input_output_aliases=aliases or {},
        compiler_params=pltpu.CompilerParams(vmem_limit_bytes=limit * MIB),
        cost_estimate=cost(us),
    )
    keeps = [keep for _, keep in in_specs]
    return lambda *args: run(
        *[held(x, keep) if keep else x for x, keep in zip(args, keeps, strict=True)]
    )


def held(x, space):
    return pltpu.with_memory_space_constraint(x, space)


def vmem(count):
    return [(VMEM, None)] * count


def resident(count):
    return [(VMEM, VMEM)] * count


def loaded(count):
    return [(VMEM, pltpu.HBM)] * count


def hbm(count):
    return [(pltpu.HBM, pltpu.HBM)] * count


smem = (pltpu.SMEM, None)


def struct(*shape, dtype=f32):
    return jax.ShapeDtypeStruct(shape, dtype)


def near(*shape, dtype=f32):
    return pltpu.VMEM(shape, dtype)


def kept(*shape, dtype=f32):
    return pltpu.HBM(shape, dtype)


def own_half(part):
    return part % 2


def lane_half(x_ref, half):
    return x_ref.at[:, :, pl.ds(pl.multiple_of(half * LANES, LANES), LANES)]


def lon_half(x_ref, half):
    width = x_ref.shape[1] // 2
    return x_ref.at[:, pl.ds(pl.multiple_of(half * width, 8), width), :]


def pair_copies(half, own_hbm, other_hbms, target, sems):
    copies = [pltpu.make_async_copy(lane_half(own_hbm, half), lon_half(target, half), sems.at[0])]
    there = lon_half(target, 1 - half)
    for row, other_hbm in enumerate(other_hbms):
        copies.append(
            pltpu.make_async_copy(other_hbm, there.at[pl.ds(row, 1)], sems.at[1 + row])
        )
    for copy in copies:
        copy.start()
    return copies


def join_kernel(part_ref, field_ref, own_ref, *refs):
    o_ref = refs[-1]
    half = own_half(part_ref[0])
    mine, theirs = (
        pl.ds(pl.multiple_of(place * LANES, LANES), LANES) for place in (half, 1 - half)
    )
    o_ref[:, :, mine] = field_ref[:, :, mine] + own_ref[...]
    for row, other_ref in enumerate(refs[:-1]):
        this = pl.ds(row, 1)
        o_ref[this, :, theirs] = field_ref[this, :, theirs] + other_ref[...]


def join(part, field, own, *others):
    return call(
        join_kernel, kept(*field.shape), [smem] + loaded(2) + vmem(len(others))
    )(part, field, own, *others)


def side_by_side(x):
    return jnp.concatenate([x[0], x[1]], axis=1)


def three(table_high, table_low, high, low):
    dot = lambda u, v: jnp.dot(u, v, preferred_element_type=f32)
    return dot(table_high, high) + (dot(table_high, low) + dot(table_low, high))


def fetches(sources, targets, sems, pieces):
    copies = []
    for index, (source, target) in enumerate(zip(sources, targets, strict=True)):
        tile = source.shape[0] // pieces
        copies.append(
            [
                pltpu.make_async_copy(
                    source.at[pl.ds(piece * tile, tile)],
                    target.at[pl.ds(piece * tile, tile)],
                    sems.at[index, piece],
                )
                for piece in range(pieces)
            ]
        )
    for piece in range(pieces):
        for group in copies:
            group[piece].start()
    return lambda index, piece: copies[index][piece].wait()


def bring_kernel(views, part_ref, *refs):
    sources, targets, sems = refs[: len(views)], refs[len(views) : -1], refs[-1]
    copies = [
        pltpu.make_async_copy(view(source, part_ref[0]), target, sems.at[index])
        for index, (view, source, target) in enumerate(zip(views, sources, targets, strict=True))
    ]
    for copy in copies:
        copy.start()
    for copy in copies:
        copy.wait()


def bring(part, sources, view=None, us=2.0):
    views = [view or (lambda ref, part: ref)] * len(sources)
    shapes = [x.shape[1:] if view else x.shape for x in sources]
    return call(
        functools.partial(bring_kernel, views),
        [near(*shape, dtype=x.dtype) for shape, x in zip(shapes, sources, strict=True)],
        [smem] + hbm(len(sources)),
        [pltpu.SemaphoreType.DMA((len(sources),))],
        us=us,
        limit=8,
    )(part, *sources)


def there_already(index, piece):
    del index, piece


def analyze_rows(x, sign, high_ref, low_ref, wait, store):
    high, low = split(x)
    wait(0, 0)
    wait(1, 0)
    value = three(high_ref[...], low_ref[...], high, low)
    count = value.shape[0] // 2
    store(pl.ds(0, count), value[:count])
    store(pl.ds(count, count), value[count:] * sign)


def compose_rows(modes, sign, thigh_ref, tlow_ref, wait, store, pieces):
    count = modes.shape[0] // 2
    high, low = split(jnp.concatenate([modes[:count], modes[count:] * sign], axis=0))
    tile = thigh_ref.shape[0] // pieces
    for piece in range(pieces):
        rows = pl.ds(piece * tile, tile)
        wait(0, piece)
        wait(1, piece)
        store(rows, three(thigh_ref[rows, :], tlow_ref[rows, :], high, low))


def turn_sign(part):
    return (1 - 2 * (part // 2)).astype(f32)


def analyze_kernel(scale, part_ref, own_hbm, other_ref, high_ref, low_ref, o_ref, field_hbm,
                   x_ref, pair_sem, out_sem):
    part = part_ref[0]
    half = own_half(part)
    mine = pltpu.make_async_copy(lane_half(own_hbm, half), lon_half(x_ref, half), pair_sem)
    mine.start()
    lon_half(x_ref, 1 - half)[...] = other_ref[...]
    mine.wait()
    out = pltpu.make_async_copy(x_ref, field_hbm, out_sem)
    out.start()

    def store(rows, value):
        o_ref[rows, :] = value * scale

    analyze_rows(side_by_side(x_ref[...]), turn_sign(part), high_ref, low_ref, there_already, store)
    out.wait()


def analyze(part, lon_total, own, other, high, low):
    rows, lons, _ = own.shape
    field = (rows, 2 * lons, LANES)
    return call(
        functools.partial(analyze_kernel, 1.0 / lon_total),
        (struct(2 * M, rows * LANES), kept(*field)),
        [smem] + hbm(1) + vmem(1) + resident(2),
        [VMEM(field, f32), pltpu.SemaphoreType.DMA, pltpu.SemaphoreType.DMA],
        us=3.0,
        out_spaces=(VMEM, pltpu.HBM),
    )(part, own, other, high, low)


def grid_kernel(part_ref, s_ref, first_ref, second_ref, thigh_ref, tlow_ref, local_hbm, cot_hbm,
                high_hbm, low_hbm,
                mode_ref, own_hbm, send_first_hbm, send_second_hbm, err_hbm,
                local_ref, cot_ref, spec_ref, out_ref, err_ref,
                high_ref, low_ref, sems, other_sems, out_sems):
    part = part_ref[0]
    half, sign = own_half(part), turn_sign(part)
    others = [
        pltpu.make_async_copy(local_hbm, local_ref, other_sems.at[0]),
        pltpu.make_async_copy(lane_half(cot_hbm, half), lon_half(cot_ref, half), other_sems.at[1]),
    ]
    for copy in others:
        copy.start()
    wait = fetches((high_hbm, low_hbm), (high_ref, low_ref), sems, 1)
    there = lon_half(cot_ref, 1 - half)
    for row, other_ref in enumerate((first_ref, second_ref)):
        there[pl.ds(row, 1)] = other_ref[...]

    def store_spec(rows, value):
        spec_ref[rows, :] = value

    modes = s_ref[...].reshape(thigh_ref.shape[1], s_ref.shape[2])
    compose_rows(modes, sign, thigh_ref, tlow_ref, there_already, store_spec, 1)
    for copy in others:
        copy.wait()
    tile = cot_ref.shape[1] // 6
    for row in range(cot_ref.shape[0]):
        for piece in range(6):
            lons = pl.ds(piece * tile, tile)
            hidden = local_ref[row, lons, :] + spec_ref[lons, pl.ds(row * LANES, LANES)]
            gate = 1.0 / (1.0 + jnp.exp(-hidden))
            out_ref[row, lons, :] = hidden * gate
            err_ref[row, lons, :] = cot_ref[row, lons, :] * (gate * (1.0 + hidden * (1.0 - gate)))
    there = lon_half(out_ref, 1 - half)
    outs = [
        pltpu.make_async_copy(source, target, out_sems.at[index])
        for index, (source, target) in enumerate(
            (
                (err_ref, err_hbm),
                (lon_half(out_ref, half), own_hbm),
                (there.at[pl.ds(0, 1)], send_first_hbm),
                (there.at[pl.ds(1, 1)], send_second_hbm),
            )
        )
    ]
    for copy in outs:
        copy.start()

    def store(rows, value):
        mode_ref[rows, :] = value

    analyze_rows(side_by_side(err_ref[...]), sign, high_ref, low_ref, wait, store)
    for copy in outs:
        copy.wait()


def grid_stage(part, synthesis, local, cotangent, others, tables):
    rows, lons, _ = local.shape
    block = (rows, lons // 2, LANES)
    grid = VMEM(local.shape, f32)
    return call(
        grid_kernel,
        (
            struct(2 * M, rows * LANES),
            kept(*block),
            kept(1, *block[1:]),
            kept(1, *block[1:]),
            kept(*local.shape),
        ),
        [smem] + vmem(3) + resident(2) + hbm(4),
        [grid, grid, VMEM((lons, rows * LANES), f32), grid, grid]
        + [VMEM(table.shape, bf16) for table in tables[:2]]
        + [pltpu.SemaphoreType.DMA((2, 1))]
        + [pltpu.SemaphoreType.DMA((count,)) for count in (2, 4)],
        us=4.0,
        limit=32,
        out_spaces=(VMEM,) + (pltpu.HBM,) * 4,
    )(part, synthesis, *others, *tables[2:], local, cotangent, *tables[:2])


def final_kernel(scale, rows_own, theirs, part_ref, s_ref, base_hbm, *refs):
    part = part_ref[0]
    half = 1 - own_half(part) if theirs else own_half(part)
    if theirs:
        thigh_ref, tlow_ref, o_ref, *shares_ref, base_ref, base_sem = refs
        wait = there_already
        if shares_ref:
            share = jnp.sum(s_ref[:, pl.ds(rows_own, shares_ref[0].shape[1]), :], axis=0)
            shares_ref[0][...] = jnp.broadcast_to(share[None], shares_ref[0].shape)
    else:
        thigh_hbm, tlow_hbm, out_hbm, o_ref, base_ref, thigh_ref, tlow_ref, sems, base_sem = refs
        wait = fetches((thigh_hbm.at[half], tlow_hbm.at[half]), (thigh_ref, tlow_ref), sems, 1)
    base_copy = pltpu.make_async_copy(lon_half(base_hbm, half), base_ref, base_sem)
    base_copy.start()
    modes = s_ref[:, pl.ds(0, rows_own), :].reshape(thigh_ref.shape[1], s_ref.shape[2])
    total = o_ref.shape[1]

    def store(lons, value):
        count = min(lons.size, total - lons.start)
        for row in range(base_ref.shape[0]):
            lanes = slice(row * LANES, (row + 1) * LANES)
            o_ref[row, pl.ds(lons.start, count), :] = scale * value[:count, lanes]

    compose_rows(modes, turn_sign(part), thigh_ref, tlow_ref, wait, store, 1)
    base_copy.wait()
    o_ref[...] = o_ref[...] + base_ref[...]
    if not theirs:
        out = pltpu.make_async_copy(o_ref, lane_half(out_hbm, half), base_sem)
        out.start()
        out.wait()


def final_stage(part, lon_total, rows_own, modes, base, high_t, low_t, theirs):
    rows, lons, _ = base.shape
    block = (rows, lons // 2, LANES)
    scratch = [VMEM(block, f32)]
    out_shape = [struct(*block)]
    share = modes.shape[1] - rows_own
    if share:
        out_shape.append(struct(modes.shape[0], share, modes.shape[2]))
    if not theirs:
        out_shape = kept(rows, lons // 2, 2 * LANES)
        table = VMEM(high_t.shape[1:], bf16)
        scratch = [VMEM(block, f32)] * 2 + [table, table, pltpu.SemaphoreType.DMA((2, 1))]
    return call(
        functools.partial(final_kernel, 1.0 / lon_total, rows_own, theirs),
        out_shape,
        [smem] + vmem(1) + hbm(1) + (resident(2) if theirs else hbm(2)),
        scratch + [pltpu.SemaphoreType.DMA],
        us=2.0,
        out_spaces=None if theirs else pltpu.HBM,
    )(part, modes, base, high_t, low_t)


def close_kernel(part_ref, held_hbm, other_ref, o_hbm, sem):
    del held_hbm
    copy = pltpu.make_async_copy(other_ref, lane_half(o_hbm, 1 - own_half(part_ref[0])), sem)
    copy.start()
    copy.wait()


def close(part, held_half, other):
    return call(
        close_kernel,
        kept(*held_half.shape),
        [smem] + hbm(1) + vmem(1),
        [pltpu.SemaphoreType.DMA],
        us=8.0,
        out_spaces=pltpu.HBM,
        aliases={1: 0},
    )(part, held_half, other)


def filter_sums(refs, edge_refs, coef_ref, finish, sums_ref):
    lons = refs[0].shape[1]
    tile = lons // 18
    sources = [(x_ref, row) for x_ref in refs for row in range(x_ref.shape[0])]
    for row in range(2):
        def add(values, rows, row=row):
            for tap in range(KLON):
                total = values[0] * coef_ref[row, pl.ds(tap, 1), :]
                for offset in range(1, SPAN):
                    total = total + values[offset] * coef_ref[row, pl.ds(offset * KLON + tap, 1), :]
                sums_ref[tap, rows, :] = total

        near = sources[row : row + SPAN]
        edges = [(edge_ref, k) for edge_ref in edge_refs for k in range(2)][row : row + SPAN]
        add([edge_ref[k, pl.ds(8, 8), :] for edge_ref, k in edges], pl.ds(0, 8))
        add([edge_ref[k, pl.ds(0, 8), :] for edge_ref, k in edges], pl.ds(lons + 8, 8))

        @pl.loop(0, 18)
        def _(piece, near=near, add=add):
            start = pl.multiple_of(piece * tile, 8)
            values = [x_ref[k, pl.ds(start, tile), :] for x_ref, k in near]
            add(values, pl.ds(pl.multiple_of(start + 8, 8), tile))

        for piece in range(18):
            total = None
            for tap in range(KLON):
                value = sums_ref[tap, pl.ds(piece * tile + 8 + tap - KLON // 2, tile), :]
                total = value if total is None else total + value
            finish(row, pl.ds(piece * tile, tile), total)


def filter_kernel(prev_ref, own_ref, next_ref, lower_ref, middle_ref, upper_ref, o_ref, adjoint_ref,
                  sums_ref):
    def finish(row, lons, value):
        o_ref[row, lons, :] = value

    taps = pl.ds(EDGES, TAPS)
    coef_refs = [ref.at[:, taps] for ref in (lower_ref, middle_ref, upper_ref)]
    filter_sums(
        (prev_ref, own_ref, next_ref), (lower_ref, middle_ref, upper_ref), coef_refs[1], finish, sums_ref
    )
    adjoint_ref[...] = jnp.zeros_like(adjoint_ref)
    sources = [(c_ref, row) for c_ref in coef_refs for row in range(2)]
    for row in range(2):
        for offset in range(SPAN):
            c_ref, k = sources[row + offset]
            for tap in range(KLON):
                mirrored = (SPAN - 1 - offset) * KLON + KLON - 1 - tap
                adjoint_ref[row, pl.ds(offset * KLON + tap, 1), :] = c_ref[k, pl.ds(mirrored, 1), :]


def adjoint_kernel(part_ref, first_ref, second_ref, own_ref, next_ref, lower_ref, middle_ref, upper_ref, coef_ref,
                   cot_hbm, first_hbm, second_hbm,
                   o_ref, sums_ref, cot_ref, cot_sems):
    copies = pair_copies(
        own_half(part_ref[0]), cot_hbm, (first_hbm, second_hbm), cot_ref, cot_sems
    )
    for copy in copies:
        copy.wait()

    def finish(row, lons, value):
        o_ref[row, lons, :] = cot_ref[row, lons, :] + value

    edge_refs = (lower_ref, middle_ref, upper_ref)
    filter_sums((first_ref, second_ref, own_ref, next_ref), edge_refs, coef_ref, finish, sums_ref)


def local_filter(prev, own, behind, *edges):
    return call(
        filter_kernel,
        (kept(*own.shape), kept(own.shape[0], TAPS, LANES)),
        loaded(3) + vmem(3),
        [VMEM((KLON, own.shape[1] + 16, LANES), f32)],
        us=4.0,
    )(prev, own, behind, *edges)


def adjoint_filter(part, first, second, own, behind, lower, middle, upper, coef, cotangent, others):
    return call(
        adjoint_kernel,
        kept(*own.shape),
        [smem] + loaded(4) + vmem(4) + hbm(3),
        [VMEM((KLON, own.shape[1] + 16, LANES), f32), VMEM(own.shape, f32)]
        + [pltpu.SemaphoreType.DMA((3,))],
        us=4.0,
    )(part, first, second, own, behind, lower, middle, upper, coef, cotangent, *others)


def coupling_kernel(lat_total, first_ref, gain_ref, o_hbm, step_ref, back_ref, start_ref, leg_ref,
                    scale_ref, padded_ref, column_ref, o_ref, out_sems):
    degree_count, chans = gain_ref.shape
    depth = padded_ref.shape[0]
    own = LANES // lat_total
    first_row = float((POLAR - lat_total) // 2)
    lane = lax.broadcasted_iota(jnp.int32, (1, LANES), 1)
    order = 2 * (lane % own) + first_ref[0]
    colatitude = math.pi * ((lane // own).astype(f32) + first_row) / POLAR
    cosine, log_sine = jnp.cos(colatitude), jnp.log(jnp.sin(colatitude))
    k = lax.broadcasted_iota(jnp.int32, (M, LANES), 0)
    k_f = k.astype(f32)
    log_terms = jnp.log((2.0 * k_f + 1.0) / jnp.maximum(2.0 * k_f, 1.0))
    log_norm = -0.5 * math.log(4.0 * math.pi) + 0.5 * jnp.sum(
        jnp.where((k > 0) & (k <= order), log_terms, 0.0), axis=0, keepdims=True
    )
    norm_start = jnp.exp(log_norm)
    degree = lax.broadcasted_iota(jnp.int32, (degree_count, LANES), 0)
    degree_f, order_f = degree.astype(f32), order.astype(f32)
    step = jnp.where(
        degree > order,
        jnp.sqrt(
            jnp.maximum(4.0 * degree_f * degree_f - 1.0, 0.0)
            / jnp.maximum(degree_f * degree_f - order_f * order_f, 1.0)
        ),
        0.0,
    )
    lower = degree_f - 1.0
    back = jnp.sqrt(
        jnp.maximum(lower * lower - order_f * order_f, 0.0) / (4.0 * lower * lower - 1.0)
    )
    step_ref[...] = step * cosine
    back_ref[...] = step * back
    start_ref[...] = jnp.where(degree == order, norm_start, 0.0)
    zeros = jnp.zeros((1, LANES), f32)

    def block(index, carry):
        previous, second, log_scale = carry
        first = pl.multiple_of(index * 8, 8)
        scale_ref[pl.ds(first, 8), :] = jnp.broadcast_to(log_scale, (8, LANES))
        for offset in range(8):
            row = pl.ds(first + offset, 1)
            rest = start_ref[row, :] - back_ref[row, :] * second
            current = step_ref[row, :] * previous + rest
            leg_ref[row, :] = current
            second, previous = previous, current
        too_large = jnp.abs(previous) > upper_bound
        second = jnp.where(too_large, second * lower_factor, second)
        previous = jnp.where(too_large, previous * lower_factor, previous)
        return previous, second, jnp.where(too_large, log_scale + log_step, log_scale)

    lax.fori_loop(0, degree_count // 8, block, (zeros, zeros, order_f * log_sine))
    leg_ref[pl.ds(0, degree_count), :] = leg_ref[pl.ds(0, degree_count), :] * jnp.exp(scale_ref[...])
    rest = depth - degree_count
    leg_ref[pl.ds(degree_count, rest), :] = jnp.zeros((rest, LANES), f32)
    padded_ref[pl.ds(0, degree_count), :] = gain_ref[...]
    padded_ref[pl.ds(degree_count, rest), :] = jnp.zeros((rest, chans), f32)
    column_ref[...] = leg_ref[...].T

    high, low = split(padded_ref[...])
    row = lax.broadcasted_iota(jnp.int32, (LANES, LANES), 0)
    quad = 2.0 * math.pi * math.pi / POLAR * jnp.sin(
        math.pi * ((row // own).astype(f32) + first_row) / POLAR
    )
    weight = quad * jnp.where(row % own + first_ref[0] == 0, 1.0, 2.0)
    weight = jnp.concatenate([weight] * (chans // LANES), axis=1)
    group = lat_total // out_sems.shape[0]
    copies = []
    for piece in range(out_sems.shape[0]):
        both = jnp.concatenate(
            [
                column_ref[...]
                * jnp.concatenate([column_ref[pl.ds(j * own, own), :]] * lat_total, axis=0)
                for j in range(piece * group, (piece + 1) * group)
            ],
            axis=0,
        )
        total = three(*split(both), high, low)
        for j in range(group):
            o_ref[piece * group + j] = (total[j * LANES : (j + 1) * LANES] * weight).reshape(
                lat_total, own, chans
            )
        block_of = pl.ds(piece * group, group)
        copies.append(
            pltpu.make_async_copy(o_ref.at[block_of], o_hbm.at[block_of], out_sems.at[piece])
        )
        copies[-1].start()
    for copy in copies:
        copy.wait()


def coupling(first_order, degree_gain, lat_total):
    degrees, chans = degree_gain.shape
    own = LANES // lat_total
    depth = (degrees + LANES - 1) // LANES * LANES
    table = (lat_total, lat_total, own, chans)
    rows = VMEM((degrees, LANES), f32)
    return call(
        functools.partial(coupling_kernel, lat_total),
        kept(*table),
        [smem] + loaded(1),
        [rows, rows, rows, VMEM((depth, LANES), f32), rows]
        + [VMEM((depth, chans), f32), VMEM((LANES, depth), f32), VMEM(table, f32)]
        + [pltpu.SemaphoreType.DMA((4,))],
        us=6.0,
        out_spaces=pltpu.HBM,
    )(first_order, degree_gain)


def gather_modes(r_ref, write, parts):
    for band in range(r_ref.shape[0] // parts):
        for half in range(2):
            both = r_ref[band * parts + half]
            for other in range(half + 2, parts, 2):
                both = both + r_ref[band * parts + other]
            for row in range(2):
                lanes = slice(row * LANES, (row + 1) * LANES)
                write(2 * band + row, pl.ds(half * LANES, LANES), both[:, lanes])


def scatter_modes(read, s_ref, parts, rows):
    for band in range(s_ref.shape[0] // parts):
        for part in range(parts):
            for row in range(2):
                lanes = pl.ds(row * LANES, LANES)
                value = read(2 * band + row, pl.ds(part % 2 * LANES, LANES))
                s_ref[band * parts + part, pl.ds(0, rows), lanes] = value


def forward_modes_kernel(parts, r_ref, w_ref, coupling_hbm, x_ref, s_ref, y_ref, z_ref,
                         coupling_ref, sems):
    wait = fetches((coupling_hbm,), (coupling_ref,), sems, 8)

    def write(j, lanes, value):
        x_ref[j, :, lanes] = value

    gather_modes(r_ref, write, parts)
    lats, rows, chans = x_ref.shape
    own = rows // 2
    y_ref[...] = dot_split(
        x_ref[...].reshape(lats * rows, chans), w_ref[...], ((1,), (0,))
    ).reshape(lats, rows, chans)
    for piece in range(8):
        wait(0, piece)

        @pl.loop(piece * (lats // 8), (piece + 1) * (lats // 8))
        def _(j):
            totals = [jnp.zeros((own, chans), f32)] * 2
            for other in range(lats):
                factor = coupling_ref[j, other]
                for p in range(2):
                    totals[p] = totals[p] + factor * y_ref[other, pl.ds(p * own, own), :]
            for p in range(2):
                z_ref[j, pl.ds(p * own, own), :] = totals[p]

    scatter_modes(lambda j, lanes: z_ref[j, :, lanes], s_ref, parts, rows)


def backward_modes_kernel(parts, r_ref, coupling_hbm, w_hbm, x_hbm, s_hbm, s_ref, e_ref, v_ref,
                          coupling_ref, w_ref, x_ref, sems, out_sems):
    wait = fetches((coupling_hbm,), (coupling_ref,), sems.at[pl.ds(0, 1)], 8)
    wait_rest = fetches((w_hbm, x_hbm), (w_ref, x_ref), sems.at[pl.ds(1, 2)], 2)

    def write(j, lanes, value):
        e_ref[j, :, lanes] = value

    gather_modes(r_ref, write, parts)
    lats, rows, chans = x_ref.shape
    own = rows // 2
    for piece in range(8):
        wait(0, piece)

    @pl.loop(0, lats)
    def _(j):
        totals = [jnp.zeros((own, chans), f32)] * 2
        for other in range(lats):
            factor = coupling_ref[other, j]
            for p in range(2):
                totals[p] = totals[p] + factor * e_ref[other, pl.ds(p * own, own), :]
        for p in range(2):
            v_ref[j, pl.ds(p * own, own), :] = totals[p]

    for piece in range(2):
        for index in range(2):
            wait_rest(index, piece)
    v = v_ref[...].reshape(lats * rows, chans)
    e_ref[...] = dot_split(v, w_ref[...], ((1,), (1,))).reshape(lats, rows, chans)
    scatter_modes(lambda j, lanes: e_ref[j, :, lanes], s_ref, parts, rows)
    sent = pltpu.make_async_copy(
        s_ref.at[:, pl.ds(0, rows), :], s_hbm.at[:, pl.ds(0, rows), :], out_sems.at[0]
    )
    sent.start()
    weight_part = dot_split(x_ref[...].reshape(lats * rows, chans), v, ((0,), (0,)))
    share = chans // s_ref.shape[0]
    s_ref[:, pl.ds(rows, share), :] = weight_part.reshape(s_ref.shape[0], share, chans)
    shares = pltpu.make_async_copy(
        s_ref.at[:, pl.ds(rows, share), :], s_hbm.at[:, pl.ds(rows, share), :], out_sems.at[1]
    )
    shares.start()
    sent.wait()
    shares.wait()


def legendre_orders(colatitude, orders, log_norm, degree_count):
    cosine = jnp.cos(colatitude)[None, :]
    log_sine = jnp.log(jnp.sin(colatitude))[None, :]
    order_f = orders.astype(f32)[:, None]
    norm_start = jnp.exp(log_norm)[:, None] + jnp.zeros_like(cosine)
    zeros_state = jnp.zeros((orders.shape[0], colatitude.shape[0]), f32)

    def advance(carry, degree):
        previous, second, log_scale = carry
        degree_f = degree.astype(f32)
        step_factor = jnp.where(
            degree > orders[:, None],
            jnp.sqrt(
                jnp.maximum(4.0 * degree_f * degree_f - 1.0, 0.0)
                / jnp.maximum(degree_f * degree_f - order_f * order_f, 1.0)
            ),
            0.0,
        )
        lower_degree = degree_f - 1.0
        back_factor = jnp.sqrt(
            jnp.maximum(lower_degree * lower_degree - order_f * order_f, 0.0)
            / (4.0 * lower_degree * lower_degree - 1.0)
        )
        current = jnp.where(
            degree == orders[:, None],
            norm_start,
            step_factor * (cosine * previous - back_factor * second),
        )
        too_large = jnp.abs(current) > upper_bound
        current = jnp.where(too_large, current * lower_factor, current)
        previous = jnp.where(too_large, previous * lower_factor, previous)
        log_scale = jnp.where(too_large, log_scale + log_step, log_scale)
        return ((current, previous, log_scale), current * jnp.exp(log_scale))

    start_state = (zeros_state, zeros_state, order_f * log_sine)
    _, tables = lax.scan(advance, start_state, jnp.arange(degree_count, dtype=jnp.int32), unroll=8)
    return tables


def plain_gather(received, parts, own):
    bands = received.shape[0] // parts
    blocks = received.reshape(bands, parts // 2, 2, 2, own, 2, LANES).sum(axis=1)
    return blocks.transpose(0, 4, 2, 3, 1, 5).reshape(2 * bands, 2, own, 2 * LANES)


def plain_scatter(modes, parts):
    lats, _, own, _ = modes.shape
    bands = lats // 2
    blocks = modes.reshape(bands, 2, 2, own, 2, LANES).transpose(0, 4, 2, 3, 1, 5)
    blocks = jnp.broadcast_to(blocks[:, None], (bands, parts // 2) + blocks.shape[1:])
    return blocks.reshape(bands * parts, 2 * own, 2 * LANES)


def mode_factors(first_order, own, lat_total, degree_gain):
    if own % 8 == 0 and own * lat_total == LANES and degree_gain.shape[0] % 8 == 0:
        return coupling(first_order[None], degree_gain, lat_total)
    orders = first_order + 2 * jnp.arange(own, dtype=jnp.int32)
    log_norm = jnp.take(log_norms(M), orders)
    return legendre_orders(grid_tables(lat_total)[0], orders, log_norm, degree_gain.shape[0])


def mode_stages(first_order, own, parts, factors, degree_gain, spec_weight):
    if factors.ndim == 4:
        chans = spec_weight.shape[0]
        shape = (factors.shape[0], 2 * own, chans)

        def forward(received, tied):
            (weight,) = bring(tied, [spec_weight], us=0.1)
            return call(
                functools.partial(forward_modes_kernel, parts),
                (kept(*shape), struct(*received.shape)),
                vmem(1) + resident(1) + hbm(1),
                [VMEM(shape, f32), VMEM(shape, f32), VMEM(factors.shape, f32)]
                + [pltpu.SemaphoreType.DMA((1, 8))],
                us=2.0,
            )(received, weight, factors)

        def backward(received, spectrum):
            sent = (received.shape[0], 2 * own + chans // received.shape[0], chans)
            return call(
                functools.partial(backward_modes_kernel, parts),
                kept(*sent),
                vmem(1) + hbm(3),
                [VMEM(sent, f32), VMEM(shape, f32), VMEM(shape, f32), VMEM(factors.shape, f32)]
                + [VMEM(spec_weight.shape, f32), VMEM(shape, f32)]
                + [pltpu.SemaphoreType.DMA((3, 8)), pltpu.SemaphoreType.DMA((2,))],
                us=2.0,
                out_spaces=pltpu.HBM,
            )(received, factors, spec_weight, spectrum)

        return forward, backward

    legendre, lat_total = factors, factors.shape[2]
    quad_weight = grid_tables(lat_total)[1]
    orders = first_order + 2 * jnp.arange(own, dtype=jnp.int32)
    order_weight = jnp.where(orders == 0, 1.0, 2.0).astype(f32)[None, None, :, None]
    quad_column = quad_weight[:, None, None, None]
    dot = functools.partial(jnp.einsum, precision=highest)

    def forward(received, tied):
        del tied
        spectrum = plain_gather(received, parts, own)
        mixed = dot("jpmc,cd->jpmd", spectrum, spec_weight) * quad_column
        degree = dot("lmj,jpmd->lpmd", legendre, mixed) * degree_gain[:, None, None, :]
        synthesis = dot("lmj,lpmd->jpmd", legendre, degree) * order_weight
        return spectrum, plain_scatter(synthesis, parts)

    def backward(received, spectrum):
        error = plain_gather(received, parts, own) * order_weight
        gained = dot("lmj,jpmd->lpmd", legendre, error) * degree_gain[:, None, None, :]
        back = dot("lmj,lpmd->jpmd", legendre, gained) * quad_column
        sent = plain_scatter(dot("jpmd,cd->jpmc", back, spec_weight), parts)
        weight_part = dot("jpmc,jpmd->cd", spectrum, back)
        shares = weight_part.reshape(sent.shape[0], -1, weight_part.shape[1])
        return jnp.concatenate([sent, shares], axis=1)

    return forward, backward


def filter_coefficients(filters, disco_weight, band_start, band_reach):
    coefficient = jnp.einsum("ikrt,kc->irtc", filters, disco_weight, precision=highest)
    window = jnp.arange(WIN, dtype=jnp.int32)
    coefficient = jnp.where(
        (window[None, :] < band_reach[:, None])[:, :, None, None], coefficient, 0.0
    )
    offset = jnp.arange(-HMAX, HMAX + 1, dtype=jnp.int32)
    lands = offset[None, :, None] == band_start[:, None, None] + window[None, None, :]
    by_offset = jnp.sum(
        jnp.where(lands[:, :, :, None, None], coefficient[:, None], 0.0), axis=2
    )
    coef = by_offset.reshape(filters.shape[0], SPAN * KLON, LANES)
    return jnp.pad(coef, ((0, 0), (0, TAPS - SPAN * KLON), (0, 0)))


def swap_parts(x, axis):
    return lax.all_to_all(x, axis, split_axis=0, concat_axis=0, tiled=True)


def after(first, *later):
    return lax.optimization_barrier((first, *later))


def body(
    grid_field, filters, disco_weight, band_start, band_reach, spec_weight, degree_gain, cotangent
):
    band_rows, lon_local, chans = grid_field.shape
    bands, parts = lax.axis_size("lat"), lax.axis_size("chan")
    devices = bands * parts
    lat_total, lon_total = band_rows * bands, lon_local * parts
    own, share = M // devices, chans // devices
    assert band_rows == HMAX and chans == 2 * LANES and parts == 4
    band, part = lax.axis_index("lat"), lax.axis_index("chan")
    me, half, part_index = band * parts + part, part % 2, part[None]
    both_axes = ("lat", "chan")
    high, low = wave_tables(lon_total, own)
    depth = (lon_local + LANES - 1) // LANES * LANES
    apart_t = [
        jnp.asarray(np.ascontiguousarray(half_tables(table, depth).transpose(0, 2, 1)))
        for table in (high, low)
    ]
    high_t, low_t = (jnp.asarray(np.ascontiguousarray(t.T)) for t in (high, low))
    high, low = jnp.asarray(high), jnp.asarray(low)
    up = [(i, i + 1) for i in range(bands - 1)]
    down = [(i + 1, i) for i in range(bands - 1)]

    def halo(x):
        return lax.ppermute(x, "lat", up), x, lax.ppermute(x, "lat", down)

    def part_swap(x, distance):
        return lax.ppermute(x, "chan", [(i, i ^ distance) for i in range(parts)])

    def half_of(x, which):
        return lax.dynamic_slice_in_dim(x, which * LANES, LANES, axis=2)

    def edges(x):
        return part_swap(jnp.concatenate([x[:, :8], x[:, -8:]], axis=1), 2)

    def exchange(modes):
        return swap_parts(modes.reshape(devices, -1, modes.shape[-1]), both_axes)

    outgoing, cotangent, degree_gain, disco_weight, band_start, tied = after(
        half_of(grid_field, 1 - half), cotangent, degree_gain, disco_weight, band_start, part_index
    )
    field_other = part_swap(outgoing, 1)
    first_order = owned_orders(me, devices)
    factors = mode_factors(first_order, own, lat_total, degree_gain)
    cot_out = half_of(cotangent, 1 - half)
    field_other, factors, cot_out = after(field_other, factors, cot_out)
    tables = bring(tied, [high, low])
    modes, field = analyze(part_index, lon_total, grid_field, field_other, *tables)

    modes, field_sent, cot_out, disco_weight, band_start, tied = after(
        modes, field, cot_out, disco_weight, band_start, part_index
    )
    mine = lax.dynamic_slice_in_dim(disco_weight, half * LANES, LANES, axis=1)
    coef = filter_coefficients(filters, mine, band_start, band_reach)
    rows = halo(field_sent)
    cot_others = [part_swap(cot_out[row : row + 1], 1) for row in range(band_rows)]
    forward, backward = mode_stages(first_order, own, parts, factors, degree_gain, spec_weight)
    spectrum, synthesis = forward(exchange(modes), tied)
    synthesis, edge, cot_others[0] = after(synthesis, edges(field_sent), cot_others[0])

    local, adjoint = local_filter(*rows, *halo(jnp.concatenate([edge, coef], axis=1)))
    local, tied = after(local, part_index)
    error_modes, out_own, *out_sends, error = grid_stage(
        part_index, exchange(synthesis), local, cotangent, cot_others,
        (high, low, *bring(tied, [high_t, low_t], us=0.1)),
    )

    out_others = [part_swap(x, 1) for x in out_sends]
    rows = [lax.ppermute(error[row : row + 1], "lat", up) for row in range(band_rows)]
    rows += [error, lax.ppermute(error, "lat", down)]
    sent = backward(exchange(error_modes), spectrum)
    sent, edge, out_others[0], rows[0], rows[3], tied = after(
        sent, edges(error), out_others[0], rows[0], rows[3], part_index
    )
    base = adjoint_filter(part_index, *rows, *halo(edge), adjoint, cotangent, cot_others)
    received = exchange(sent)
    modes = received if own % 8 == 0 else received[:, : 2 * own]
    tables = bring(tied, apart_t, lambda ref, part: ref.at[1 - own_half(part)])
    grad_send, *shares = final_stage(part_index, lon_total, 2 * own, modes, base, *tables, True)
    if shares:
        grad_send, shares, *out_others = after(grad_send, shares[0], *out_others)
    else:
        shares = jnp.sum(received[:, 2 * own :], axis=0, keepdims=True)
        shares = jnp.broadcast_to(shares, (devices,) + shares.shape[1:])
    grad_other = part_swap(grad_send, 1)
    grad_weight = swap_parts(shares, both_axes).reshape(chans, chans)
    grad_own = final_stage(part_index, lon_total, 2 * own, modes, base, *apart_t, False)
    output = join(part_index, grid_field, out_own, *out_others)
    grad_input, grad_weight = after(close(part_index, grad_own, grad_other), grad_weight)
    return (output, grad_input, grad_weight)


def solution(mesh):
    in_specs = (
        P("lat", "chan", None),
        P("lat", None, None, None),
        P(),
        P("lat"),
        P("lat"),
        P(),
        P(),
        P("lat", "chan", None),
    )
    out_specs = (P("lat", "chan", None), P("lat", "chan", None), P())
    return jax.shard_map(body, mesh=mesh, in_specs=in_specs, out_specs=out_specs, check_vma=False)
```

```python
import functools
import math

import jax
import jax.numpy as jnp
import ml_dtypes
import numpy as np
from jax import lax
from jax.experimental import pallas as pl
from jax.experimental.pallas import tpu as pltpu
from jax.sharding import PartitionSpec as P

L = 360
M = 256
WIN = 3
HMAX = 2
KLON = 5
POLAR = 720
SPAN = 2 * HMAX + 1
TAPS = 32
EDGES = 16
LANES = 128
MIB = 2**20


highest = lax.Precision.HIGHEST
upper_bound = 2.0**32
lower_factor = 2.0 ** (-32)
log_step = 32.0 * math.log(2.0)

f32 = jnp.float32
bf16 = jnp.bfloat16
VMEM = pltpu.VMEM


@functools.lru_cache(maxsize=None)
def wave_tables(lon_total, own_count):
    orders = np.concatenate([np.arange(0, M, 2), np.arange(1, M, 2)]).reshape(-1, own_count)
    lons = np.arange(lon_total // 2)
    angle = (orders[:, :, None] * lons) % lon_total * (2.0 * np.pi / lon_total)
    table = np.stack([np.cos(angle), -np.sin(angle)], axis=1).reshape(2 * M, lon_total // 2)
    high = table.astype(ml_dtypes.bfloat16)
    low = (table - high.astype(np.float64)).astype(ml_dtypes.bfloat16)
    return high, low


def half_tables(table, depth):
    rows, lons = table.shape
    blocks = table.reshape(rows, 2, lons // 2).transpose(1, 0, 2)
    return np.pad(blocks, ((0, 0), (0, 0), (0, depth - lons // 2)))


def owned_orders(owner, devices):
    half = devices // 2
    return owner % half * (2 * (M // devices)) + owner // half


def grid_tables(lat_total):
    first_row = (POLAR - lat_total) // 2
    colatitude = math.pi * (jnp.arange(lat_total, dtype=f32) + float(first_row)) / POLAR
    quad_weight = 2.0 * math.pi * math.pi / POLAR * jnp.sin(colatitude)
    return (colatitude, quad_weight)


def log_norms(order_count):
    order_index = jnp.arange(order_count, dtype=f32)
    log_terms = jnp.where(
        order_index > 0.0,
        jnp.log((2.0 * order_index + 1.0) / jnp.maximum(2.0 * order_index, 1.0)),
        0.0,
    )
    return -0.5 * math.log(4.0 * math.pi) + 0.5 * jnp.cumsum(log_terms)


def split(x):
    high = x.astype(bf16)
    return high, (x - high.astype(f32)).astype(bf16)


def dot_split(a, b, dims):
    (ah, al), (bh, bl) = split(a), split(b)
    dot = lambda u, v: lax.dot_general(u, v, (dims, ((), ())), preferred_element_type=f32)
    return dot(ah, bh) + (dot(ah, bl) + dot(al, bh))


def cost(us):
    return pl.CostEstimate(flops=int(us * 1e9), bytes_accessed=int(us * 3e6), transcendentals=0)


def call(kernel, out_shape, in_specs, scratch=(), us=1.0, limit=16, out_spaces=None, aliases=None):
    run = pl.pallas_call(
        kernel,
        out_shape=out_shape,
        in_specs=[pl.BlockSpec(memory_space=space) for space, _ in in_specs],
        out_specs=jax.tree.map(
            lambda space: pl.BlockSpec(memory_space=space),
            out_spaces or jax.tree.map(lambda _: VMEM, out_shape),
        ),
        scratch_shapes=list(scratch),
        input_output_aliases=aliases or {},
        compiler_params=pltpu.CompilerParams(vmem_limit_bytes=limit * MIB),
        cost_estimate=cost(us),
    )
    keeps = [keep for _, keep in in_specs]
    return lambda *args: run(
        *[held(x, keep) if keep else x for x, keep in zip(args, keeps, strict=True)]
    )


def held(x, space):
    return pltpu.with_memory_space_constraint(x, space)


def vmem(count):
    return [(VMEM, None)] * count


def resident(count):
    return [(VMEM, VMEM)] * count


def loaded(count):
    return [(VMEM, pltpu.HBM)] * count


def hbm(count):
    return [(pltpu.HBM, pltpu.HBM)] * count


smem = (pltpu.SMEM, None)


def struct(*shape, dtype=f32):
    return jax.ShapeDtypeStruct(shape, dtype)


def near(*shape, dtype=f32):
    return pltpu.VMEM(shape, dtype)


def kept(*shape, dtype=f32):
    return pltpu.HBM(shape, dtype)


def own_half(part):
    return part % 2


def lane_half(x_ref, half):
    return x_ref.at[:, :, pl.ds(pl.multiple_of(half * LANES, LANES), LANES)]


def lon_half(x_ref, half):
    width = x_ref.shape[1] // 2
    return x_ref.at[:, pl.ds(pl.multiple_of(half * width, 8), width), :]


def pair_copies(half, own_hbm, other_hbms, target, sems):
    copies = [pltpu.make_async_copy(lane_half(own_hbm, half), lon_half(target, half), sems.at[0])]
    there = lon_half(target, 1 - half)
    for row, other_hbm in enumerate(other_hbms):
        copies.append(
            pltpu.make_async_copy(other_hbm, there.at[pl.ds(row, 1)], sems.at[1 + row])
        )
    for copy in copies:
        copy.start()
    return copies


def join_kernel(part_ref, field_ref, own_ref, *refs):
    o_ref = refs[-1]
    half = own_half(part_ref[0])
    mine, theirs = (
        pl.ds(pl.multiple_of(place * LANES, LANES), LANES) for place in (half, 1 - half)
    )
    o_ref[:, :, mine] = field_ref[:, :, mine] + own_ref[...]
    for row, other_ref in enumerate(refs[:-1]):
        this = pl.ds(row, 1)
        o_ref[this, :, theirs] = field_ref[this, :, theirs] + other_ref[...]


def join(part, field, own, *others):
    return call(
        join_kernel, kept(*field.shape), [smem] + loaded(2) + vmem(len(others))
    )(part, field, own, *others)


def side_by_side(x):
    return jnp.concatenate([x[0], x[1]], axis=1)


def three(table_high, table_low, high, low):
    dot = lambda u, v: jnp.dot(u, v, preferred_element_type=f32)
    return dot(table_high, high) + (dot(table_high, low) + dot(table_low, high))


def fetches(sources, targets, sems, pieces):
    copies = []
    for index, (source, target) in enumerate(zip(sources, targets, strict=True)):
        tile = source.shape[0] // pieces
        copies.append(
            [
                pltpu.make_async_copy(
                    source.at[pl.ds(piece * tile, tile)],
                    target.at[pl.ds(piece * tile, tile)],
                    sems.at[index, piece],
                )
                for piece in range(pieces)
            ]
        )
    for piece in range(pieces):
        for group in copies:
            group[piece].start()
    return lambda index, piece: copies[index][piece].wait()


def bring_kernel(views, part_ref, *refs):
    sources, targets, sems = refs[: len(views)], refs[len(views) : -1], refs[-1]
    copies = [
        pltpu.make_async_copy(view(source, part_ref[0]), target, sems.at[index])
        for index, (view, source, target) in enumerate(zip(views, sources, targets, strict=True))
    ]
    for copy in copies:
        copy.start()
    for copy in copies:
        copy.wait()


def bring(part, sources, view=None, us=2.0, first=0):
    views = [view or (lambda ref, part: ref)] * len(sources)
    shapes = [x.shape[1:] if view else x.shape for x in sources]
    if first:
        views[0] = lambda ref, part: ref.at[pl.ds(0, first)]
        shapes[0] = (first, *shapes[0][1:])
    return call(
        functools.partial(bring_kernel, views),
        [near(*shape, dtype=x.dtype) for shape, x in zip(shapes, sources, strict=True)],
        [smem] + hbm(len(sources)),
        [pltpu.SemaphoreType.DMA((len(sources),))],
        us=us,
        limit=8,
    )(part, *sources)


def there_already(index, piece):
    del index, piece


def analyze_rows(x, sign, high_ref, low_ref, wait, store):
    high, low = split(x)
    wait(0, 0)
    wait(1, 0)
    value = three(high_ref[...], low_ref[...], high, low)
    count = value.shape[0] // 2
    store(pl.ds(0, count), value[:count])
    store(pl.ds(count, count), value[count:] * sign)


def compose_rows(modes, sign, thigh_ref, tlow_ref, wait, store, pieces):
    count = modes.shape[0] // 2
    high, low = split(jnp.concatenate([modes[:count], modes[count:] * sign], axis=0))
    tile = thigh_ref.shape[0] // pieces
    for piece in range(pieces):
        rows = pl.ds(piece * tile, tile)
        wait(0, piece)
        wait(1, piece)
        store(rows, three(thigh_ref[rows, :], tlow_ref[rows, :], high, low))


def turn_sign(part):
    return (1 - 2 * (part // 2)).astype(f32)


def analyze_kernel(scale, part_ref, own_hbm, other_ref, high_ref, low_ref, o_ref, field_hbm,
                   x_ref, pair_sem, out_sem):
    part = part_ref[0]
    half = own_half(part)
    mine = pltpu.make_async_copy(lane_half(own_hbm, half), lon_half(x_ref, half), pair_sem)
    mine.start()
    lon_half(x_ref, 1 - half)[...] = other_ref[...]
    mine.wait()
    out = pltpu.make_async_copy(x_ref, field_hbm, out_sem)
    out.start()

    def store(rows, value):
        o_ref[rows, :] = value * scale

    analyze_rows(side_by_side(x_ref[...]), turn_sign(part), high_ref, low_ref, there_already, store)
    out.wait()


def analyze(part, lon_total, own, other, high, low):
    rows, lons, _ = own.shape
    field = (rows, 2 * lons, LANES)
    return call(
        functools.partial(analyze_kernel, 1.0 / lon_total),
        (struct(2 * M, rows * LANES), kept(*field)),
        [smem] + hbm(1) + vmem(1) + resident(2),
        [VMEM(field, f32), pltpu.SemaphoreType.DMA, pltpu.SemaphoreType.DMA],
        us=3.0,
        out_spaces=(VMEM, pltpu.HBM),
    )(part, own, other, high, low)


def grid_kernel(part_ref, s_ref, first_ref, second_ref, thigh_ref, tlow_ref, local_ref, cot_hbm,
                high_hbm, low_hbm,
                mode_ref, own_hbm, send_first_hbm, send_second_hbm, err_hbm,
                cot_ref, spec_ref, out_ref, err_ref,
                high_ref, low_ref, sems, other_sems, out_sems):
    part = part_ref[0]
    half, sign = own_half(part), turn_sign(part)
    others = [
        pltpu.make_async_copy(lane_half(cot_hbm, half), lon_half(cot_ref, half), other_sems.at[0]),
    ]
    for copy in others:
        copy.start()
    wait = fetches((high_hbm, low_hbm), (high_ref, low_ref), sems, 1)
    there = lon_half(cot_ref, 1 - half)
    for row, other_ref in enumerate((first_ref, second_ref)):
        there[pl.ds(row, 1)] = other_ref[...]

    def store_spec(rows, value):
        spec_ref[rows, :] = value

    modes = s_ref[...].reshape(thigh_ref.shape[1], s_ref.shape[2])
    compose_rows(modes, sign, thigh_ref, tlow_ref, there_already, store_spec, 1)
    for copy in others:
        copy.wait()
    tile = cot_ref.shape[1] // 6
    for row in range(cot_ref.shape[0]):
        for piece in range(6):
            lons = pl.ds(piece * tile, tile)
            hidden = local_ref[row, lons, :] + spec_ref[lons, pl.ds(row * LANES, LANES)]
            gate = 1.0 / (1.0 + jnp.exp(-hidden))
            out_ref[row, lons, :] = hidden * gate
            err_ref[row, lons, :] = cot_ref[row, lons, :] * (gate * (1.0 + hidden * (1.0 - gate)))
    there = lon_half(out_ref, 1 - half)
    outs = [
        pltpu.make_async_copy(source, target, out_sems.at[index])
        for index, (source, target) in enumerate(
            (
                (err_ref, err_hbm),
                (lon_half(out_ref, half), own_hbm),
                (there.at[pl.ds(0, 1)], send_first_hbm),
                (there.at[pl.ds(1, 1)], send_second_hbm),
            )
        )
    ]
    for copy in outs:
        copy.start()

    def store(rows, value):
        mode_ref[rows, :] = value

    analyze_rows(side_by_side(err_ref[...]), sign, high_ref, low_ref, wait, store)
    for copy in outs:
        copy.wait()


def grid_stage(part, synthesis, local, cotangent, others, tables):
    rows, lons, _ = local.shape
    block = (rows, lons // 2, LANES)
    grid = VMEM(local.shape, f32)
    return call(
        grid_kernel,
        (
            struct(2 * M, rows * LANES),
            kept(*block),
            kept(1, *block[1:]),
            kept(1, *block[1:]),
            kept(*local.shape),
        ),
        [smem] + vmem(3) + resident(3) + hbm(3),
        [grid, VMEM((lons, rows * LANES), f32), grid, grid]
        + [VMEM(table.shape, bf16) for table in tables[:2]]
        + [pltpu.SemaphoreType.DMA((2, 1))]
        + [pltpu.SemaphoreType.DMA((count,)) for count in (1, 4)],
        us=4.0,
        limit=32,
        out_spaces=(VMEM,) + (pltpu.HBM,) * 4,
    )(part, synthesis, *others, *tables[2:], local, cotangent, *tables[:2])


def final_kernel(scale, rows_own, theirs, part_ref, s_ref, base_hbm, *refs):
    part = part_ref[0]
    half = 1 - own_half(part) if theirs else own_half(part)
    if theirs:
        thigh_ref, tlow_ref, o_ref, *shares_ref, base_ref, base_sem = refs
        wait = there_already
        if shares_ref:
            share = jnp.sum(s_ref[:, pl.ds(rows_own, shares_ref[0].shape[1]), :], axis=0)
            shares_ref[0][...] = jnp.broadcast_to(share[None], shares_ref[0].shape)
    else:
        thigh_hbm, tlow_hbm, out_hbm, o_ref, base_ref, thigh_ref, tlow_ref, sems, base_sem = refs
        wait = fetches((thigh_hbm.at[half], tlow_hbm.at[half]), (thigh_ref, tlow_ref), sems, 1)
    base_copy = pltpu.make_async_copy(lon_half(base_hbm, half), base_ref, base_sem)
    base_copy.start()
    modes = s_ref[:, pl.ds(0, rows_own), :].reshape(thigh_ref.shape[1], s_ref.shape[2])
    total = o_ref.shape[1]

    def store(lons, value):
        count = min(lons.size, total - lons.start)
        for row in range(base_ref.shape[0]):
            lanes = slice(row * LANES, (row + 1) * LANES)
            o_ref[row, pl.ds(lons.start, count), :] = scale * value[:count, lanes]

    compose_rows(modes, turn_sign(part), thigh_ref, tlow_ref, wait, store, 1)
    base_copy.wait()
    o_ref[...] = o_ref[...] + base_ref[...]
    if not theirs:
        out = pltpu.make_async_copy(o_ref, lane_half(out_hbm, half), base_sem)
        out.start()
        out.wait()


def final_stage(part, lon_total, rows_own, modes, base, high_t, low_t, theirs):
    rows, lons, _ = base.shape
    block = (rows, lons // 2, LANES)
    scratch = [VMEM(block, f32)]
    out_shape = [struct(*block)]
    share = modes.shape[1] - rows_own
    if share:
        out_shape.append(struct(modes.shape[0], share, modes.shape[2]))
    if not theirs:
        out_shape = kept(rows, lons // 2, 2 * LANES)
        table = VMEM(high_t.shape[1:], bf16)
        scratch = [VMEM(block, f32)] * 2 + [table, table, pltpu.SemaphoreType.DMA((2, 1))]
    return call(
        functools.partial(final_kernel, 1.0 / lon_total, rows_own, theirs),
        out_shape,
        [smem] + vmem(1) + hbm(1) + (resident(2) if theirs else hbm(2)),
        scratch + [pltpu.SemaphoreType.DMA],
        us=2.0,
        out_spaces=None if theirs else pltpu.HBM,
    )(part, modes, base, high_t, low_t)


def close_kernel(part_ref, held_hbm, other_ref, o_hbm, sem):
    del held_hbm
    copy = pltpu.make_async_copy(other_ref, lane_half(o_hbm, 1 - own_half(part_ref[0])), sem)
    copy.start()
    copy.wait()


def close(part, held_half, other):
    return call(
        close_kernel,
        kept(*held_half.shape),
        [smem] + hbm(1) + vmem(1),
        [pltpu.SemaphoreType.DMA],
        us=8.0,
        out_spaces=pltpu.HBM,
        aliases={1: 0},
    )(part, held_half, other)


def filter_sums(refs, edge_refs, coef_ref, finish, sums_ref):
    lons = refs[0].shape[1]
    tile = lons // 18
    sources = [(x_ref, row) for x_ref in refs for row in range(x_ref.shape[0])]
    for row in range(2):
        def add(values, rows, row=row):
            for tap in range(KLON):
                total = values[0] * coef_ref[row, pl.ds(tap, 1), :]
                for offset in range(1, SPAN):
                    total = total + values[offset] * coef_ref[row, pl.ds(offset * KLON + tap, 1), :]
                sums_ref[tap, rows, :] = total

        near = sources[row : row + SPAN]
        edges = [(edge_ref, k) for edge_ref in edge_refs for k in range(2)][row : row + SPAN]
        add([edge_ref[k, pl.ds(8, 8), :] for edge_ref, k in edges], pl.ds(0, 8))
        add([edge_ref[k, pl.ds(0, 8), :] for edge_ref, k in edges], pl.ds(lons + 8, 8))

        @pl.loop(0, 18)
        def _(piece, near=near, add=add):
            start = pl.multiple_of(piece * tile, 8)
            values = [x_ref[k, pl.ds(start, tile), :] for x_ref, k in near]
            add(values, pl.ds(pl.multiple_of(start + 8, 8), tile))

        for piece in range(18):
            total = None
            for tap in range(KLON):
                value = sums_ref[tap, pl.ds(piece * tile + 8 + tap - KLON // 2, tile), :]
                total = value if total is None else total + value
            finish(row, pl.ds(piece * tile, tile), total)


def filter_kernel(prev_ref, own_ref, next_ref, lower_ref, middle_ref, upper_ref, o_ref, adjoint_ref,
                  sums_ref):
    def finish(row, lons, value):
        o_ref[row, lons, :] = value

    taps = pl.ds(EDGES, TAPS)
    coef_refs = [ref.at[:, taps] for ref in (lower_ref, middle_ref, upper_ref)]
    filter_sums(
        (prev_ref, own_ref, next_ref), (lower_ref, middle_ref, upper_ref), coef_refs[1], finish, sums_ref
    )
    adjoint_ref[...] = jnp.zeros_like(adjoint_ref)
    sources = [(c_ref, row) for c_ref in coef_refs for row in range(2)]
    for row in range(2):
        for offset in range(SPAN):
            c_ref, k = sources[row + offset]
            for tap in range(KLON):
                mirrored = (SPAN - 1 - offset) * KLON + KLON - 1 - tap
                adjoint_ref[row, pl.ds(offset * KLON + tap, 1), :] = c_ref[k, pl.ds(mirrored, 1), :]


def adjoint_kernel(part_ref, first_ref, second_ref, own_ref, next_ref, lower_ref, middle_ref, upper_ref, coef_ref,
                   cot_hbm, first_hbm, second_hbm,
                   o_ref, sums_ref, cot_ref, cot_sems):
    copies = pair_copies(
        own_half(part_ref[0]), cot_hbm, (first_hbm, second_hbm), cot_ref, cot_sems
    )
    for copy in copies:
        copy.wait()

    def finish(row, lons, value):
        o_ref[row, lons, :] = cot_ref[row, lons, :] + value

    edge_refs = (lower_ref, middle_ref, upper_ref)
    filter_sums((first_ref, second_ref, own_ref, next_ref), edge_refs, coef_ref, finish, sums_ref)


def local_filter(prev, own, behind, *edges):
    return call(
        filter_kernel,
        (near(*own.shape), kept(own.shape[0], TAPS, LANES)),
        loaded(3) + vmem(3),
        [VMEM((KLON, own.shape[1] + 16, LANES), f32)],
        us=4.0,
    )(prev, own, behind, *edges)


def adjoint_filter(part, first, second, own, behind, lower, middle, upper, coef, cotangent, others):
    return call(
        adjoint_kernel,
        kept(*own.shape),
        [smem] + loaded(4) + vmem(4) + hbm(3),
        [VMEM((KLON, own.shape[1] + 16, LANES), f32), VMEM(own.shape, f32)]
        + [pltpu.SemaphoreType.DMA((3,))],
        us=4.0,
    )(part, first, second, own, behind, lower, middle, upper, coef, cotangent, *others)


def coupling_kernel(lat_total, first_ref, gain_ref, o_hbm, step_ref, back_ref, start_ref, leg_ref,
                    scale_ref, padded_ref, column_ref, o_ref, out_sems):
    degree_count, chans = gain_ref.shape
    depth = padded_ref.shape[0]
    own = LANES // lat_total
    first_row = float((POLAR - lat_total) // 2)
    lane = lax.broadcasted_iota(jnp.int32, (1, LANES), 1)
    order = 2 * (lane % own) + first_ref[0]
    colatitude = math.pi * ((lane // own).astype(f32) + first_row) / POLAR
    cosine, log_sine = jnp.cos(colatitude), jnp.log(jnp.sin(colatitude))
    k = lax.broadcasted_iota(jnp.int32, (M, LANES), 0)
    k_f = k.astype(f32)
    log_terms = jnp.log((2.0 * k_f + 1.0) / jnp.maximum(2.0 * k_f, 1.0))
    log_norm = -0.5 * math.log(4.0 * math.pi) + 0.5 * jnp.sum(
        jnp.where((k > 0) & (k <= order), log_terms, 0.0), axis=0, keepdims=True
    )
    norm_start = jnp.exp(log_norm)
    degree = lax.broadcasted_iota(jnp.int32, (degree_count, LANES), 0)
    degree_f, order_f = degree.astype(f32), order.astype(f32)
    step = jnp.where(
        degree > order,
        jnp.sqrt(
            jnp.maximum(4.0 * degree_f * degree_f - 1.0, 0.0)
            / jnp.maximum(degree_f * degree_f - order_f * order_f, 1.0)
        ),
        0.0,
    )
    lower = degree_f - 1.0
    back = jnp.sqrt(
        jnp.maximum(lower * lower - order_f * order_f, 0.0) / (4.0 * lower * lower - 1.0)
    )
    step_ref[...] = step * cosine
    back_ref[...] = step * back
    start_ref[...] = jnp.where(degree == order, norm_start, 0.0)
    zeros = jnp.zeros((1, LANES), f32)

    def block(index, carry):
        previous, second, log_scale = carry
        first = pl.multiple_of(index * 8, 8)
        scale_ref[pl.ds(first, 8), :] = jnp.broadcast_to(log_scale, (8, LANES))
        for offset in range(8):
            row = pl.ds(first + offset, 1)
            rest = start_ref[row, :] - back_ref[row, :] * second
            current = step_ref[row, :] * previous + rest
            leg_ref[row, :] = current
            second, previous = previous, current
        too_large = jnp.abs(previous) > upper_bound
        second = jnp.where(too_large, second * lower_factor, second)
        previous = jnp.where(too_large, previous * lower_factor, previous)
        return previous, second, jnp.where(too_large, log_scale + log_step, log_scale)

    lax.fori_loop(0, degree_count // 8, block, (zeros, zeros, order_f * log_sine))
    leg_ref[pl.ds(0, degree_count), :] = leg_ref[pl.ds(0, degree_count), :] * jnp.exp(scale_ref[...])
    rest = depth - degree_count
    leg_ref[pl.ds(degree_count, rest), :] = jnp.zeros((rest, LANES), f32)
    padded_ref[pl.ds(0, degree_count), :] = gain_ref[...]
    padded_ref[pl.ds(degree_count, rest), :] = jnp.zeros((rest, chans), f32)
    column_ref[...] = leg_ref[...].T

    high, low = split(padded_ref[...])
    row = lax.broadcasted_iota(jnp.int32, (LANES, LANES), 0)
    quad = 2.0 * math.pi * math.pi / POLAR * jnp.sin(
        math.pi * ((row // own).astype(f32) + first_row) / POLAR
    )
    weight = quad * jnp.where(row % own + first_ref[0] == 0, 1.0, 2.0)
    weight = jnp.concatenate([weight] * (chans // LANES), axis=1)
    group = lat_total // out_sems.shape[0]
    copies = []
    for piece in range(out_sems.shape[0]):
        both = jnp.concatenate(
            [
                column_ref[...]
                * jnp.concatenate([column_ref[pl.ds(j * own, own), :]] * lat_total, axis=0)
                for j in range(piece * group, (piece + 1) * group)
            ],
            axis=0,
        )
        total = three(*split(both), high, low)
        for j in range(group):
            o_ref[piece * group + j] = (total[j * LANES : (j + 1) * LANES] * weight).reshape(
                lat_total, own, chans
            )
        block_of = pl.ds(piece * group, group)
        copies.append(
            pltpu.make_async_copy(o_ref.at[block_of], o_hbm.at[block_of], out_sems.at[piece])
        )
        copies[-1].start()
    for copy in copies:
        copy.wait()


def coupling(first_order, degree_gain, lat_total):
    degrees, chans = degree_gain.shape
    own = LANES // lat_total
    depth = (degrees + LANES - 1) // LANES * LANES
    table = (lat_total, lat_total, own, chans)
    rows = VMEM((degrees, LANES), f32)
    return call(
        functools.partial(coupling_kernel, lat_total),
        kept(*table),
        [smem] + loaded(1),
        [rows, rows, rows, VMEM((depth, LANES), f32), rows]
        + [VMEM((depth, chans), f32), VMEM((LANES, depth), f32), VMEM(table, f32)]
        + [pltpu.SemaphoreType.DMA((4,))],
        us=6.0,
        out_spaces=pltpu.HBM,
    )(first_order, degree_gain)


def gather_modes(r_ref, write, parts):
    for band in range(r_ref.shape[0] // parts):
        for half in range(2):
            both = r_ref[band * parts + half]
            for other in range(half + 2, parts, 2):
                both = both + r_ref[band * parts + other]
            for row in range(2):
                lanes = slice(row * LANES, (row + 1) * LANES)
                write(2 * band + row, pl.ds(half * LANES, LANES), both[:, lanes])


def scatter_modes(read, s_ref, parts, rows):
    for band in range(s_ref.shape[0] // parts):
        for part in range(parts):
            for row in range(2):
                lanes = pl.ds(row * LANES, LANES)
                value = read(2 * band + row, pl.ds(part % 2 * LANES, LANES))
                s_ref[band * parts + part, pl.ds(0, rows), lanes] = value


def forward_modes_kernel(parts, r_ref, w_ref, coupling_hbm, x_ref, s_ref, y_ref, z_ref,
                         coupling_ref, sems):
    wait = fetches((coupling_hbm,), (coupling_ref,), sems, 8)

    def write(j, lanes, value):
        x_ref[j, :, lanes] = value

    gather_modes(r_ref, write, parts)
    lats, rows, chans = x_ref.shape
    own = rows // 2
    y_ref[...] = dot_split(
        x_ref[...].reshape(lats * rows, chans), w_ref[...], ((1,), (0,))
    ).reshape(lats, rows, chans)
    for piece in range(8):
        wait(0, piece)

        @pl.loop(piece * (lats // 8), (piece + 1) * (lats // 8))
        def _(j):
            totals = [jnp.zeros((own, chans), f32)] * 2
            for other in range(lats):
                factor = coupling_ref[j, other]
                for p in range(2):
                    totals[p] = totals[p] + factor * y_ref[other, pl.ds(p * own, own), :]
            for p in range(2):
                z_ref[j, pl.ds(p * own, own), :] = totals[p]

    scatter_modes(lambda j, lanes: z_ref[j, :, lanes], s_ref, parts, rows)


def backward_modes_kernel(parts, r_ref, early_ref, w_ref, x_ref, coupling_hbm, s_hbm,
                          s_ref, e_ref, v_ref, coupling_ref, sems, out_sems):
    early = early_ref.shape[0]
    wait = fetches((coupling_hbm.at[pl.ds(early, coupling_ref.shape[0])],), (coupling_ref,), sems, 4)

    def write(j, lanes, value):
        e_ref[j, :, lanes] = value

    gather_modes(r_ref, write, parts)
    lats, rows, chans = x_ref.shape
    own = rows // 2
    for piece in range(4):
        wait(0, piece)

    @pl.loop(0, lats)
    def _(j):
        totals = [jnp.zeros((own, chans), f32)] * 2
        for other in range(lats):
            factor = early_ref[other, j] if other < early else coupling_ref[other - early, j]
            for p in range(2):
                totals[p] = totals[p] + factor * e_ref[other, pl.ds(p * own, own), :]
        for p in range(2):
            v_ref[j, pl.ds(p * own, own), :] = totals[p]

    v = v_ref[...].reshape(lats * rows, chans)
    e_ref[...] = dot_split(v, w_ref[...], ((1,), (1,))).reshape(lats, rows, chans)
    scatter_modes(lambda j, lanes: e_ref[j, :, lanes], s_ref, parts, rows)
    sent = pltpu.make_async_copy(
        s_ref.at[:, pl.ds(0, rows), :], s_hbm.at[:, pl.ds(0, rows), :], out_sems.at[0]
    )
    sent.start()
    weight_part = dot_split(x_ref[...].reshape(lats * rows, chans), v, ((0,), (0,)))
    share = chans // s_ref.shape[0]
    s_ref[:, pl.ds(rows, share), :] = weight_part.reshape(s_ref.shape[0], share, chans)
    shares = pltpu.make_async_copy(
        s_ref.at[:, pl.ds(rows, share), :], s_hbm.at[:, pl.ds(rows, share), :], out_sems.at[1]
    )
    shares.start()
    sent.wait()
    shares.wait()


def legendre_orders(colatitude, orders, log_norm, degree_count):
    cosine = jnp.cos(colatitude)[None, :]
    log_sine = jnp.log(jnp.sin(colatitude))[None, :]
    order_f = orders.astype(f32)[:, None]
    norm_start = jnp.exp(log_norm)[:, None] + jnp.zeros_like(cosine)
    zeros_state = jnp.zeros((orders.shape[0], colatitude.shape[0]), f32)

    def advance(carry, degree):
        previous, second, log_scale = carry
        degree_f = degree.astype(f32)
        step_factor = jnp.where(
            degree > orders[:, None],
            jnp.sqrt(
                jnp.maximum(4.0 * degree_f * degree_f - 1.0, 0.0)
                / jnp.maximum(degree_f * degree_f - order_f * order_f, 1.0)
            ),
            0.0,
        )
        lower_degree = degree_f - 1.0
        back_factor = jnp.sqrt(
            jnp.maximum(lower_degree * lower_degree - order_f * order_f, 0.0)
            / (4.0 * lower_degree * lower_degree - 1.0)
        )
        current = jnp.where(
            degree == orders[:, None],
            norm_start,
            step_factor * (cosine * previous - back_factor * second),
        )
        too_large = jnp.abs(current) > upper_bound
        current = jnp.where(too_large, current * lower_factor, current)
        previous = jnp.where(too_large, previous * lower_factor, previous)
        log_scale = jnp.where(too_large, log_scale + log_step, log_scale)
        return ((current, previous, log_scale), current * jnp.exp(log_scale))

    start_state = (zeros_state, zeros_state, order_f * log_sine)
    _, tables = lax.scan(advance, start_state, jnp.arange(degree_count, dtype=jnp.int32), unroll=8)
    return tables


def plain_gather(received, parts, own):
    bands = received.shape[0] // parts
    blocks = received.reshape(bands, parts // 2, 2, 2, own, 2, LANES).sum(axis=1)
    return blocks.transpose(0, 4, 2, 3, 1, 5).reshape(2 * bands, 2, own, 2 * LANES)


def plain_scatter(modes, parts):
    lats, _, own, _ = modes.shape
    bands = lats // 2
    blocks = modes.reshape(bands, 2, 2, own, 2, LANES).transpose(0, 4, 2, 3, 1, 5)
    blocks = jnp.broadcast_to(blocks[:, None], (bands, parts // 2) + blocks.shape[1:])
    return blocks.reshape(bands * parts, 2 * own, 2 * LANES)


def mode_factors(first_order, own, lat_total, degree_gain):
    if own % 8 == 0 and own * lat_total == LANES and degree_gain.shape[0] % 8 == 0:
        return coupling(first_order[None], degree_gain, lat_total)
    orders = first_order + 2 * jnp.arange(own, dtype=jnp.int32)
    log_norm = jnp.take(log_norms(M), orders)
    return legendre_orders(grid_tables(lat_total)[0], orders, log_norm, degree_gain.shape[0])


def mode_stages(first_order, own, parts, factors, degree_gain, spec_weight):
    if factors.ndim == 4:
        chans = spec_weight.shape[0]
        shape = (factors.shape[0], 2 * own, chans)

        def forward(received, tied):
            (weight,) = bring(tied, [spec_weight], us=0.1)
            return call(
                functools.partial(forward_modes_kernel, parts),
                (kept(*shape), struct(*received.shape)),
                vmem(1) + resident(1) + hbm(1),
                [VMEM(shape, f32), VMEM(shape, f32), VMEM(factors.shape, f32)]
                + [pltpu.SemaphoreType.DMA((1, 8))],
                us=2.0,
            )(received, weight, factors)

        def backward(received, spectrum, tied):
            sent = (received.shape[0], 2 * own + chans // received.shape[0], chans)
            half = (factors.shape[0] // 2, *factors.shape[1:])
            early, weight, spectrum = bring(
                tied,
                [factors, spec_weight, spectrum],
                us=0.1,
                first=half[0],
            )
            return call(
                functools.partial(backward_modes_kernel, parts),
                kept(*sent),
                vmem(1) + resident(3) + hbm(1),
                [VMEM(sent, f32), VMEM(shape, f32), VMEM(shape, f32), VMEM(half, f32)]
                + [pltpu.SemaphoreType.DMA((1, 4)), pltpu.SemaphoreType.DMA((2,))],
                us=2.0,
                out_spaces=pltpu.HBM,
            )(received, early, weight, spectrum, factors)

        return forward, backward

    legendre, lat_total = factors, factors.shape[2]
    quad_weight = grid_tables(lat_total)[1]
    orders = first_order + 2 * jnp.arange(own, dtype=jnp.int32)
    order_weight = jnp.where(orders == 0, 1.0, 2.0).astype(f32)[None, None, :, None]
    quad_column = quad_weight[:, None, None, None]
    dot = functools.partial(jnp.einsum, precision=highest)

    def forward(received, tied):
        del tied
        spectrum = plain_gather(received, parts, own)
        mixed = dot("jpmc,cd->jpmd", spectrum, spec_weight) * quad_column
        degree = dot("lmj,jpmd->lpmd", legendre, mixed) * degree_gain[:, None, None, :]
        synthesis = dot("lmj,lpmd->jpmd", legendre, degree) * order_weight
        return spectrum, plain_scatter(synthesis, parts)

    def backward(received, spectrum, tied):
        del tied
        error = plain_gather(received, parts, own) * order_weight
        gained = dot("lmj,jpmd->lpmd", legendre, error) * degree_gain[:, None, None, :]
        back = dot("lmj,lpmd->jpmd", legendre, gained) * quad_column
        sent = plain_scatter(dot("jpmd,cd->jpmc", back, spec_weight), parts)
        weight_part = dot("jpmc,jpmd->cd", spectrum, back)
        shares = weight_part.reshape(sent.shape[0], -1, weight_part.shape[1])
        return jnp.concatenate([sent, shares], axis=1)

    return forward, backward


def filter_coefficients(filters, disco_weight, band_start, band_reach):
    coefficient = jnp.einsum("ikrt,kc->irtc", filters, disco_weight, precision=highest)
    window = jnp.arange(WIN, dtype=jnp.int32)
    coefficient = jnp.where(
        (window[None, :] < band_reach[:, None])[:, :, None, None], coefficient, 0.0
    )
    offset = jnp.arange(-HMAX, HMAX + 1, dtype=jnp.int32)
    lands = offset[None, :, None] == band_start[:, None, None] + window[None, None, :]
    by_offset = jnp.sum(
        jnp.where(lands[:, :, :, None, None], coefficient[:, None], 0.0), axis=2
    )
    coef = by_offset.reshape(filters.shape[0], SPAN * KLON, LANES)
    return jnp.pad(coef, ((0, 0), (0, TAPS - SPAN * KLON), (0, 0)))


def swap_parts(x, axis):
    return lax.all_to_all(x, axis, split_axis=0, concat_axis=0, tiled=True)


def after(first, *later):
    return lax.optimization_barrier((first, *later))


def body(
    grid_field, filters, disco_weight, band_start, band_reach, spec_weight, degree_gain, cotangent
):
    band_rows, lon_local, chans = grid_field.shape
    bands, parts = lax.axis_size("lat"), lax.axis_size("chan")
    devices = bands * parts
    lat_total, lon_total = band_rows * bands, lon_local * parts
    own, share = M // devices, chans // devices
    assert band_rows == HMAX and chans == 2 * LANES and parts == 4
    band, part = lax.axis_index("lat"), lax.axis_index("chan")
    me, half, part_index = band * parts + part, part % 2, part[None]
    both_axes = ("lat", "chan")
    high, low = wave_tables(lon_total, own)
    depth = (lon_local + LANES - 1) // LANES * LANES
    apart_t = [
        jnp.asarray(np.ascontiguousarray(half_tables(table, depth).transpose(0, 2, 1)))
        for table in (high, low)
    ]
    high_t, low_t = (jnp.asarray(np.ascontiguousarray(t.T)) for t in (high, low))
    high, low = jnp.asarray(high), jnp.asarray(low)
    up = [(i, i + 1) for i in range(bands - 1)]
    down = [(i + 1, i) for i in range(bands - 1)]

    def halo(x):
        return lax.ppermute(x, "lat", up), x, lax.ppermute(x, "lat", down)

    def part_swap(x, distance):
        return lax.ppermute(x, "chan", [(i, i ^ distance) for i in range(parts)])

    def half_of(x, which):
        return lax.dynamic_slice_in_dim(x, which * LANES, LANES, axis=2)

    def edges(x):
        return part_swap(jnp.concatenate([x[:, :8], x[:, -8:]], axis=1), 2)

    def exchange(modes):
        return swap_parts(modes.reshape(devices, -1, modes.shape[-1]), both_axes)

    outgoing, cotangent, degree_gain, disco_weight, band_start, tied = after(
        half_of(grid_field, 1 - half), cotangent, degree_gain, disco_weight, band_start, part_index
    )
    field_other = part_swap(outgoing, 1)
    first_order = owned_orders(me, devices)
    factors = mode_factors(first_order, own, lat_total, degree_gain)
    cot_out = half_of(cotangent, 1 - half)
    field_other, factors, cot_out = after(field_other, factors, cot_out)
    tables = bring(tied, [high, low])
    modes, field = analyze(part_index, lon_total, grid_field, field_other, *tables)

    modes, field_sent, cot_out, disco_weight, band_start, tied = after(
        modes, field, cot_out, disco_weight, band_start, part_index
    )
    mine = lax.dynamic_slice_in_dim(disco_weight, half * LANES, LANES, axis=1)
    coef = filter_coefficients(filters, mine, band_start, band_reach)
    rows = halo(field_sent)
    cot_others = [part_swap(cot_out[row : row + 1], 1) for row in range(band_rows)]
    forward, backward = mode_stages(first_order, own, parts, factors, degree_gain, spec_weight)
    spectrum, synthesis = forward(exchange(modes), tied)
    synthesis, edge, cot_others[0] = after(synthesis, edges(field_sent), cot_others[0])

    local, adjoint = local_filter(*rows, *halo(jnp.concatenate([edge, coef], axis=1)))
    local, tied = after(local, part_index)
    error_modes, out_own, *out_sends, error = grid_stage(
        part_index, exchange(synthesis), local, cotangent, cot_others,
        (high, low, *bring(tied, [high_t, low_t], us=0.1)),
    )

    out_others = [part_swap(x, 1) for x in out_sends]
    rows = [lax.ppermute(error[row : row + 1], "lat", up) for row in range(band_rows)]
    rows += [error, lax.ppermute(error, "lat", down)]
    error_modes, tied = after(error_modes, part_index)
    sent = backward(exchange(error_modes), spectrum, tied)
    sent, edge, out_others[0], rows[0], rows[3], tied = after(
        sent, edges(error), out_others[0], rows[0], rows[3], part_index
    )
    base = adjoint_filter(part_index, *rows, *halo(edge), adjoint, cotangent, cot_others)
    received = exchange(sent)
    modes = received if own % 8 == 0 else received[:, : 2 * own]
    tables = bring(tied, apart_t, lambda ref, part: ref.at[1 - own_half(part)])
    grad_send, *shares = final_stage(part_index, lon_total, 2 * own, modes, base, *tables, True)
    if shares:
        grad_send, shares, *out_others = after(grad_send, shares[0], *out_others)
    else:
        shares = jnp.sum(received[:, 2 * own :], axis=0, keepdims=True)
        shares = jnp.broadcast_to(shares, (devices,) + shares.shape[1:])
    grad_other = part_swap(grad_send, 1)
    grad_weight = swap_parts(shares, both_axes).reshape(chans, chans)
    grad_own = final_stage(part_index, lon_total, 2 * own, modes, base, *apart_t, False)
    output = join(part_index, grid_field, out_own, *out_others)
    grad_input, grad_weight = after(close(part_index, grad_own, grad_other), grad_weight)
    return (output, grad_input, grad_weight)


def solution(mesh):
    in_specs = (
        P("lat", "chan", None),
        P("lat", None, None, None),
        P(),
        P("lat"),
        P("lat"),
        P(),
        P(),
        P("lat", "chan", None),
    )
    out_specs = (P("lat", "chan", None), P("lat", "chan", None), P())
    return jax.shard_map(body, mesh=mesh, in_specs=in_specs, out_specs=out_specs, check_vma=False)
```

```python
import functools
import math

import jax
import jax.numpy as jnp
import ml_dtypes
import numpy as np
from jax import lax
from jax.experimental import pallas as pl
from jax.experimental.pallas import tpu as pltpu
from jax.sharding import PartitionSpec as P

L = 360
M = 256
WIN = 3
HMAX = 2
KLON = 5
POLAR = 720
SPAN = 2 * HMAX + 1
TAPS = 32
EDGES = 16
LANES = 128
MIB = 2**20


highest = lax.Precision.HIGHEST
upper_bound = 2.0**32
lower_factor = 2.0 ** (-32)
log_step = 32.0 * math.log(2.0)

f32 = jnp.float32
bf16 = jnp.bfloat16
VMEM = pltpu.VMEM


@functools.lru_cache(maxsize=None)
def wave_tables(lon_total, own_count):
    orders = np.concatenate([np.arange(0, M, 2), np.arange(1, M, 2)]).reshape(-1, own_count)
    lons = np.arange(lon_total // 2)
    angle = (orders[:, :, None] * lons) % lon_total * (2.0 * np.pi / lon_total)
    table = np.stack([np.cos(angle), -np.sin(angle)], axis=1).reshape(2 * M, lon_total // 2)
    high = table.astype(ml_dtypes.bfloat16)
    low = (table - high.astype(np.float64)).astype(ml_dtypes.bfloat16)
    return high, low


def half_tables(table, depth):
    rows, lons = table.shape
    blocks = table.reshape(rows, 2, lons // 2).transpose(1, 0, 2)
    return np.pad(blocks, ((0, 0), (0, 0), (0, depth - lons // 2)))


def owned_orders(owner, devices):
    half = devices // 2
    return owner % half * (2 * (M // devices)) + owner // half


def grid_tables(lat_total):
    first_row = (POLAR - lat_total) // 2
    colatitude = math.pi * (jnp.arange(lat_total, dtype=f32) + float(first_row)) / POLAR
    quad_weight = 2.0 * math.pi * math.pi / POLAR * jnp.sin(colatitude)
    return (colatitude, quad_weight)


def log_norms(order_count):
    order_index = jnp.arange(order_count, dtype=f32)
    log_terms = jnp.where(
        order_index > 0.0,
        jnp.log((2.0 * order_index + 1.0) / jnp.maximum(2.0 * order_index, 1.0)),
        0.0,
    )
    return -0.5 * math.log(4.0 * math.pi) + 0.5 * jnp.cumsum(log_terms)


def split(x):
    high = x.astype(bf16)
    return high, (x - high.astype(f32)).astype(bf16)


def dot_split(a, b, dims):
    (ah, al), (bh, bl) = split(a), split(b)
    dot = lambda u, v: lax.dot_general(u, v, (dims, ((), ())), preferred_element_type=f32)
    return dot(ah, bh) + (dot(ah, bl) + dot(al, bh))


def cost(us):
    return pl.CostEstimate(flops=int(us * 1e9), bytes_accessed=int(us * 3e6), transcendentals=0)


def call(kernel, out_shape, in_specs, scratch=(), us=1.0, limit=16, out_spaces=None, aliases=None):
    run = pl.pallas_call(
        kernel,
        out_shape=out_shape,
        in_specs=[pl.BlockSpec(memory_space=space) for space, _ in in_specs],
        out_specs=jax.tree.map(
            lambda space: pl.BlockSpec(memory_space=space),
            out_spaces or jax.tree.map(lambda _: VMEM, out_shape),
        ),
        scratch_shapes=list(scratch),
        input_output_aliases=aliases or {},
        compiler_params=pltpu.CompilerParams(vmem_limit_bytes=limit * MIB),
        cost_estimate=cost(us),
    )
    keeps = [keep for _, keep in in_specs]
    return lambda *args: run(
        *[held(x, keep) if keep else x for x, keep in zip(args, keeps, strict=True)]
    )


def held(x, space):
    return pltpu.with_memory_space_constraint(x, space)


def vmem(count):
    return [(VMEM, None)] * count


def resident(count):
    return [(VMEM, VMEM)] * count


def loaded(count):
    return [(VMEM, pltpu.HBM)] * count


def hbm(count):
    return [(pltpu.HBM, pltpu.HBM)] * count


smem = (pltpu.SMEM, None)


def struct(*shape, dtype=f32):
    return jax.ShapeDtypeStruct(shape, dtype)


def near(*shape, dtype=f32):
    return pltpu.VMEM(shape, dtype)


def kept(*shape, dtype=f32):
    return pltpu.HBM(shape, dtype)


def own_half(part):
    return part % 2


def lane_half(x_ref, half):
    return x_ref.at[:, :, pl.ds(pl.multiple_of(half * LANES, LANES), LANES)]


def lon_half(x_ref, half):
    width = x_ref.shape[1] // 2
    return x_ref.at[:, pl.ds(pl.multiple_of(half * width, 8), width), :]


def pair_copies(half, own_hbm, other_hbms, target, sems):
    copies = [pltpu.make_async_copy(lane_half(own_hbm, half), lon_half(target, half), sems.at[0])]
    there = lon_half(target, 1 - half)
    for row, other_hbm in enumerate(other_hbms):
        copies.append(
            pltpu.make_async_copy(other_hbm, there.at[pl.ds(row, 1)], sems.at[1 + row])
        )
    for copy in copies:
        copy.start()
    return copies


def join_kernel(part_ref, field_ref, own_ref, *refs):
    o_ref = refs[-1]
    half = own_half(part_ref[0])
    mine, theirs = (
        pl.ds(pl.multiple_of(place * LANES, LANES), LANES) for place in (half, 1 - half)
    )
    o_ref[:, :, mine] = field_ref[:, :, mine] + own_ref[...]
    for row, other_ref in enumerate(refs[:-1]):
        this = pl.ds(row, 1)
        o_ref[this, :, theirs] = field_ref[this, :, theirs] + other_ref[...]


def join(part, field, own, *others):
    return call(
        join_kernel, kept(*field.shape), [smem] + loaded(2) + vmem(len(others))
    )(part, field, own, *others)


def side_by_side(x):
    return jnp.concatenate([x[0], x[1]], axis=1)


def three(table_high, table_low, high, low):
    dot = lambda u, v: jnp.dot(u, v, preferred_element_type=f32)
    return dot(table_high, high) + (dot(table_high, low) + dot(table_low, high))


def fetches(sources, targets, sems, pieces):
    copies = []
    for index, (source, target) in enumerate(zip(sources, targets, strict=True)):
        tile = source.shape[0] // pieces
        copies.append(
            [
                pltpu.make_async_copy(
                    source.at[pl.ds(piece * tile, tile)],
                    target.at[pl.ds(piece * tile, tile)],
                    sems.at[index, piece],
                )
                for piece in range(pieces)
            ]
        )
    for piece in range(pieces):
        for group in copies:
            group[piece].start()
    return lambda index, piece: copies[index][piece].wait()


def bring_kernel(views, part_ref, *refs):
    sources, targets, sems = refs[: len(views)], refs[len(views) : -1], refs[-1]
    copies = [
        pltpu.make_async_copy(view(source, part_ref[0]), target, sems.at[index])
        for index, (view, source, target) in enumerate(zip(views, sources, targets, strict=True))
    ]
    for copy in copies:
        copy.start()
    for copy in copies:
        copy.wait()


def bring(part, sources, view=None, us=2.0):
    views = [view or (lambda ref, part: ref)] * len(sources)
    shapes = [x.shape[1:] if view else x.shape for x in sources]
    return call(
        functools.partial(bring_kernel, views),
        [near(*shape, dtype=x.dtype) for shape, x in zip(shapes, sources, strict=True)],
        [smem] + hbm(len(sources)),
        [pltpu.SemaphoreType.DMA((len(sources),))],
        us=us,
        limit=8,
    )(part, *sources)


def there_already(index, piece):
    del index, piece


def analyze_rows(x, sign, high_ref, low_ref, wait, store):
    high, low = split(x)
    wait(0, 0)
    wait(1, 0)
    value = three(high_ref[...], low_ref[...], high, low)
    count = value.shape[0] // 2
    store(pl.ds(0, count), value[:count])
    store(pl.ds(count, count), value[count:] * sign)


def compose_rows(modes, sign, thigh_ref, tlow_ref, wait, store, pieces):
    count = modes.shape[0] // 2
    high, low = split(jnp.concatenate([modes[:count], modes[count:] * sign], axis=0))
    tile = thigh_ref.shape[0] // pieces
    for piece in range(pieces):
        rows = pl.ds(piece * tile, tile)
        wait(0, piece)
        wait(1, piece)
        store(rows, three(thigh_ref[rows, :], tlow_ref[rows, :], high, low))


def turn_sign(part):
    return (1 - 2 * (part // 2)).astype(f32)


def analyze_kernel(scale, part_ref, own_hbm, other_ref, high_ref, low_ref, o_ref, field_hbm,
                   x_ref, pair_sem, out_sem):
    part = part_ref[0]
    half = own_half(part)
    mine = pltpu.make_async_copy(lane_half(own_hbm, half), lon_half(x_ref, half), pair_sem)
    mine.start()
    lon_half(x_ref, 1 - half)[...] = other_ref[...]
    mine.wait()
    out = pltpu.make_async_copy(x_ref, field_hbm, out_sem)
    out.start()

    def store(rows, value):
        o_ref[rows, :] = value * scale

    analyze_rows(side_by_side(x_ref[...]), turn_sign(part), high_ref, low_ref, there_already, store)
    out.wait()


def analyze(part, lon_total, own, other, high, low):
    rows, lons, _ = own.shape
    field = (rows, 2 * lons, LANES)
    return call(
        functools.partial(analyze_kernel, 1.0 / lon_total),
        (struct(2 * M, rows * LANES), kept(*field)),
        [smem] + hbm(1) + vmem(1) + resident(2),
        [VMEM(field, f32), pltpu.SemaphoreType.DMA, pltpu.SemaphoreType.DMA],
        us=3.0,
        out_spaces=(VMEM, pltpu.HBM),
    )(part, own, other, high, low)


def grid_kernel(part_ref, s_ref, first_ref, second_ref, thigh_ref, tlow_ref, local_ref, cot_hbm,
                high_hbm, low_hbm,
                mode_ref, own_hbm, send_first_hbm, send_second_hbm, err_hbm,
                cot_ref, spec_ref, out_ref, err_ref,
                high_ref, low_ref, sems, other_sems, out_sems):
    part = part_ref[0]
    half, sign = own_half(part), turn_sign(part)
    others = [
        pltpu.make_async_copy(lane_half(cot_hbm, half), lon_half(cot_ref, half), other_sems.at[0]),
    ]
    for copy in others:
        copy.start()
    wait = fetches((high_hbm, low_hbm), (high_ref, low_ref), sems, 1)
    there = lon_half(cot_ref, 1 - half)
    for row, other_ref in enumerate((first_ref, second_ref)):
        there[pl.ds(row, 1)] = other_ref[...]

    def store_spec(rows, value):
        spec_ref[rows, :] = value

    modes = s_ref[...].reshape(thigh_ref.shape[1], s_ref.shape[2])
    compose_rows(modes, sign, thigh_ref, tlow_ref, there_already, store_spec, 1)
    for copy in others:
        copy.wait()
    tile = cot_ref.shape[1] // 6
    for row in range(cot_ref.shape[0]):
        for piece in range(6):
            lons = pl.ds(piece * tile, tile)
            hidden = local_ref[row, lons, :] + spec_ref[lons, pl.ds(row * LANES, LANES)]
            gate = 1.0 / (1.0 + jnp.exp(-hidden))
            out_ref[row, lons, :] = hidden * gate
            err_ref[row, lons, :] = cot_ref[row, lons, :] * (gate * (1.0 + hidden * (1.0 - gate)))
    there = lon_half(out_ref, 1 - half)
    outs = [
        pltpu.make_async_copy(source, target, out_sems.at[index])
        for index, (source, target) in enumerate(
            (
                (err_ref, err_hbm),
                (lon_half(out_ref, half), own_hbm),
                (there.at[pl.ds(0, 1)], send_first_hbm),
                (there.at[pl.ds(1, 1)], send_second_hbm),
            )
        )
    ]
    for copy in outs:
        copy.start()

    def store(rows, value):
        mode_ref[rows, :] = value

    analyze_rows(side_by_side(err_ref[...]), sign, high_ref, low_ref, wait, store)
    for copy in outs:
        copy.wait()


def grid_stage(part, synthesis, local, cotangent, others, tables):
    rows, lons, _ = local.shape
    block = (rows, lons // 2, LANES)
    grid = VMEM(local.shape, f32)
    return call(
        grid_kernel,
        (
            struct(2 * M, rows * LANES),
            kept(*block),
            kept(1, *block[1:]),
            kept(1, *block[1:]),
            kept(*local.shape),
        ),
        [smem] + vmem(3) + resident(3) + hbm(3),
        [grid, VMEM((lons, rows * LANES), f32), grid, grid]
        + [VMEM(table.shape, bf16) for table in tables[:2]]
        + [pltpu.SemaphoreType.DMA((2, 1))]
        + [pltpu.SemaphoreType.DMA((count,)) for count in (1, 4)],
        us=4.0,
        limit=32,
        out_spaces=(VMEM,) + (pltpu.HBM,) * 4,
    )(part, synthesis, *others, *tables[2:], local, cotangent, *tables[:2])


def final_kernel(scale, rows_own, theirs, part_ref, s_ref, base_hbm, *refs):
    part = part_ref[0]
    half = 1 - own_half(part) if theirs else own_half(part)
    if theirs:
        thigh_ref, tlow_ref, o_ref, *shares_ref, base_ref, base_sem = refs
        wait = there_already
        if shares_ref:
            share = jnp.sum(s_ref[:, pl.ds(rows_own, shares_ref[0].shape[1]), :], axis=0)
            shares_ref[0][...] = jnp.broadcast_to(share[None], shares_ref[0].shape)
    else:
        thigh_hbm, tlow_hbm, out_hbm, o_ref, base_ref, thigh_ref, tlow_ref, sems, base_sem = refs
        wait = fetches((thigh_hbm.at[half], tlow_hbm.at[half]), (thigh_ref, tlow_ref), sems, 1)
    base_copy = pltpu.make_async_copy(lon_half(base_hbm, half), base_ref, base_sem)
    base_copy.start()
    modes = s_ref[:, pl.ds(0, rows_own), :].reshape(thigh_ref.shape[1], s_ref.shape[2])
    total = o_ref.shape[1]

    def store(lons, value):
        count = min(lons.size, total - lons.start)
        for row in range(base_ref.shape[0]):
            lanes = slice(row * LANES, (row + 1) * LANES)
            o_ref[row, pl.ds(lons.start, count), :] = scale * value[:count, lanes]

    compose_rows(modes, turn_sign(part), thigh_ref, tlow_ref, wait, store, 1)
    base_copy.wait()
    o_ref[...] = o_ref[...] + base_ref[...]
    if not theirs:
        out = pltpu.make_async_copy(o_ref, lane_half(out_hbm, half), base_sem)
        out.start()
        out.wait()


def final_stage(part, lon_total, rows_own, modes, base, high_t, low_t, theirs):
    rows, lons, _ = base.shape
    block = (rows, lons // 2, LANES)
    scratch = [VMEM(block, f32)]
    out_shape = [struct(*block)]
    share = modes.shape[1] - rows_own
    if share:
        out_shape.append(struct(modes.shape[0], share, modes.shape[2]))
    if not theirs:
        out_shape = kept(rows, lons // 2, 2 * LANES)
        table = VMEM(high_t.shape[1:], bf16)
        scratch = [VMEM(block, f32)] * 2 + [table, table, pltpu.SemaphoreType.DMA((2, 1))]
    return call(
        functools.partial(final_kernel, 1.0 / lon_total, rows_own, theirs),
        out_shape,
        [smem] + vmem(1) + hbm(1) + (resident(2) if theirs else hbm(2)),
        scratch + [pltpu.SemaphoreType.DMA],
        us=2.0,
        out_spaces=None if theirs else pltpu.HBM,
    )(part, modes, base, high_t, low_t)


def close_kernel(part_ref, held_hbm, other_ref, o_hbm, sem):
    del held_hbm
    copy = pltpu.make_async_copy(other_ref, lane_half(o_hbm, 1 - own_half(part_ref[0])), sem)
    copy.start()
    copy.wait()


def close(part, held_half, other):
    return call(
        close_kernel,
        kept(*held_half.shape),
        [smem] + hbm(1) + vmem(1),
        [pltpu.SemaphoreType.DMA],
        us=8.0,
        out_spaces=pltpu.HBM,
        aliases={1: 0},
    )(part, held_half, other)


def filter_sums(refs, edge_refs, coef_ref, finish, sums_ref):
    lons = refs[0].shape[1]
    tile = lons // 18
    sources = [(x_ref, row) for x_ref in refs for row in range(x_ref.shape[0])]
    for row in range(2):
        def add(values, rows, row=row):
            for tap in range(KLON):
                total = values[0] * coef_ref[row, pl.ds(tap, 1), :]
                for offset in range(1, SPAN):
                    total = total + values[offset] * coef_ref[row, pl.ds(offset * KLON + tap, 1), :]
                sums_ref[tap, rows, :] = total

        near = sources[row : row + SPAN]
        edges = [(edge_ref, k) for edge_ref in edge_refs for k in range(2)][row : row + SPAN]
        add([edge_ref[k, pl.ds(8, 8), :] for edge_ref, k in edges], pl.ds(0, 8))
        add([edge_ref[k, pl.ds(0, 8), :] for edge_ref, k in edges], pl.ds(lons + 8, 8))

        @pl.loop(0, 18)
        def _(piece, near=near, add=add):
            start = pl.multiple_of(piece * tile, 8)
            values = [x_ref[k, pl.ds(start, tile), :] for x_ref, k in near]
            add(values, pl.ds(pl.multiple_of(start + 8, 8), tile))

        for piece in range(18):
            total = None
            for tap in range(KLON):
                value = sums_ref[tap, pl.ds(piece * tile + 8 + tap - KLON // 2, tile), :]
                total = value if total is None else total + value
            finish(row, pl.ds(piece * tile, tile), total)


def filter_kernel(prev_ref, own_ref, next_ref, lower_ref, middle_ref, upper_ref, o_ref, adjoint_ref,
                  sums_ref):
    def finish(row, lons, value):
        o_ref[row, lons, :] = value

    taps = pl.ds(EDGES, TAPS)
    coef_refs = [ref.at[:, taps] for ref in (lower_ref, middle_ref, upper_ref)]
    filter_sums(
        (prev_ref, own_ref, next_ref), (lower_ref, middle_ref, upper_ref), coef_refs[1], finish, sums_ref
    )
    adjoint_ref[...] = jnp.zeros_like(adjoint_ref)
    sources = [(c_ref, row) for c_ref in coef_refs for row in range(2)]
    for row in range(2):
        for offset in range(SPAN):
            c_ref, k = sources[row + offset]
            for tap in range(KLON):
                mirrored = (SPAN - 1 - offset) * KLON + KLON - 1 - tap
                adjoint_ref[row, pl.ds(offset * KLON + tap, 1), :] = c_ref[k, pl.ds(mirrored, 1), :]


def adjoint_kernel(part_ref, first_ref, second_ref, own_ref, next_ref, lower_ref, middle_ref, upper_ref, coef_ref,
                   cot_hbm, first_hbm, second_hbm,
                   o_ref, sums_ref, cot_ref, cot_sems):
    copies = pair_copies(
        own_half(part_ref[0]), cot_hbm, (first_hbm, second_hbm), cot_ref, cot_sems
    )
    for copy in copies:
        copy.wait()

    def finish(row, lons, value):
        o_ref[row, lons, :] = cot_ref[row, lons, :] + value

    edge_refs = (lower_ref, middle_ref, upper_ref)
    filter_sums((first_ref, second_ref, own_ref, next_ref), edge_refs, coef_ref, finish, sums_ref)


def local_filter(prev, own, behind, *edges):
    return call(
        filter_kernel,
        (near(*own.shape), kept(own.shape[0], TAPS, LANES)),
        loaded(3) + vmem(3),
        [VMEM((KLON, own.shape[1] + 16, LANES), f32)],
        us=4.0,
    )(prev, own, behind, *edges)


def adjoint_filter(part, first, second, own, behind, lower, middle, upper, coef, cotangent, others):
    return call(
        adjoint_kernel,
        kept(*own.shape),
        [smem] + loaded(4) + vmem(4) + hbm(3),
        [VMEM((KLON, own.shape[1] + 16, LANES), f32), VMEM(own.shape, f32)]
        + [pltpu.SemaphoreType.DMA((3,))],
        us=4.0,
    )(part, first, second, own, behind, lower, middle, upper, coef, cotangent, *others)


def coupling_kernel(lat_total, first_ref, gain_ref, o_hbm, step_ref, back_ref, start_ref, leg_ref,
                    scale_ref, padded_ref, column_ref, o_ref, out_sems):
    degree_count, chans = gain_ref.shape
    depth = padded_ref.shape[0]
    own = LANES // lat_total
    first_row = float((POLAR - lat_total) // 2)
    lane = lax.broadcasted_iota(jnp.int32, (1, LANES), 1)
    order = 2 * (lane % own) + first_ref[0]
    colatitude = math.pi * ((lane // own).astype(f32) + first_row) / POLAR
    cosine, log_sine = jnp.cos(colatitude), jnp.log(jnp.sin(colatitude))
    k = lax.broadcasted_iota(jnp.int32, (M, LANES), 0)
    k_f = k.astype(f32)
    log_terms = jnp.log((2.0 * k_f + 1.0) / jnp.maximum(2.0 * k_f, 1.0))
    log_norm = -0.5 * math.log(4.0 * math.pi) + 0.5 * jnp.sum(
        jnp.where((k > 0) & (k <= order), log_terms, 0.0), axis=0, keepdims=True
    )
    norm_start = jnp.exp(log_norm)
    degree = lax.broadcasted_iota(jnp.int32, (degree_count, LANES), 0)
    degree_f, order_f = degree.astype(f32), order.astype(f32)
    step = jnp.where(
        degree > order,
        jnp.sqrt(
            jnp.maximum(4.0 * degree_f * degree_f - 1.0, 0.0)
            / jnp.maximum(degree_f * degree_f - order_f * order_f, 1.0)
        ),
        0.0,
    )
    lower = degree_f - 1.0
    back = jnp.sqrt(
        jnp.maximum(lower * lower - order_f * order_f, 0.0) / (4.0 * lower * lower - 1.0)
    )
    step_ref[...] = step * cosine
    back_ref[...] = step * back
    start_ref[...] = jnp.where(degree == order, norm_start, 0.0)
    zeros = jnp.zeros((1, LANES), f32)

    def block(index, carry):
        previous, second, log_scale = carry
        first = pl.multiple_of(index * 8, 8)
        scale_ref[pl.ds(first, 8), :] = jnp.broadcast_to(log_scale, (8, LANES))
        for offset in range(8):
            row = pl.ds(first + offset, 1)
            rest = start_ref[row, :] - back_ref[row, :] * second
            current = step_ref[row, :] * previous + rest
            leg_ref[row, :] = current
            second, previous = previous, current
        too_large = jnp.abs(previous) > upper_bound
        second = jnp.where(too_large, second * lower_factor, second)
        previous = jnp.where(too_large, previous * lower_factor, previous)
        return previous, second, jnp.where(too_large, log_scale + log_step, log_scale)

    lax.fori_loop(0, degree_count // 8, block, (zeros, zeros, order_f * log_sine))
    leg_ref[pl.ds(0, degree_count), :] = leg_ref[pl.ds(0, degree_count), :] * jnp.exp(scale_ref[...])
    rest = depth - degree_count
    leg_ref[pl.ds(degree_count, rest), :] = jnp.zeros((rest, LANES), f32)
    padded_ref[pl.ds(0, degree_count), :] = gain_ref[...]
    padded_ref[pl.ds(degree_count, rest), :] = jnp.zeros((rest, chans), f32)
    column_ref[...] = leg_ref[...].T

    high, low = split(padded_ref[...])
    row = lax.broadcasted_iota(jnp.int32, (LANES, LANES), 0)
    quad = 2.0 * math.pi * math.pi / POLAR * jnp.sin(
        math.pi * ((row // own).astype(f32) + first_row) / POLAR
    )
    weight = quad * jnp.where(row % own + first_ref[0] == 0, 1.0, 2.0)
    weight = jnp.concatenate([weight] * (chans // LANES), axis=1)
    group = lat_total // out_sems.shape[0]
    copies = []
    for piece in range(out_sems.shape[0]):
        both = jnp.concatenate(
            [
                column_ref[...]
                * jnp.concatenate([column_ref[pl.ds(j * own, own), :]] * lat_total, axis=0)
                for j in range(piece * group, (piece + 1) * group)
            ],
            axis=0,
        )
        total = three(*split(both), high, low)
        for j in range(group):
            o_ref[piece * group + j] = (total[j * LANES : (j + 1) * LANES] * weight).reshape(
                lat_total, own, chans
            )
        block_of = pl.ds(piece * group, group)
        copies.append(
            pltpu.make_async_copy(o_ref.at[block_of], o_hbm.at[block_of], out_sems.at[piece])
        )
        copies[-1].start()
    for copy in copies:
        copy.wait()


def coupling(first_order, degree_gain, lat_total):
    degrees, chans = degree_gain.shape
    own = LANES // lat_total
    depth = (degrees + LANES - 1) // LANES * LANES
    table = (lat_total, lat_total, own, chans)
    rows = VMEM((degrees, LANES), f32)
    return call(
        functools.partial(coupling_kernel, lat_total),
        kept(*table),
        [smem] + loaded(1),
        [rows, rows, rows, VMEM((depth, LANES), f32), rows]
        + [VMEM((depth, chans), f32), VMEM((LANES, depth), f32), VMEM(table, f32)]
        + [pltpu.SemaphoreType.DMA((4,))],
        us=6.0,
        out_spaces=pltpu.HBM,
    )(first_order, degree_gain)


def gather_modes(r_ref, write, parts):
    for band in range(r_ref.shape[0] // parts):
        for half in range(2):
            both = r_ref[band * parts + half]
            for other in range(half + 2, parts, 2):
                both = both + r_ref[band * parts + other]
            for row in range(2):
                lanes = slice(row * LANES, (row + 1) * LANES)
                write(2 * band + row, pl.ds(half * LANES, LANES), both[:, lanes])


def scatter_modes(read, s_ref, parts, rows):
    for band in range(s_ref.shape[0] // parts):
        for part in range(parts):
            for row in range(2):
                lanes = pl.ds(row * LANES, LANES)
                value = read(2 * band + row, pl.ds(part % 2 * LANES, LANES))
                s_ref[band * parts + part, pl.ds(0, rows), lanes] = value


def forward_modes_kernel(parts, r_ref, w_ref, coupling_hbm, x_ref, s_ref, y_ref, z_ref,
                         coupling_ref, sems):
    wait = fetches((coupling_hbm,), (coupling_ref,), sems, 8)

    def write(j, lanes, value):
        x_ref[j, :, lanes] = value

    gather_modes(r_ref, write, parts)
    lats, rows, chans = x_ref.shape
    own = rows // 2
    y_ref[...] = dot_split(
        x_ref[...].reshape(lats * rows, chans), w_ref[...], ((1,), (0,))
    ).reshape(lats, rows, chans)
    for piece in range(8):
        wait(0, piece)

        @pl.loop(piece * (lats // 8), (piece + 1) * (lats // 8))
        def _(j):
            totals = [jnp.zeros((own, chans), f32)] * 2
            for other in range(lats):
                factor = coupling_ref[j, other]
                for p in range(2):
                    totals[p] = totals[p] + factor * y_ref[other, pl.ds(p * own, own), :]
            for p in range(2):
                z_ref[j, pl.ds(p * own, own), :] = totals[p]

    scatter_modes(lambda j, lanes: z_ref[j, :, lanes], s_ref, parts, rows)


def backward_modes_kernel(parts, r_ref, coupling_hbm, w_hbm, x_hbm, s_hbm, s_ref, e_ref, v_ref,
                          coupling_ref, w_ref, x_ref, sems, out_sems):
    wait = fetches((coupling_hbm,), (coupling_ref,), sems.at[pl.ds(0, 1)], 8)
    wait_rest = fetches((w_hbm, x_hbm), (w_ref, x_ref), sems.at[pl.ds(1, 2)], 2)

    def write(j, lanes, value):
        e_ref[j, :, lanes] = value

    gather_modes(r_ref, write, parts)
    lats, rows, chans = x_ref.shape
    own = rows // 2
    for piece in range(8):
        wait(0, piece)

    @pl.loop(0, lats)
    def _(j):
        totals = [jnp.zeros((own, chans), f32)] * 2
        for other in range(lats):
            factor = coupling_ref[other, j]
            for p in range(2):
                totals[p] = totals[p] + factor * e_ref[other, pl.ds(p * own, own), :]
        for p in range(2):
            v_ref[j, pl.ds(p * own, own), :] = totals[p]

    for piece in range(2):
        for index in range(2):
            wait_rest(index, piece)
    v = v_ref[...].reshape(lats * rows, chans)
    e_ref[...] = dot_split(v, w_ref[...], ((1,), (1,))).reshape(lats, rows, chans)
    scatter_modes(lambda j, lanes: e_ref[j, :, lanes], s_ref, parts, rows)
    sent = pltpu.make_async_copy(
        s_ref.at[:, pl.ds(0, rows), :], s_hbm.at[:, pl.ds(0, rows), :], out_sems.at[0]
    )
    sent.start()
    weight_part = dot_split(x_ref[...].reshape(lats * rows, chans), v, ((0,), (0,)))
    share = chans // s_ref.shape[0]
    s_ref[:, pl.ds(rows, share), :] = weight_part.reshape(s_ref.shape[0], share, chans)
    shares = pltpu.make_async_copy(
        s_ref.at[:, pl.ds(rows, share), :], s_hbm.at[:, pl.ds(rows, share), :], out_sems.at[1]
    )
    shares.start()
    sent.wait()
    shares.wait()


def legendre_orders(colatitude, orders, log_norm, degree_count):
    cosine = jnp.cos(colatitude)[None, :]
    log_sine = jnp.log(jnp.sin(colatitude))[None, :]
    order_f = orders.astype(f32)[:, None]
    norm_start = jnp.exp(log_norm)[:, None] + jnp.zeros_like(cosine)
    zeros_state = jnp.zeros((orders.shape[0], colatitude.shape[0]), f32)

    def advance(carry, degree):
        previous, second, log_scale = carry
        degree_f = degree.astype(f32)
        step_factor = jnp.where(
            degree > orders[:, None],
            jnp.sqrt(
                jnp.maximum(4.0 * degree_f * degree_f - 1.0, 0.0)
                / jnp.maximum(degree_f * degree_f - order_f * order_f, 1.0)
            ),
            0.0,
        )
        lower_degree = degree_f - 1.0
        back_factor = jnp.sqrt(
            jnp.maximum(lower_degree * lower_degree - order_f * order_f, 0.0)
            / (4.0 * lower_degree * lower_degree - 1.0)
        )
        current = jnp.where(
            degree == orders[:, None],
            norm_start,
            step_factor * (cosine * previous - back_factor * second),
        )
        too_large = jnp.abs(current) > upper_bound
        current = jnp.where(too_large, current * lower_factor, current)
        previous = jnp.where(too_large, previous * lower_factor, previous)
        log_scale = jnp.where(too_large, log_scale + log_step, log_scale)
        return ((current, previous, log_scale), current * jnp.exp(log_scale))

    start_state = (zeros_state, zeros_state, order_f * log_sine)
    _, tables = lax.scan(advance, start_state, jnp.arange(degree_count, dtype=jnp.int32), unroll=8)
    return tables


def plain_gather(received, parts, own):
    bands = received.shape[0] // parts
    blocks = received.reshape(bands, parts // 2, 2, 2, own, 2, LANES).sum(axis=1)
    return blocks.transpose(0, 4, 2, 3, 1, 5).reshape(2 * bands, 2, own, 2 * LANES)


def plain_scatter(modes, parts):
    lats, _, own, _ = modes.shape
    bands = lats // 2
    blocks = modes.reshape(bands, 2, 2, own, 2, LANES).transpose(0, 4, 2, 3, 1, 5)
    blocks = jnp.broadcast_to(blocks[:, None], (bands, parts // 2) + blocks.shape[1:])
    return blocks.reshape(bands * parts, 2 * own, 2 * LANES)


def mode_factors(first_order, own, lat_total, degree_gain):
    if own % 8 == 0 and own * lat_total == LANES and degree_gain.shape[0] % 8 == 0:
        return coupling(first_order[None], degree_gain, lat_total)
    orders = first_order + 2 * jnp.arange(own, dtype=jnp.int32)
    log_norm = jnp.take(log_norms(M), orders)
    return legendre_orders(grid_tables(lat_total)[0], orders, log_norm, degree_gain.shape[0])


def mode_stages(first_order, own, parts, factors, degree_gain, spec_weight):
    if factors.ndim == 4:
        chans = spec_weight.shape[0]
        shape = (factors.shape[0], 2 * own, chans)

        def forward(received, tied):
            (weight,) = bring(tied, [spec_weight], us=0.1)
            return call(
                functools.partial(forward_modes_kernel, parts),
                (kept(*shape), struct(*received.shape)),
                vmem(1) + resident(1) + hbm(1),
                [VMEM(shape, f32), VMEM(shape, f32), VMEM(factors.shape, f32)]
                + [pltpu.SemaphoreType.DMA((1, 8))],
                us=2.0,
            )(received, weight, factors)

        def backward(received, spectrum):
            sent = (received.shape[0], 2 * own + chans // received.shape[0], chans)
            return call(
                functools.partial(backward_modes_kernel, parts),
                kept(*sent),
                vmem(1) + hbm(3),
                [VMEM(sent, f32), VMEM(shape, f32), VMEM(shape, f32), VMEM(factors.shape, f32)]
                + [VMEM(spec_weight.shape, f32), VMEM(shape, f32)]
                + [pltpu.SemaphoreType.DMA((3, 8)), pltpu.SemaphoreType.DMA((2,))],
                us=2.0,
                out_spaces=pltpu.HBM,
            )(received, factors, spec_weight, spectrum)

        return forward, backward

    legendre, lat_total = factors, factors.shape[2]
    quad_weight = grid_tables(lat_total)[1]
    orders = first_order + 2 * jnp.arange(own, dtype=jnp.int32)
    order_weight = jnp.where(orders == 0, 1.0, 2.0).astype(f32)[None, None, :, None]
    quad_column = quad_weight[:, None, None, None]
    dot = functools.partial(jnp.einsum, precision=highest)

    def forward(received, tied):
        del tied
        spectrum = plain_gather(received, parts, own)
        mixed = dot("jpmc,cd->jpmd", spectrum, spec_weight) * quad_column
        degree = dot("lmj,jpmd->lpmd", legendre, mixed) * degree_gain[:, None, None, :]
        synthesis = dot("lmj,lpmd->jpmd", legendre, degree) * order_weight
        return spectrum, plain_scatter(synthesis, parts)

    def backward(received, spectrum):
        error = plain_gather(received, parts, own) * order_weight
        gained = dot("lmj,jpmd->lpmd", legendre, error) * degree_gain[:, None, None, :]
        back = dot("lmj,lpmd->jpmd", legendre, gained) * quad_column
        sent = plain_scatter(dot("jpmd,cd->jpmc", back, spec_weight), parts)
        weight_part = dot("jpmc,jpmd->cd", spectrum, back)
        shares = weight_part.reshape(sent.shape[0], -1, weight_part.shape[1])
        return jnp.concatenate([sent, shares], axis=1)

    return forward, backward


def filter_coefficients(filters, disco_weight, band_start, band_reach):
    coefficient = jnp.einsum("ikrt,kc->irtc", filters, disco_weight, precision=highest)
    window = jnp.arange(WIN, dtype=jnp.int32)
    coefficient = jnp.where(
        (window[None, :] < band_reach[:, None])[:, :, None, None], coefficient, 0.0
    )
    offset = jnp.arange(-HMAX, HMAX + 1, dtype=jnp.int32)
    lands = offset[None, :, None] == band_start[:, None, None] + window[None, None, :]
    by_offset = jnp.sum(
        jnp.where(lands[:, :, :, None, None], coefficient[:, None], 0.0), axis=2
    )
    coef = by_offset.reshape(filters.shape[0], SPAN * KLON, LANES)
    return jnp.pad(coef, ((0, 0), (0, TAPS - SPAN * KLON), (0, 0)))


def swap_parts(x, axis):
    return lax.all_to_all(x, axis, split_axis=0, concat_axis=0, tiled=True)


def after(first, *later):
    return lax.optimization_barrier((first, *later))


def body(
    grid_field, filters, disco_weight, band_start, band_reach, spec_weight, degree_gain, cotangent
):
    band_rows, lon_local, chans = grid_field.shape
    bands, parts = lax.axis_size("lat"), lax.axis_size("chan")
    devices = bands * parts
    lat_total, lon_total = band_rows * bands, lon_local * parts
    own, share = M // devices, chans // devices
    assert band_rows == HMAX and chans == 2 * LANES and parts == 4
    band, part = lax.axis_index("lat"), lax.axis_index("chan")
    me, half, part_index = band * parts + part, part % 2, part[None]
    both_axes = ("lat", "chan")
    high, low = wave_tables(lon_total, own)
    depth = (lon_local + LANES - 1) // LANES * LANES
    apart_t = [
        jnp.asarray(np.ascontiguousarray(half_tables(table, depth).transpose(0, 2, 1)))
        for table in (high, low)
    ]
    high_t, low_t = (jnp.asarray(np.ascontiguousarray(t.T)) for t in (high, low))
    high, low = jnp.asarray(high), jnp.asarray(low)
    up = [(i, i + 1) for i in range(bands - 1)]
    down = [(i + 1, i) for i in range(bands - 1)]

    def halo(x):
        return lax.ppermute(x, "lat", up), x, lax.ppermute(x, "lat", down)

    def part_swap(x, distance):
        return lax.ppermute(x, "chan", [(i, i ^ distance) for i in range(parts)])

    def half_of(x, which):
        return lax.dynamic_slice_in_dim(x, which * LANES, LANES, axis=2)

    def edges(x):
        return part_swap(jnp.concatenate([x[:, :8], x[:, -8:]], axis=1), 2)

    def exchange(modes):
        return swap_parts(modes.reshape(devices, -1, modes.shape[-1]), both_axes)

    outgoing, cotangent, degree_gain, disco_weight, band_start, tied = after(
        half_of(grid_field, 1 - half), cotangent, degree_gain, disco_weight, band_start, part_index
    )
    field_other = part_swap(outgoing, 1)
    first_order = owned_orders(me, devices)
    factors = mode_factors(first_order, own, lat_total, degree_gain)
    cot_out = half_of(cotangent, 1 - half)
    field_other, factors, cot_out = after(field_other, factors, cot_out)
    tables = bring(tied, [high, low])
    modes, field = analyze(part_index, lon_total, grid_field, field_other, *tables)

    modes, field_sent, cot_out, disco_weight, band_start, tied = after(
        modes, field, cot_out, disco_weight, band_start, part_index
    )
    mine = lax.dynamic_slice_in_dim(disco_weight, half * LANES, LANES, axis=1)
    coef = filter_coefficients(filters, mine, band_start, band_reach)
    rows = halo(field_sent)
    cot_others = [part_swap(cot_out[row : row + 1], 1) for row in range(band_rows)]
    forward, backward = mode_stages(first_order, own, parts, factors, degree_gain, spec_weight)
    spectrum, synthesis = forward(exchange(modes), tied)
    synthesis, edge, cot_others[0] = after(synthesis, edges(field_sent), cot_others[0])

    local, adjoint = local_filter(*rows, *halo(jnp.concatenate([edge, coef], axis=1)))
    local, tied = after(local, part_index)
    error_modes, out_own, *out_sends, error = grid_stage(
        part_index, exchange(synthesis), local, cotangent, cot_others,
        (high, low, *bring(tied, [high_t, low_t], us=0.1)),
    )

    out_others = [part_swap(x, 1) for x in out_sends]
    rows = [lax.ppermute(error[row : row + 1], "lat", up) for row in range(band_rows)]
    rows += [error, lax.ppermute(error, "lat", down)]
    sent = backward(exchange(error_modes), spectrum)
    sent, edge, out_others[0], rows[0], rows[3], tied = after(
        sent, edges(error), out_others[0], rows[0], rows[3], part_index
    )
    base = adjoint_filter(part_index, *rows, *halo(edge), adjoint, cotangent, cot_others)
    received = exchange(sent)
    modes = received if own % 8 == 0 else received[:, : 2 * own]
    tables = bring(tied, apart_t, lambda ref, part: ref.at[1 - own_half(part)])
    grad_send, *shares = final_stage(part_index, lon_total, 2 * own, modes, base, *tables, True)
    if shares:
        grad_send, shares, *out_others = after(grad_send, shares[0], *out_others)
    else:
        shares = jnp.sum(received[:, 2 * own :], axis=0, keepdims=True)
        shares = jnp.broadcast_to(shares, (devices,) + shares.shape[1:])
    grad_other = part_swap(grad_send, 1)
    grad_weight = swap_parts(shares, both_axes).reshape(chans, chans)
    grad_own = final_stage(part_index, lon_total, 2 * own, modes, base, *apart_t, False)
    output = join(part_index, grid_field, out_own, *out_others)
    grad_input, grad_weight = after(close(part_index, grad_own, grad_other), grad_weight)
    return (output, grad_input, grad_weight)


def solution(mesh):
    in_specs = (
        P("lat", "chan", None),
        P("lat", None, None, None),
        P(),
        P("lat"),
        P("lat"),
        P(),
        P(),
        P("lat", "chan", None),
    )
    out_specs = (P("lat", "chan", None), P("lat", "chan", None), P())
    return jax.shard_map(body, mesh=mesh, in_specs=in_specs, out_specs=out_specs, check_vma=False)
```
